32 devices in a mesh: dp: 8 (over z, y), tensor: 4 (over x, core).
Axes of the slice: x: 2, y: 2, z: 4, core: 2. Of those that a mesh axis runs over, the one named last changes fastest.
Arguments:
- frames: bfloat16 [16384, 768], P(('dp', 'tensor')), may hold values from -6 to 6
- segment_ids: int32 [8, 2048], P('dp'), may hold values from 0 to 4, as said below
- project_weight: bfloat16 [3, 768, 768], P(None, None, 'tensor'), may hold values from -0.3125 to 0.3125
- query_value_bias: bfloat16 [2, 768], P(None, 'tensor'), may hold values from -3 to 3
- output_weight: bfloat16 [768, 768], P('tensor'), may hold values from -1.75 to 1.75
- output_bias: bfloat16 [768], replicated, may hold values from -3 to 3
- first_gain: bfloat16 [768], replicated, may hold values from 0.5 to 1.5
- first_shift: bfloat16 [768], replicated, may hold values from -3 to 3
- expand_weight: bfloat16 [768, 3072], P(None, 'tensor'), may hold values from -0.21875 to 0.21875
- expand_bias: bfloat16 [3072], P('tensor'), may hold values from -3 to 3
- reduce_weight: bfloat16 [3072, 768], P('tensor'), may hold values from -0.109375 to 0.109375
- reduce_bias: bfloat16 [768], replicated, may hold values from -3 to 3
- second_gain: bfloat16 [768], replicated, may hold values from 0.5 to 1.5
- second_shift: bfloat16 [768], replicated, may hold values from -3 to 3
- cotangent: bfloat16 [16384, 768], P(('dp', 'tensor')), may hold values from -6 to 6
Outputs:
- layer_out: bfloat16 [16384, 768], P(('dp', 'tensor'))
- frames_grad: float32 [16384, 768], P(('dp', 'tensor'))
- project_grad: float32 [3, 768, 768], P(None, 'dp', 'tensor')
- attend_bias_grad: float32 [2, 768], P(None, 'tensor')
- output_grad: float32 [768, 768], P('tensor', 'dp')
- expand_grad: float32 [768, 3072], P('dp', 'tensor')
- expand_bias_grad: float32 [3072], P('tensor')
- reduce_grad: float32 [3072, 768], P('tensor', 'dp')
- vector_grads: float32 [6, 768], replicated
The draws below stay inside these ranges and needn't reach their ends.
Inputs may be any that keep to these rules, and one draw needn't show every extreme that they name: `segment_ids`: within each row of 2048 frames the ids never fall, and frames of one id form one clip; a row holds two to five clips, one of which starts within the first 256 frames and ends within the last 256; the last frame of every row has id 4.
All inputs are finite; a program needn't handle non-finite values.
Results may differ from the reference program's by a relative error of at most 0.02.
The reference program's roundings to bfloat16 on the way count: a program that leaves them out, or rounds other values in their place, can miss the bound.
Values may be sent and summed in bfloat16 or wider, within the bound.
No kernel may reach another device: no remote copies, remote signals or barrier semaphores. Data moves between devices by JAX's collectives and lax.ppermute only.
A program may use at most 128 MiB of HBM per device.

```python
import jax
import jax.numpy as jnp
from jax import lax

D = 768
HEAD_DIM = 64
FF = 3072
ROW_LEN = 2048
ROWS = 8
TOKENS = 16384


def draw_segment_ids(key, part):
    key = jax.random.fold_in(key, 7)
    key_a, key_b, key_c, key_d = jax.random.split(key, 4)
    edge = max(ROW_LEN // 8, 2)
    start = jax.random.randint(key_a, (ROWS, 1), 1, edge)
    stop = ROW_LEN - jax.random.randint(key_b, (ROWS, 1), 1, edge)
    first = jax.random.randint(key_c, (ROWS, 1), 0, start)
    final = jax.random.randint(key_d, (ROWS, 1), stop, ROW_LEN)
    position = jnp.arange(ROW_LEN, dtype=jnp.int32)[None, :]
    ident = (position >= first).astype(jnp.int32) + (position >= start).astype(jnp.int32) + (position >= stop).astype(jnp.int32) + (position >= final).astype(jnp.int32)
    return ident.astype(jnp.int32)


def spiked(array, stream_key, source, target, parts, factor):
    owner, partner = [(jnp.arange(array.shape[dim]) // (array.shape[dim] // parts)).reshape([-1 if axis == dim else 1 for axis in range(array.ndim)]) for dim in (source, target)]
    chosen = jax.random.permutation(stream_key, parts)[partner]
    strong = (owner == chosen) | (owner == (partner + parts // 2) % parts)
    return jnp.where(strong, factor * array, array)


def shard_levels(own_key, shape, cuts, least, largest):
    level, own = 1.0, jax.random.fold_in(own_key, 6)
    for dim, shards_of in cuts:
        heights = jnp.exp(jax.random.uniform(jax.random.fold_in(own, dim), (shards_of,), jnp.float32, least / len(cuts), largest / len(cuts)))
        level = level * jnp.repeat(heights, shape[dim] // shards_of).reshape([-1 if axis == dim else 1 for axis in range(len(shape))])
    return level


def scatter_about(rng, extent, deviation, bound, shards=(), held_as=jnp.bfloat16):
    drawn = jax.random.normal(rng, extent, jnp.float32) * deviation
    if len(shards) > 0:
        drawn = shard_levels(rng, extent, shards, -0.22, 0.18) * drawn
    return jnp.clip(drawn, min=-bound, max=bound).astype(held_as)


def heavy_noise(key, dims, scale, bound, shards, heavy, kind=jnp.bfloat16):
    array = scale * jax.random.normal(key, dims, jnp.float32)
    if shards:
        array = array * shard_levels(key, dims, shards, -0.22, 0.18)
    return jnp.clip(spiked(array, jax.random.fold_in(key, 3), *heavy), -bound, bound).astype(kind)


def setup_inputs(seed: int = 0) -> dict:
    streams_of = jax.random.split(jax.random.key(seed), 16)
    return {
        "frames": scatter_about(streams_of[0], (TOKENS, D), 1.0, 6.0, ((0, 32),)),
        "segment_ids": draw_segment_ids(jax.random.fold_in(streams_of[15], 71), 0),
        "project_weight": scatter_about(streams_of[2], (3, D, D), (D // 2) ** -0.5, 0.3125, ((2, 4),)),
        "query_value_bias": scatter_about(streams_of[3], (2, D), 0.5, 3.0, ((1, 4),)),
        "output_weight": scatter_about(streams_of[4], (D, D), (max(D // 64, 1)) ** -0.5, 1.75, ((0, 4),)),
        "output_bias": scatter_about(streams_of[5], (D,), 0.5, 3.0),
        "first_gain": jnp.clip(1.0 + 0.1 * jax.random.normal(streams_of[6], (D,), jnp.float32), 0.5, 1.5).astype(jnp.bfloat16),
        "first_shift": scatter_about(streams_of[7], (D,), 0.5, 3.0),
        "expand_weight": scatter_about(streams_of[8], (D, FF), D ** -0.5, 0.21875, ((1, 4),)),
        "expand_bias": scatter_about(streams_of[9], (FF,), 0.5, 3.0, ((0, 4),)),
        "reduce_weight": scatter_about(streams_of[10], (FF, D), FF ** -0.5, 0.109375, ((0, 4),)),
        "reduce_bias": scatter_about(streams_of[11], (D,), 0.5, 3.0),
        "second_gain": jnp.clip(1.0 + 0.1 * jax.random.normal(streams_of[12], (D,), jnp.float32), 0.5, 1.5).astype(jnp.bfloat16),
        "second_shift": scatter_about(streams_of[13], (D,), 0.5, 3.0),
        "cotangent": heavy_noise(streams_of[14], (TOKENS, D), 1.0, 6.0, ((0, 32),), (0, 1, 32, 2.75)),
    }


HIGH = lax.Precision.HIGHEST
EPS = 1e-05

@jax.custom_vjp
def low(v):
    return lax.optimization_barrier(v.astype(jnp.bfloat16)).astype(jnp.float32)

@jax.custom_vjp
def low_back(v):
    return v

def low_keep(v):
    return (low(v), None)

def low_pass(kept, grad):
    return (grad,)

def back_keep(v):
    return (v, None)

def back_low(kept, grad):
    return (low(grad),)
low.defvjp(low_keep, low_pass)
low_back.defvjp(back_keep, back_low)

def normalize(values, gain, shift):
    mean = lax.optimization_barrier(jnp.mean(values, axis=-1, keepdims=True))
    center = values - mean
    variance = lax.optimization_barrier(jnp.mean(center * center, axis=-1, keepdims=True))
    return center * lax.rsqrt(variance + EPS) * gain + shift

def row_attention(packed):
    queries, keys, values, segs = packed
    scores = jnp.einsum('qhd,khd->hqk', queries, keys, precision=HIGH) * HEAD_DIM ** (-0.5)
    scores = low_back(scores)
    same = segs[:, None] == segs[None, :]
    scores = jnp.where(same[None], scores, -1e+30)
    weights = low(jax.nn.softmax(scores, axis=-1))
    return jnp.einsum('hqk,khd->qhd', weights, values, precision=HIGH)

def forward(segment_ids, inputs, project_weight, query_value_bias, output_weight, output_bias, first_gain, first_shift, expand_weight, expand_bias, reduce_weight, reduce_bias, second_gain, second_shift):
    tokens, width = inputs.shape
    heads = width // HEAD_DIM
    projected = jnp.einsum('td,ide->tie', inputs, project_weight, precision=HIGH)
    shift = jnp.stack([query_value_bias[0], jnp.zeros_like(query_value_bias[0]), query_value_bias[1]])
    projected = low_back(low(projected + shift[None]))
    split = projected.reshape(ROWS, ROW_LEN, 3, heads, HEAD_DIM)
    attended = lax.map(jax.checkpoint(row_attention), (split[:, :, 0], split[:, :, 1], split[:, :, 2], segment_ids))
    attended = low_back(low(attended.reshape(tokens, width)))
    branch = low_back(jnp.dot(attended, output_weight, precision=HIGH))
    normed = normalize(inputs + branch + output_bias, first_gain, first_shift)
    inner = low_back(jnp.dot(low(normed), expand_weight, precision=HIGH) + expand_bias)
    active = low(jax.nn.gelu(inner, approximate=False))
    second = low_back(jnp.dot(active, reduce_weight, precision=HIGH))
    return normalize(normed + second + reduce_bias, second_gain, second_shift)

def reference(frames, segment_ids, project_weight, query_value_bias, output_weight, output_bias, first_gain, first_shift, expand_weight, expand_bias, reduce_weight, reduce_bias, second_gain, second_shift, cotangent):
    params = tuple((a.astype(jnp.float32) for a in (frames, project_weight, query_value_bias, output_weight, output_bias, first_gain, first_shift, expand_weight, expand_bias, reduce_weight, reduce_bias, second_gain, second_shift)))

    def closed(*values):
        return forward(segment_ids, *values)
    result, pull = jax.vjp(closed, *params)
    grads = pull(cotangent.astype(jnp.float32))
    vectors = jnp.stack([grads[4], grads[5], grads[6], grads[10], grads[11], grads[12]])
    return (result.astype(jnp.bfloat16), grads[0], grads[1], grads[2], grads[3], grads[7], grads[8], grads[9], vectors)
```

```python
import functools

import jax
import jax.numpy as jnp
import numpy as np
from jax import lax
from jax.experimental import pallas as pl
from jax.experimental.pallas import tpu as pltpu
from jax.sharding import PartitionSpec as P

HEAD_DIM = 64
ROW_LEN = 2048
EPS = 1e-05
FLOAT = jnp.float32
BRAIN = jnp.bfloat16
BIG = 1e30
SCALE = HEAD_DIM ** (-0.5)
VMEM_BYTES = 60 << 20
IDS = 8
LANES = 128

NN = (((1,), (0,)), ((), ()))
NT = (((1,), (1,)), ((), ()))


def dot(left, right, dims=NN):
    return lax.dot_general(left, right, dims, preferred_element_type=FLOAT)


def swap(value, axis, size, bits):
    return lax.ppermute(value, axis, [(i, i ^ bits) for i in range(size)])


def whole(shape):
    return pl.BlockSpec(shape, lambda *_: (0,) * len(shape), pipeline_mode=pl.Buffered(1))


def split_three(value):
    top = value.astype(BRAIN).astype(FLOAT)
    rest = value - top
    middle = rest.astype(BRAIN).astype(FLOAT)
    return top, middle, rest - middle


def project_kernel(heads, rows, *refs):
    x_refs = refs[:4]
    w_ref, bias_ref, ktail_ref, qtail_ref = refs[4:8]
    qt_ref, ka_ref, vt_ref, qz_ref, kt_ref, va_ref, xt_ref = refs[8:]
    lane = lax.broadcasted_iota(jnp.int32, (rows, HEAD_DIM), 1)
    minus = jnp.where(lane < 3, -1.0, 0.0).astype(BRAIN)
    empty = jnp.zeros((rows, HEAD_DIM), BRAIN)
    for k in range(4):
        at = pl.ds(k * rows, rows)
        x = x_refs[k][...]
        query = (dot(x, w_ref[0]) + bias_ref[0:1]).astype(BRAIN).astype(FLOAT) * SCALE
        key = dot(x, w_ref[1])
        value = dot(x, w_ref[2]) + bias_ref[1:2]
        xt_ref[:, at] = x.T
        for h in range(heads):
            own = slice(h * HEAD_DIM, (h + 1) * HEAD_DIM)
            q, k_, v = query[:, own], key[:, own], value[:, own]
            qt_ref[h, :HEAD_DIM, at] = q.T.astype(BRAIN)
            qt_ref[h, HEAD_DIM:, at] = qtail_ref[:, at]
            kt_ref[h, :, at] = k_.T.astype(BRAIN)
            vt_ref[h, :, at] = v.T.astype(BRAIN)
            ka_ref[h, at, :] = jnp.concatenate([k_.astype(BRAIN), ktail_ref[at, :]], axis=1)
            va_ref[h, at, :] = jnp.concatenate([v.astype(BRAIN), minus], axis=1)
            qz_ref[h, at, :] = jnp.concatenate([empty, q.astype(BRAIN)], axis=1)


def project(pieces, weight, bias, ktail, qtail):
    rows, width = pieces[0].shape
    cols = weight.shape[2]
    heads = cols // HEAD_DIM
    length = 4 * rows
    shapes = [
        (heads, LANES, length),
        (heads, length, LANES),
        (heads, HEAD_DIM, length),
        (heads, length, LANES),
        (heads, HEAD_DIM, length),
        (heads, length, LANES),
        (width, length),
    ]
    return pl.pallas_call(
        functools.partial(project_kernel, heads, rows),
        out_shape=[jax.ShapeDtypeStruct(s, BRAIN) for s in shapes],
        compiler_params=pltpu.CompilerParams(vmem_limit_bytes=VMEM_BYTES),
        cost_estimate=pl.CostEstimate(
            flops=6 * length * width * cols, bytes_accessed=16 << 20, transcendentals=0
        ),
        name="project",
    )(*pieces, weight, bias, ktail, qtail)


def attend_kernel(rows, blocks, *refs):
    qt_ref, ka_ref, vt_ref = refs[:3]
    outs = refs[3:]
    for n in range(len(blocks)):
        out_ref, exact_ref, log_ref = outs[3 * n : 3 * n + 3]
        scores = dot(ka_ref[0], qt_ref[0, :, n * rows : (n + 1) * rows])
        highest = jnp.max(scores, axis=0, keepdims=True)
        raised = jnp.exp(scores - highest)
        total = jnp.sum(raised, axis=0, keepdims=True)
        mixed = dot(vt_ref[0], raised.astype(BRAIN)) / total
        out_ref[...] = mixed.astype(BRAIN)
        exact_ref[...] = mixed
        log_ref[0] = highest + jnp.log(total)


def attend(qt, ka, vt, rows, blocks):
    heads, _, length = qt.shape
    count = len(blocks)
    first = blocks[0] // count
    out_shape, out_specs = [], []
    for _ in blocks:
        for kind in (BRAIN, FLOAT):
            out_shape.append(jax.ShapeDtypeStruct((heads * HEAD_DIM, rows), kind))
            out_specs.append(pl.BlockSpec((HEAD_DIM, rows), lambda h: (h, 0)))
        out_shape.append(jax.ShapeDtypeStruct((heads, 1, rows), FLOAT))
        out_specs.append(pl.BlockSpec((1, 1, rows), lambda h: (h, 0, 0)))
    outs = pl.pallas_call(
        functools.partial(attend_kernel, rows, blocks),
        grid=(heads,),
        in_specs=[
            pl.BlockSpec((1, LANES, count * rows), lambda h: (h, 0, first)),
            pl.BlockSpec((1, length, LANES), lambda h: (h, 0, 0)),
            pl.BlockSpec((1, HEAD_DIM, length), lambda h: (h, 0, 0)),
        ],
        out_specs=out_specs,
        out_shape=out_shape,
        compiler_params=pltpu.CompilerParams(vmem_limit_bytes=VMEM_BYTES),
        cost_estimate=pl.CostEstimate(
            flops=8 * heads * length * count * rows * LANES,
            bytes_accessed=8 << 20,
            transcendentals=heads * length * count * rows,
        ),
        name="attend",
    )(qt, ka, vt)
    return [outs[3 * n : 3 * n + 3] for n in range(count)]


def attend_back_kernel(rows, *refs):
    qt_ref, ka_ref, qz_ref, kt_ref, va_ref, xt_ref = refs[:6]
    grad_refs, exact_refs, log_refs = refs[6:10], refs[10:14], refs[14:18]
    out_refs, project_ref, bias_ref = refs[18:22], refs[22], refs[23]
    queries, grads, rows_grad, total = refs[24:]
    step = pl.program_id(0)
    low = lax.broadcasted_iota(jnp.int32, (8, rows), 0)

    def stacked(value):
        top, middle, bottom = split_three(value)
        return jnp.where(
            low == 0, top, jnp.where(low == 1, middle, jnp.where(low == 2, bottom, 0.0))
        )

    @pl.when(step == 0)
    def _():
        queries[...] = jnp.zeros_like(queries)
        grads[...] = jnp.zeros_like(grads)

    for k in range(4):

        @pl.when(step == k)
        def _():
            grad = grad_refs[k][...].astype(FLOAT)
            delta = jnp.sum(grad * exact_refs[k][...], axis=0, keepdims=True)
            queries[:HEAD_DIM, :] = qt_ref[0, :HEAD_DIM, :]
            ids = qt_ref[0, HEAD_DIM : HEAD_DIM + 16, :].astype(FLOAT)[:IDS]
            queries[HEAD_DIM : HEAD_DIM + 16, :] = jnp.concatenate(
                [ids, stacked(log_refs[k][0])], axis=0
            ).astype(BRAIN)
            grads[:HEAD_DIM, :] = grad_refs[k][...]
            grads[HEAD_DIM : HEAD_DIM + 16, :] = jnp.concatenate(
                [stacked(delta), jnp.zeros((8, rows), FLOAT)], axis=0
            ).astype(BRAIN)
            rows_grad[...] = jnp.concatenate([grad, jnp.zeros_like(grad)], axis=0).T.astype(BRAIN)

    probs = jnp.exp(dot(ka_ref[0], queries[...]))
    grad_scores = (probs * dot(va_ref[0], grads[...])).astype(BRAIN)
    added = dot(probs.astype(BRAIN), rows_grad[...]) + dot(grad_scores, qz_ref[0])
    grad_query = (dot(kt_ref[0], grad_scores) * SCALE).T

    @pl.when(step == 0)
    def _():
        total[...] = added

    @pl.when(step > 0)
    def _():
        total[...] += added

    for k in range(4):

        @pl.when(step == k)
        def _():
            out_refs[k][:, 2 * HEAD_DIM :] = grad_query.astype(BRAIN)

    @pl.when(step == 3)
    def _():
        grad_project = jnp.zeros(project_ref.shape, FLOAT)
        bias = jnp.zeros(bias_ref.shape, FLOAT)
        for k in range(4):
            at = pl.ds(k * rows, rows)
            out_refs[k][:, : 2 * HEAD_DIM] = total[at, :].astype(BRAIN)
            piece = out_refs[k][...]
            grad_project += dot(xt_ref[:, at], piece)
            bias += jnp.sum(piece.astype(FLOAT), axis=0, keepdims=True)
        project_ref[...] = grad_project.astype(BRAIN)
        bias_ref[...] = bias


def attend_back(head, forms, grads, exacts, logs):
    qt, ka, qz, kt, va, xt = forms
    length, width = ka.shape[1], xt.shape[0]
    rows = length // 4
    cols = 3 * HEAD_DIM
    head_block = [pl.BlockSpec((HEAD_DIM, rows), lambda i: (head, 0))] * 4
    return pl.pallas_call(
        functools.partial(attend_back_kernel, rows),
        grid=(4,),
        in_specs=[
            pl.BlockSpec((1, LANES, rows), lambda i: (head, 0, i)),
            pl.BlockSpec((1, length, LANES), lambda i: (head, 0, 0)),
            pl.BlockSpec((1, rows, LANES), lambda i: (head, i, 0)),
            pl.BlockSpec((1, HEAD_DIM, length), lambda i: (head, 0, 0)),
            pl.BlockSpec((1, length, LANES), lambda i: (head, 0, 0)),
            whole((width, length)),
        ]
        + head_block
        + head_block
        + [pl.BlockSpec((1, 1, rows), lambda i: (head, 0, 0))] * 4,
        out_specs=[whole((rows, cols))] * 4 + [whole((width, cols)), whole((1, cols))],
        out_shape=[jax.ShapeDtypeStruct((rows, cols), BRAIN)] * 4
        + [jax.ShapeDtypeStruct((width, cols), BRAIN), jax.ShapeDtypeStruct((1, cols), FLOAT)],
        scratch_shapes=[
            pltpu.VMEM((LANES, rows), BRAIN),
            pltpu.VMEM((LANES, rows), BRAIN),
            pltpu.VMEM((rows, LANES), BRAIN),
            pltpu.VMEM((length, LANES), FLOAT),
        ],
        compiler_params=pltpu.CompilerParams(vmem_limit_bytes=VMEM_BYTES),
        cost_estimate=pl.CostEstimate(
            flops=24 * length * length * LANES,
            bytes_accessed=8 << 20,
            transcendentals=length * length,
        ),
        name="attend_back",
    )(qt, ka, qz, kt, va, xt, *grads, *exacts, *logs)


def gelu_parts(values):
    t = 1.0 / (1.0 + (0.3275911 * 0.7071067811865476) * jnp.abs(values))
    bell = jnp.exp(-0.5 * values * values)
    poly = 0.5 * 1.061405429
    for c in (-1.453152027, 1.421413741, -0.284496736, 0.254829592):
        poly = poly * t + 0.5 * c
    tail = poly * t * bell
    below = jnp.where(values >= 0, 1.0 - tail, tail)
    return values * below, below + values * bell * 0.3989422804014327


def mean_of(values):
    return jnp.mean(values, axis=-1, keepdims=True)


def layer_kernel(
    t_ref,
    o0,
    o1,
    o2,
    o3,
    x_ref,
    cot_ref,
    vec_ref,
    wo_ref,
    eb_ref,
    we_ref,
    wr_ref,
    out_ref,
    grad_first_ref,
    d0,
    d1,
    d2,
    d3,
    small_ref,
    keep_a,
    send_a,
    keep_b,
    send_b,
    orow,
    normed,
    hb,
    hbt,
    unit_one,
    inv_one,
    act,
    slope,
    acc,
    grad_second,
    dfb,
    dfbt,
    stage,
    tail_stage,
    sem,
    tail_sem,
):
    step = pl.program_id(0)
    me = t_ref[0]
    width = x_ref.shape[1]
    part = o0.shape[0]
    bias_out, gain_one, shift_one, bias_red, gain_two, shift_two = (
        vec_ref[i : i + 1] for i in range(6)
    )

    @pl.when(step == 0)
    def _():
        for k, ref in enumerate((o0, o1, o2, o3)):
            orow[:, k * part : (k + 1) * part] = ref[...].astype(FLOAT).T.astype(BRAIN)
        total = x_ref[...].astype(FLOAT) + bias_out
        branch = jnp.zeros_like(total)
        for k in range(4):
            branch += dot(orow[:, k * part : (k + 1) * part], wo_ref[me ^ k])
        total = total + branch
        center = total - mean_of(total)
        inverse = lax.rsqrt(mean_of(center * center) + EPS)
        unit = center * inverse
        value = unit * gain_one + shift_one
        unit_one[...] = unit
        inv_one[...] = inverse
        normed[...] = value
        hb[...] = value.astype(BRAIN)
        hbt[...] = value.T.astype(BRAIN)
        acc[...] = jnp.zeros_like(acc)

    for j in range(4):

        @pl.when(step == j)
        def _():
            inner = dot(hb[...], we_ref[0]) + eb_ref[me ^ j]
            active, derivative = gelu_parts(inner)
            active = active.astype(BRAIN)
            act[j] = active
            slope[j] = derivative
            acc[...] += dot(active, wr_ref[0])

    @pl.when(step == 3)
    def _():
        total = normed[...] + acc[...] + bias_red
        center = total - mean_of(total)
        inverse = lax.rsqrt(mean_of(center * center) + EPS)
        unit = center * inverse
        out_ref[...] = (unit * gain_two + shift_two).astype(BRAIN)
        cot = cot_ref[...].astype(FLOAT)
        scaled = cot * gain_two
        grad = inverse * (scaled - mean_of(scaled) - unit * mean_of(scaled * unit))
        small_ref[3:4] = jnp.sum(grad, axis=0, keepdims=True)
        small_ref[4:5] = jnp.sum(cot * unit, axis=0, keepdims=True)
        small_ref[5:6] = jnp.sum(cot, axis=0, keepdims=True)
        grad_second[...] = grad
        dfb[...] = grad.astype(BRAIN)
        dfbt[...] = grad.T.astype(BRAIN)
        acc[...] = grad

    def copies(j):
        block = 7 - j
        slot = j % 2
        ref_a = keep_a if block in (0, 2) else send_a
        ref_b = keep_b if block in (0, 2) else send_b
        return [
            pltpu.make_async_copy(
                stage.at[slot, n], ref.at[block // 2, :, pl.ds(0, width)], sem.at[slot, n]
            )
            for n, ref in enumerate((ref_a, ref_b))
        ]

    for j in range(4, 8):

        @pl.when(step == j)
        def _():
            block = 7 - j
            slot = j % 2
            if j >= 6:
                for copy in copies(j - 2):
                    copy.wait()
            grad_inner = (dot(dfb[...], wr_ref[0], NT) * slope[block]).astype(BRAIN)
            small_ref[8 + block : 9 + block] = jnp.sum(
                grad_inner.astype(FLOAT), axis=0, keepdims=True
            )
            stage[slot, 0] = dot(hbt[...], grad_inner).astype(BRAIN)
            stage[slot, 1] = dot(dfbt[...], act[block]).astype(BRAIN)
            for copy in copies(j):
                copy.start()
            acc[...] += dot(grad_inner, we_ref[0], NT)

    @pl.when(step == 7)
    def _():
        grad = acc[...]
        unit = unit_one[...]
        small_ref[1:2] = jnp.sum(grad * unit, axis=0, keepdims=True)
        small_ref[2:3] = jnp.sum(grad, axis=0, keepdims=True)
        scaled = grad * gain_one
        first = inv_one[...] * (scaled - mean_of(scaled) - unit * mean_of(scaled * unit))
        small_ref[0:1] = jnp.sum(first, axis=0, keepdims=True)
        grad_first_ref[...] = first
        attend_grad = first.astype(BRAIN)
        for k, ref in enumerate((d0, d1, d2, d3)):
            ref[...] = dot(wo_ref[me ^ k], attend_grad, NT).astype(BRAIN)
        attend_grad_t = first.T.astype(BRAIN)
        output_grad = dot(attend_grad_t, orow[...]).astype(BRAIN)
        last = []
        for k in range(4):
            ref_a, ref_b = (keep_a, keep_b) if k in (0, 2) else (send_a, send_b)
            own = output_grad[:, k * part : (k + 1) * part]
            own = jnp.concatenate([own, jnp.zeros((width, 2 * LANES - part), BRAIN)], axis=1)
            for n, ref in enumerate((ref_a, ref_b)):
                tail_stage[k, n] = own[:, n * LANES : (n + 1) * LANES]
                last.append(
                    pltpu.make_async_copy(
                        tail_stage.at[k, n],
                        ref.at[k // 2, :, pl.ds(width, LANES)],
                        tail_sem.at[k, n],
                    )
                )
        for copy in last:
            copy.start()
        for j in (6, 7):
            for copy in copies(j):
                copy.wait()
        for copy in last:
            copy.wait()


def layer(me, mixed, frames, cotangent, vectors, wo, eb, we, wr):
    rows, width = frames.shape
    part = mixed[0].shape[0]
    hidden = we.shape[2]
    order = lambda j, t: (t[0] ^ jnp.minimum(j, 7 - j), 0, 0)
    grads = jax.ShapeDtypeStruct((2, width, hidden + LANES), BRAIN)
    grid_spec = pltpu.PrefetchScalarGridSpec(
        num_scalar_prefetch=1,
        grid=(8,),
        in_specs=[whole((part, rows))] * 4
        + [
            whole((rows, width)),
            whole((rows, width)),
            whole(vectors.shape),
            whole(wo.shape),
            whole(eb.shape),
            pl.BlockSpec((1, width, hidden), order),
            pl.BlockSpec((1, hidden, width), order),
        ],
        out_specs=[whole((rows, width)), whole((rows, width))]
        + [whole((part, rows))] * 4
        + [whole((16, width))]
        + [pl.BlockSpec(memory_space=pl.ANY)] * 4,
        scratch_shapes=[
            pltpu.VMEM((rows, width), BRAIN),
            pltpu.VMEM((rows, width), FLOAT),
            pltpu.VMEM((rows, width), BRAIN),
            pltpu.VMEM((width, rows), BRAIN),
            pltpu.VMEM((rows, width), FLOAT),
            pltpu.VMEM((rows, 1), FLOAT),
            pltpu.VMEM((4, rows, hidden), BRAIN),
            pltpu.VMEM((4, rows, hidden), FLOAT),
            pltpu.VMEM((rows, width), FLOAT),
            pltpu.VMEM((rows, width), FLOAT),
            pltpu.VMEM((rows, width), BRAIN),
            pltpu.VMEM((width, rows), BRAIN),
            pltpu.VMEM((2, 2, width, hidden), BRAIN),
            pltpu.VMEM((4, 2, width, LANES), BRAIN),
            pltpu.SemaphoreType.DMA((2, 2)),
            pltpu.SemaphoreType.DMA((4, 2)),
        ],
    )
    return pl.pallas_call(
        layer_kernel,
        grid_spec=grid_spec,
        out_shape=[
            jax.ShapeDtypeStruct((rows, width), BRAIN),
            jax.ShapeDtypeStruct((rows, width), FLOAT),
        ]
        + [jax.ShapeDtypeStruct((part, rows), BRAIN)] * 4
        + [jax.ShapeDtypeStruct((16, width), FLOAT)]
        + [grads] * 4,
        compiler_params=pltpu.CompilerParams(vmem_limit_bytes=VMEM_BYTES),
        cost_estimate=pl.CostEstimate(
            flops=2 * rows * width * (24 * hidden + 3 * width),
            bytes_accessed=40 << 20,
            transcendentals=8 * rows * hidden,
        ),
        name="layer",
    )(me, *mixed, frames, cotangent, vectors, wo, eb, we, wr)


def frames_kernel(count, *refs):
    t_ref, base_ref = refs[:2]
    pieces = refs[2 : 2 + 4 * count]
    w_ref, out_ref = refs[2 + 4 * count :]
    me = t_ref[0]
    total = base_ref[...]
    for n in range(count):
        for k in range(4):
            total += dot(pieces[4 * n + k][...], w_ref[me ^ k, n])
    out_ref[...] = total


def frames_back(me, base, pieces, weight, first, count):
    rows, width = base.shape
    cols = 3 * HEAD_DIM
    grid_spec = pltpu.PrefetchScalarGridSpec(
        num_scalar_prefetch=1,
        grid=(1,),
        in_specs=[whole((rows, width))]
        + [whole((rows, cols))] * (4 * count)
        + [
            pl.BlockSpec(
                (4, count, cols, width),
                lambda i, t: (0, first // count, 0, 0),
                pipeline_mode=pl.Buffered(1),
            )
        ],
        out_specs=whole((rows, width)),
    )
    return pl.pallas_call(
        functools.partial(frames_kernel, count),
        grid_spec=grid_spec,
        out_shape=jax.ShapeDtypeStruct((rows, width), FLOAT),
        compiler_params=pltpu.CompilerParams(vmem_limit_bytes=VMEM_BYTES),
        cost_estimate=pl.CostEstimate(
            flops=8 * count * rows * cols * width, bytes_accessed=8 << 20, transcendentals=0
        ),
        name="frames_back",
    )(me, base, *pieces, weight)


def halve(value, bits, bit, size):
    at = bits.index(bit)
    lead, rest = value.shape[0], value.shape[1:]
    view = value.reshape((2**at, 2, lead // 2 ** (at + 1)) + rest)
    mine = (lax.axis_index("dp") // bit) % 2
    keep = lax.dynamic_index_in_dim(view, mine, 1, keepdims=False)
    send = lax.dynamic_index_in_dim(view, 1 - mine, 1, keepdims=False)
    shape = (lead // 2,) + rest
    got = swap(send.reshape(shape), "dp", size, bit)
    total = keep.reshape(shape).astype(FLOAT) + got.astype(FLOAT)
    return total, [b for b in bits if b != bit]


def body(
    frames,
    segment_ids,
    project_weight,
    query_value_bias,
    output_weight,
    output_bias,
    first_gain,
    first_shift,
    expand_weight,
    expand_bias,
    reduce_weight,
    reduce_bias,
    second_gain,
    second_shift,
    cotangent,
    *,
    groups,
):
    rows, width = frames.shape
    cols = project_weight.shape[2]
    heads = cols // HEAD_DIM
    length = 4 * rows
    me = lax.axis_index("tensor")
    scalar = jnp.full((1,), me, jnp.int32)
    other = functools.partial(swap, axis="tensor", size=4)

    near = other(frames, bits=1)
    far = other(frames, bits=2)
    last = other(far, bits=1)
    pieces = (frames, near, far, last)

    blocks = segment_ids.reshape(4, rows)
    segs = jnp.concatenate([lax.dynamic_index_in_dim(blocks, me ^ k, 0) for k in range(4)], axis=1)
    ids = jnp.arange(IDS, dtype=jnp.int32)
    same = segs.reshape(1, length) == ids[:, None]
    qtail = jnp.pad(same.astype(BRAIN), ((0, LANES - HEAD_DIM - IDS), (0, 0)))
    differ = segs.reshape(length, 1) != ids[None, :]
    ktail = jnp.concatenate(
        [
            jnp.where(differ, -BIG, 0.0).astype(BRAIN),
            jnp.full((length, 3), -1.0, BRAIN),
            jnp.zeros((length, LANES - HEAD_DIM - IDS - 3), BRAIN),
        ],
        axis=1,
    )
    vectors = jnp.stack(
        [output_bias, first_gain, first_shift, reduce_bias, second_gain, second_shift]
    ).astype(FLOAT)
    vectors = jnp.pad(vectors, ((0, 2), (0, 0)))
    turned = jnp.transpose(
        project_weight[::-1].reshape(3, width, heads, HEAD_DIM), (2, 0, 3, 1)
    ).reshape(heads, 3 * HEAD_DIM, width)

    held = lax.optimization_barrier(
        (last, output_weight, expand_weight, expand_bias, reduce_weight, turned)
    )
    last, output_weight, expand_weight, expand_bias, reduce_weight, turned = held
    pieces = (frames, near, far, last)
    wo = lax.all_gather(output_weight, "tensor")
    eb = lax.all_gather(expand_bias[None].astype(FLOAT), "tensor")
    we = lax.all_gather(expand_weight, "tensor")
    wr = lax.all_gather(reduce_weight, "tensor")
    wt = lax.all_gather(turned, "tensor")

    qt, ka, vt, qz, kt, va, xt = project(
        pieces, project_weight, query_value_bias.astype(FLOAT), ktail, qtail
    )
    far_blocks = attend(qt, ka, vt, rows, (2, 3))
    near_blocks = attend(qt, ka, vt, rows, (0, 1))
    attended = near_blocks + far_blocks
    mixed = [attended[0][0]] + [other(attended[k][0], bits=k) for k in (1, 2, 3)]

    outs = layer(scalar, mixed, frames, cotangent, vectors, wo, eb, we, wr)
    layer_out, grad_first = outs[:2]
    small = outs[6]
    keep_a, send_a, keep_b, send_b = outs[7:]
    grad_heads = [outs[2]] + [other(outs[2 + k], bits=k) for k in (1, 2, 3)]

    everyone = lax.all_gather(small, ("dp", "tensor")).reshape(groups, 4, 16, width)
    vector_grads = jnp.sum(everyone[:, :, :6], axis=(0, 1))
    picked = [lax.dynamic_index_in_dim(everyone[:, s], 8 + (me ^ s), 1, False) for s in range(4)]
    expand_bias_grad = sum(jnp.sum(p, axis=0) for p in picked)

    bits = [2**n for n in reversed(range(groups.bit_length() - 1))]
    share = width // groups
    total_a = keep_a.astype(FLOAT) + other(send_a, bits=1).astype(FLOAT)
    total_b = keep_b.astype(FLOAT) + other(send_b, bits=1).astype(FLOAT)
    sent = other(total_a[1].astype(BRAIN), bits=2)
    part_a = (total_a[0] + sent.astype(FLOAT)).astype(BRAIN).reshape(groups, share, -1)
    part_a, left = halve(part_a, bits, 1, groups)
    part_b = jnp.swapaxes(total_b.astype(BRAIN).reshape(2, groups, share, -1), 0, 1)
    part_b, _ = halve(part_b, bits, 1, groups)
    part_b = jnp.swapaxes(part_b, 0, 1)
    sent = other(part_b[1].astype(BRAIN), bits=2)
    part_b = part_b[0] + sent.astype(FLOAT)
    part = jnp.concatenate([part_a.astype(BRAIN), part_b.astype(BRAIN)], axis=2)
    for bit in list(reversed(left)):
        part, left = halve(part.astype(BRAIN), left, bit, groups)
    part = part[0]
    hidden = expand_weight.shape[1]
    expand_grad = part[:, :hidden]
    reduce_grad = part[:, hidden + LANES : 2 * hidden + LANES].T
    output_grad = jnp.concatenate(
        [
            part[:, hidden : hidden + LANES],
            part[:, 2 * hidden + LANES : 2 * hidden + cols],
        ],
        axis=1,
    ).T

    forms = (qt, ka, qz, kt, va, xt)
    exacts = [a[1] for a in attended]
    logs = [a[2] for a in attended]
    frames_grad = grad_first
    project_parts = []
    for h in range(heads):
        res = attend_back(h, forms, grad_heads, exacts, logs)
        got = [res[0]] + [other(res[k], bits=k) for k in (1, 2, 3)]
        frames_grad = frames_back(scalar, frames_grad, got, wt, h, 1)
        spread = 3 * HEAD_DIM // share
        bias = jnp.broadcast_to(res[5].reshape(1, spread, share), (groups, spread, share))
        value = jnp.concatenate(
            [
                res[4].reshape(groups, share, 3 * HEAD_DIM),
                jnp.swapaxes(bias, 1, 2).astype(BRAIN),
                jnp.zeros((groups, share, 2 * LANES - 3 * HEAD_DIM - spread), BRAIN),
            ],
            axis=2,
        )
        left = bits
        for bit in reversed(bits):
            value, left = halve(value.astype(BRAIN), left, bit, groups)
        project_parts.append(value[0])
    project_grad = jnp.stack(
        [
            jnp.concatenate(
                [p[:, (2 - i) * HEAD_DIM : (3 - i) * HEAD_DIM] for p in project_parts], axis=1
            )
            for i in range(3)
        ]
    )
    bias_sums = [
        p[:, 3 * HEAD_DIM : 3 * HEAD_DIM + spread].T.reshape(3, HEAD_DIM) for p in project_parts
    ]
    attend_bias_grad = jnp.stack(
        [jnp.concatenate([b[i] for b in bias_sums]) for i in (2, 0)]
    )
    return (
        layer_out,
        frames_grad,
        project_grad,
        attend_bias_grad,
        output_grad,
        expand_grad,
        expand_bias_grad,
        reduce_grad,
        vector_grads,
    )


def solution(mesh):
    placed = (
        P(("dp", "tensor"), None),
        P("dp", None),
        P(None, None, "tensor"),
        P(None, "tensor"),
        P("tensor", None),
        P(),
        P(),
        P(),
        P(None, "tensor"),
        P("tensor"),
        P("tensor", None),
        P(),
        P(),
        P(),
        P(("dp", "tensor"), None),
    )
    return jax.shard_map(
        functools.partial(body, groups=mesh.shape["dp"]),
        mesh=mesh,
        in_specs=placed,
        out_specs=(
            P(("dp", "tensor"), None),
            P(("dp", "tensor"), None),
            P(None, "dp", "tensor"),
            P(None, "tensor"),
            P("tensor", "dp"),
            P("dp", "tensor"),
            P("tensor"),
            P("tensor", "dp"),
            P(),
        ),
        check_vma=False,
    )
```

```python
import functools

import jax
import jax.numpy as jnp
import numpy as np
from jax import lax
from jax.experimental import pallas as pl
from jax.experimental.pallas import tpu as pltpu
from jax.sharding import PartitionSpec as P

HEAD_DIM = 64
ROW_LEN = 2048
EPS = 1e-05
FLOAT = jnp.float32
BRAIN = jnp.bfloat16
BIG = 1e30
SCALE = HEAD_DIM ** (-0.5)
VMEM_BYTES = 60 << 20
IDS = 8
LANES = 128

NN = (((1,), (0,)), ((), ()))
NT = (((1,), (1,)), ((), ()))


def dot(left, right, dims=NN):
    return lax.dot_general(left, right, dims, preferred_element_type=FLOAT)


def swap(value, axis, size, bits):
    return lax.ppermute(value, axis, [(i, i ^ bits) for i in range(size)])


def whole(shape):
    return pl.BlockSpec(shape, lambda *_: (0,) * len(shape), pipeline_mode=pl.Buffered(1))


def split_three(value):
    top = value.astype(BRAIN).astype(FLOAT)
    rest = value - top
    middle = rest.astype(BRAIN).astype(FLOAT)
    return top, middle, rest - middle


def project_kernel(heads, rows, *refs):
    x_refs = refs[:2]
    w_ref, bias_ref, ktail_ref, qtail_ref = refs[2:6]
    qt_ref, ka_ref, vt_ref, qz_ref, kt_ref, va_ref, xt_ref = refs[-8:-1]
    held = refs[-1]
    step = pl.program_id(0)
    for k in range(2):

        @pl.when(step == k)
        def _():
            held[...] = x_refs[k][...]

    x = held[...]
    xt_ref[...] = x.T
    lane = lax.broadcasted_iota(jnp.int32, (rows, LANES), 1)
    minus = jnp.where((lane >= HEAD_DIM) & (lane < HEAD_DIM + 3), -1.0, 0.0)
    query = (dot(x, w_ref[0]) + bias_ref[0:1]).astype(BRAIN).astype(FLOAT) * SCALE
    key = dot(x, w_ref[1])
    value = dot(x, w_ref[2]) + bias_ref[1:2]
    for h in range(heads):
        own = slice(h * LANES, (h + 1) * LANES)
        q, k_, v = query[:, own], key[:, own], value[:, own]
        qt_ref[h, :HEAD_DIM, :] = qtail_ref[...]
        qt_ref[h, HEAD_DIM:, :] = q.T[HEAD_DIM:].astype(BRAIN)
        kt_ref[h] = k_.T[HEAD_DIM:].astype(BRAIN)
        vt_ref[h] = v.T[:HEAD_DIM].astype(BRAIN)
        ka_ref[h] = (k_ + ktail_ref[...]).astype(BRAIN)
        va_ref[h] = (v + minus).astype(BRAIN)
        qz_ref[h] = q.astype(BRAIN)


def project(first, pieces, weight, bias, ktail, qtail, before):
    rows, width = pieces[0].shape
    heads = weight.shape[2] // LANES
    length = 4 * rows
    by_lane = lambda i: (0, 0, first + i)
    by_row = lambda i: (0, first + i, 0)
    shapes = [
        ((heads, LANES, length), (heads, LANES, rows), by_lane),
        ((heads, length, LANES), (heads, rows, LANES), by_row),
        ((heads, HEAD_DIM, length), (heads, HEAD_DIM, rows), by_lane),
        ((heads, length, LANES), (heads, rows, LANES), by_row),
        ((heads, HEAD_DIM, length), (heads, HEAD_DIM, rows), by_lane),
        ((heads, length, LANES), (heads, rows, LANES), by_row),
        ((width, length), (width, rows), lambda i: (0, first + i)),
    ]
    return pl.pallas_call(
        functools.partial(project_kernel, heads, rows),
        grid=(2,),
        in_specs=[
            whole((rows, width)),
            whole((rows, width)),
            whole(weight.shape),
            whole(bias.shape),
            pl.BlockSpec((rows, LANES), lambda i: (first + i, 0)),
            pl.BlockSpec((HEAD_DIM, rows), lambda i: (0, first + i)),
        ]
        + [pl.BlockSpec(memory_space=pl.ANY)] * len(before),
        out_specs=[pl.BlockSpec(block, index) for _, block, index in shapes],
        out_shape=[jax.ShapeDtypeStruct(s, BRAIN) for s, _, _ in shapes],
        scratch_shapes=[pltpu.VMEM((rows, width), BRAIN)],
        input_output_aliases={6 + n: n for n in range(len(before))},
        compiler_params=pltpu.CompilerParams(vmem_limit_bytes=VMEM_BYTES),
        cost_estimate=pl.CostEstimate(
            flops=12 * rows * width * weight.shape[2], bytes_accessed=8 << 20, transcendentals=0
        ),
        name="project",
    )(*pieces, weight, bias, ktail, qtail, *before)


def attend_kernel(rows, blocks, *refs):
    qt_ref, ka_ref, vt_ref = refs[:3]
    outs = refs[3:]
    for n in range(len(blocks)):
        out_ref, exact_ref, log_ref = outs[3 * n : 3 * n + 3]
        scores = dot(ka_ref[0], qt_ref[0, :, n * rows : (n + 1) * rows])
        highest = jnp.max(scores, axis=0, keepdims=True)
        raised = jnp.exp(scores - highest)
        total = jnp.sum(raised, axis=0, keepdims=True)
        mixed = dot(vt_ref[0], raised.astype(BRAIN)) / total
        out_ref[...] = mixed.astype(BRAIN)
        exact_ref[...] = mixed
        log_ref[0] = highest + jnp.log(total)


def attend(qt, ka, vt, rows, blocks):
    heads, _, length = qt.shape
    count = len(blocks)
    first = blocks[0] // count
    out_shape, out_specs = [], []
    for _ in blocks:
        for kind in (BRAIN, FLOAT):
            out_shape.append(jax.ShapeDtypeStruct((heads * HEAD_DIM, rows), kind))
            out_specs.append(pl.BlockSpec((HEAD_DIM, rows), lambda h: (h, 0)))
        out_shape.append(jax.ShapeDtypeStruct((heads, 1, rows), FLOAT))
        out_specs.append(pl.BlockSpec((1, 1, rows), lambda h: (h, 0, 0)))
    outs = pl.pallas_call(
        functools.partial(attend_kernel, rows, blocks),
        grid=(heads,),
        in_specs=[
            pl.BlockSpec((1, LANES, count * rows), lambda h: (h, 0, first)),
            pl.BlockSpec((1, length, LANES), lambda h: (h, 0, 0)),
            pl.BlockSpec((1, HEAD_DIM, length), lambda h: (h, 0, 0)),
        ],
        out_specs=out_specs,
        out_shape=out_shape,
        compiler_params=pltpu.CompilerParams(vmem_limit_bytes=VMEM_BYTES),
        cost_estimate=pl.CostEstimate(
            flops=8 * heads * length * count * rows * LANES,
            bytes_accessed=8 << 20,
            transcendentals=heads * length * count * rows,
        ),
        name="attend",
    )(qt, ka, vt)
    return [outs[3 * n : 3 * n + 3] for n in range(count)]


def back_block(step, items, forms, scratch):
    qt_ref, ka_ref, qz_ref, kt_ref, va_ref = forms
    queries, grads, rows_grad = scratch
    rows = queries.shape[1]
    low = lax.broadcasted_iota(jnp.int32, (8, rows), 0)

    def stacked(value):
        top, middle, bottom = split_three(value)
        return jnp.where(
            low == 0, top, jnp.where(low == 1, middle, jnp.where(low == 2, bottom, 0.0))
        )

    def fill(grad_ref, exact_ref, log_ref):
        grad = grad_ref[...].astype(FLOAT)
        delta = jnp.sum(grad * exact_ref[...], axis=0, keepdims=True)
        ids = qt_ref[0, :16, :].astype(FLOAT)[:IDS]
        queries[:16, :] = jnp.concatenate([ids, stacked(log_ref[0])], axis=0).astype(BRAIN)
        queries[16:, :] = qt_ref[0, 16:, :]
        grads[:HEAD_DIM, :] = grad_ref[...]
        grads[HEAD_DIM : HEAD_DIM + 16, :] = jnp.concatenate(
            [stacked(delta), jnp.zeros((8, rows), FLOAT)], axis=0
        ).astype(BRAIN)
        rows_grad[...] = jnp.concatenate([grad, jnp.zeros_like(grad)], axis=0).T.astype(BRAIN)

    if len(items) == 1:
        fill(*items[0])
    else:
        for k, item in enumerate(items):
            pl.when(step == k)(functools.partial(fill, *item))

    probs = jnp.exp(dot(ka_ref[0], queries[...]))
    grad_scores = (probs * dot(va_ref[0], grads[...])).astype(BRAIN)
    added = dot(probs.astype(BRAIN), rows_grad[...]) + dot(grad_scores, qz_ref[0])
    grad_query = (dot(kt_ref[0], grad_scores) * SCALE).T.astype(BRAIN)
    return added, grad_query


def attend_back_own_kernel(*refs):
    forms, item = refs[:5], refs[5:8]
    total_ref, query_ref = refs[8:10]
    scratch = refs[10:]
    step = pl.program_id(0)

    @pl.when(step == 0)
    def _():
        scratch[1][...] = jnp.zeros_like(scratch[1])

    added, grad_query = back_block(step, [item], forms, scratch)
    total_ref[0] = added
    query_ref[0] = grad_query


def attend_back_own(forms, grad, exact, log):
    qt, ka, qz, kt, va, _ = forms
    heads, length = ka.shape[:2]
    rows = length // 4
    by_head = lambda h: (h, 0, 0)
    return pl.pallas_call(
        attend_back_own_kernel,
        grid=(heads,),
        in_specs=[
            pl.BlockSpec((1, LANES, rows), by_head),
            pl.BlockSpec((1, length, LANES), by_head),
            pl.BlockSpec((1, rows, LANES), by_head),
            pl.BlockSpec((1, HEAD_DIM, length), by_head),
            pl.BlockSpec((1, length, LANES), by_head),
            pl.BlockSpec((HEAD_DIM, rows), lambda h: (h, 0)),
            pl.BlockSpec((HEAD_DIM, rows), lambda h: (h, 0)),
            pl.BlockSpec((1, 1, rows), by_head),
        ],
        out_specs=[
            pl.BlockSpec((1, length, LANES), by_head),
            pl.BlockSpec((1, rows, HEAD_DIM), by_head),
        ],
        out_shape=[
            jax.ShapeDtypeStruct((heads, length, LANES), FLOAT),
            jax.ShapeDtypeStruct((heads, rows, HEAD_DIM), BRAIN),
        ],
        scratch_shapes=[
            pltpu.VMEM((LANES, rows), BRAIN),
            pltpu.VMEM((LANES, rows), BRAIN),
            pltpu.VMEM((rows, LANES), BRAIN),
        ],
        compiler_params=pltpu.CompilerParams(vmem_limit_bytes=VMEM_BYTES),
        cost_estimate=pl.CostEstimate(
            flops=18 * length * length * LANES,
            bytes_accessed=8 << 20,
            transcendentals=length * length,
        ),
        name="attend_back_own",
    )(qt, ka, qz, kt, va, grad, exact, log)


def attend_back_kernel(rows, *refs):
    forms, xt_ref = refs[:5], refs[5]
    items = [refs[6 + 3 * k : 9 + 3 * k] for k in range(3)]
    begun_ref, query_ref = refs[15:17]
    out_refs, project_ref, bias_ref = refs[17:21], refs[21], refs[22]
    total = refs[23]
    scratch = refs[24:]
    step = pl.program_id(0)

    @pl.when(step == 0)
    def _():
        scratch[1][...] = jnp.zeros_like(scratch[1])
        total[...] = begun_ref[0]
        out_refs[0][:, 2 * HEAD_DIM :] = query_ref[0]

    added, grad_query = back_block(step, items, forms, scratch)
    total[...] += added
    for k in range(3):

        @pl.when(step == k)
        def _():
            out_refs[k + 1][:, 2 * HEAD_DIM :] = grad_query

    @pl.when(step == 2)
    def _():
        grad_project = jnp.zeros(project_ref.shape, FLOAT)
        bias = jnp.zeros(bias_ref.shape, FLOAT)
        for k in range(4):
            at = pl.ds(k * rows, rows)
            out_refs[k][:, : 2 * HEAD_DIM] = total[at, :].astype(BRAIN)
            piece = out_refs[k][...]
            grad_project += dot(xt_ref[:, at], piece)
            bias += jnp.sum(piece.astype(FLOAT), axis=0, keepdims=True)
        project_ref[...] = grad_project.astype(BRAIN)
        bias_ref[...] = bias


def attend_back(head, forms, grads, exacts, logs, begun, query):
    qt, ka, qz, kt, va, xt = forms
    length, width = ka.shape[1], xt.shape[0]
    rows = length // 4
    cols = 3 * HEAD_DIM
    own = lambda i: (head, 0, 0)
    items, item_specs = [], []
    for item in zip(grads, exacts, logs):
        items += item
        item_specs += [pl.BlockSpec((HEAD_DIM, rows), lambda i: (head, 0))] * 2
        item_specs += [pl.BlockSpec((1, 1, rows), own)]
    return pl.pallas_call(
        functools.partial(attend_back_kernel, rows),
        grid=(3,),
        in_specs=[
            pl.BlockSpec((1, LANES, rows), lambda i: (head, 0, i + 1)),
            pl.BlockSpec((1, length, LANES), own),
            pl.BlockSpec((1, rows, LANES), lambda i: (head, i + 1, 0)),
            pl.BlockSpec((1, HEAD_DIM, length), own),
            pl.BlockSpec((1, length, LANES), own),
            whole((width, length)),
        ]
        + item_specs
        + [pl.BlockSpec((1, length, LANES), own), pl.BlockSpec((1, rows, HEAD_DIM), own)],
        out_specs=[whole((rows, cols))] * 4 + [whole((width, cols)), whole((1, cols))],
        out_shape=[jax.ShapeDtypeStruct((rows, cols), BRAIN)] * 4
        + [jax.ShapeDtypeStruct((width, cols), BRAIN), jax.ShapeDtypeStruct((1, cols), FLOAT)],
        scratch_shapes=[
            pltpu.VMEM((length, LANES), FLOAT),
            pltpu.VMEM((LANES, rows), BRAIN),
            pltpu.VMEM((LANES, rows), BRAIN),
            pltpu.VMEM((rows, LANES), BRAIN),
        ],
        compiler_params=pltpu.CompilerParams(vmem_limit_bytes=VMEM_BYTES),
        cost_estimate=pl.CostEstimate(
            flops=20 * length * length * LANES,
            bytes_accessed=8 << 20,
            transcendentals=length * length,
        ),
        name="attend_back",
    )(qt, ka, qz, kt, va, xt, *items, begun, query)


def gelu_parts(values):
    t = 1.0 / (1.0 + (0.3275911 * 0.7071067811865476) * jnp.abs(values))
    bell = jnp.exp(-0.5 * values * values)
    poly = 0.5 * 1.061405429
    for c in (-1.453152027, 1.421413741, -0.284496736, 0.254829592):
        poly = poly * t + 0.5 * c
    tail = poly * t * bell
    below = jnp.where(values >= 0, 1.0 - tail, tail)
    return values * below, below + values * bell * 0.3989422804014327


def mean_of(values):
    return jnp.mean(values, axis=-1, keepdims=True)


class Portion:
    def __init__(self, *spans):
        self.spans = spans
        self.columns = sum(span[2] for span in spans)


def portions(width, hidden):
    third = 5 * LANES
    if hidden == 6 * LANES:
        return (
            Portion((0, 0, third)),
            Portion((0, third, LANES), (1, 0, 4 * LANES)),
            Portion((1, 4 * LANES, 2 * LANES), (2, 0, 2 * LANES)),
        )
    return (Portion((0, 0, hidden)), Portion((1, 0, hidden)), Portion((2, 0, 2 * LANES)))


def layer_kernel(parts, *refs):
    t_ref = refs[0]
    mixed = refs[1:5]
    x_ref, cot_ref, vec_ref = refs[5:8]
    wide_refs, back_refs = refs[8:13], refs[13:17]
    out_ref, grad_first_ref = refs[17:19]
    d_refs = refs[19:23]
    small_ref = refs[23]
    keeps, sends = refs[24:27], refs[27:30]
    (
        wide,
        back,
        orow,
        normed,
        hb,
        hbt,
        unit_one,
        inv_one,
        act,
        slope,
        acc,
        dfb,
        dfbt,
        stage,
        tail_stage,
        load_sem,
        sem,
        tail_sem,
    ) = refs[30:]
    step = pl.program_id(0)
    half = t_ref[0]
    width = x_ref.shape[1]
    hidden = back.shape[1]
    part = mixed[0].shape[0]
    split = wide.shape[1] // 2
    bias_out, gain_one, shift_one, bias_red, gain_two, shift_two = (
        vec_ref[i : i + 1] for i in range(6)
    )
    wo = lambda k: wide[k, hidden_at : hidden_at + part]
    hidden_at = width

    def loads(k):
        fetched = pl.ds(pl.multiple_of(half * split, 16), split)
        relayed = pl.ds(pl.multiple_of((1 - half) * split, 16), split)
        if k < 2:
            wides = [(wide_refs[k], wide.at[k])]
        elif k == 2:
            wides = [(wide_refs[2], wide.at[2, fetched]), (wide_refs[3], wide.at[2, relayed])]
        else:
            wides = [
                (wide_refs[4].at[pl.ds(0, split)], wide.at[3, fetched]),
                (wide_refs[4].at[pl.ds(split, split)], wide.at[3, relayed]),
            ]
        pairs = wides + [(back_refs[k], back.at[k])]
        return [
            pltpu.make_async_copy(source, target, load_sem.at[k, n])
            for n, (source, target) in enumerate(pairs)
        ]

    @pl.when(step == 0)
    def _():
        every = [loads(k) for k in range(4)]
        for copies_of in every:
            for copy in copies_of:
                copy.start()
        for k, ref in enumerate(mixed):
            orow[:, k * part : (k + 1) * part] = ref[...].astype(FLOAT).T.astype(BRAIN)
        total = x_ref[...].astype(FLOAT) + bias_out
        for copies_of in every:
            for copy in copies_of:
                copy.wait()
        branch = jnp.zeros_like(total)
        for k in range(4):
            branch += dot(orow[:, k * part : (k + 1) * part], wo(k))
        total = total + branch
        center = total - mean_of(total)
        inverse = lax.rsqrt(mean_of(center * center) + EPS)
        unit = center * inverse
        value = unit * gain_one + shift_one
        unit_one[...] = unit
        inv_one[...] = inverse
        normed[...] = value
        hb[...] = value.astype(BRAIN)
        hbt[...] = value.T.astype(BRAIN)
        acc[...] = jnp.zeros_like(acc)

    for j in range(4):

        @pl.when(step == j)
        def _():
            bias = wide[j, hidden_at + part : hidden_at + part + 16].astype(FLOAT)[:1]
            inner = dot(hb[...], wide[j, :width]) + bias
            active, derivative = gelu_parts(inner)
            active = active.astype(BRAIN)
            act[j] = active
            slope[j] = derivative
            acc[...] += dot(active, back[j])

    @pl.when(step == 3)
    def _():
        total = normed[...] + acc[...] + bias_red
        center = total - mean_of(total)
        inverse = lax.rsqrt(mean_of(center * center) + EPS)
        unit = center * inverse
        out_ref[...] = (unit * gain_two + shift_two).astype(BRAIN)
        cot = cot_ref[...].astype(FLOAT)
        scaled = cot * gain_two
        grad = inverse * (scaled - mean_of(scaled) - unit * mean_of(scaled * unit))
        small_ref[3:4] = jnp.sum(grad, axis=0, keepdims=True)
        small_ref[4:5] = jnp.sum(cot * unit, axis=0, keepdims=True)
        small_ref[5:6] = jnp.sum(cot, axis=0, keepdims=True)
        dfb[...] = grad.astype(BRAIN)
        dfbt[...] = grad.T.astype(BRAIN)
        acc[...] = grad

    def outgoing(block, arrays):
        refs_of = keeps if block in (0, 2) else sends
        found = []
        for ref, portion in zip(refs_of, parts):
            at = 0
            for array, first, count in portion.spans:
                if array in arrays:
                    if array == 2:
                        source = tail_stage.at[block, :, pl.ds(first, count)]
                    else:
                        source = stage.at[(7 - block) % 2, array, :, pl.ds(first, count)]
                    found.append((source, ref.at[block // 2, :, pl.ds(at, count)]))
                at += count
        sems = tail_sem if arrays == (2,) else sem
        row = block if arrays == (2,) else (7 - block) % 2
        return [
            pltpu.make_async_copy(source, target, sems.at[row, n])
            for n, (source, target) in enumerate(found)
        ]

    for j in range(4, 8):

        @pl.when(step == j)
        def _():
            block = 7 - j
            slot = j % 2
            if j >= 6:
                for copy in outgoing(block + 2, (0, 1)):
                    copy.wait()
            grad_inner = (dot(dfb[...], back[block], NT) * slope[block]).astype(BRAIN)
            small_ref[8 + block : 9 + block] = jnp.sum(
                grad_inner.astype(FLOAT), axis=0, keepdims=True
            )
            stage[slot, 0] = dot(hbt[...], grad_inner).astype(BRAIN)
            stage[slot, 1] = dot(dfbt[...], act[block]).astype(BRAIN)
            for copy in outgoing(block, (0, 1)):
                copy.start()
            acc[...] += dot(grad_inner, wide[block, :width], NT)

    @pl.when(step == 7)
    def _():
        grad = acc[...]
        unit = unit_one[...]
        small_ref[1:2] = jnp.sum(grad * unit, axis=0, keepdims=True)
        small_ref[2:3] = jnp.sum(grad, axis=0, keepdims=True)
        scaled = grad * gain_one
        first = inv_one[...] * (scaled - mean_of(scaled) - unit * mean_of(scaled * unit))
        small_ref[0:1] = jnp.sum(first, axis=0, keepdims=True)
        grad_first_ref[...] = first
        attend_grad = first.astype(BRAIN)
        for k, ref in enumerate(d_refs):
            ref[...] = dot(wo(k), attend_grad, NT).astype(BRAIN)
        output_grad = dot(first.T.astype(BRAIN), orow[...]).astype(BRAIN)
        last = []
        for k in range(4):
            tail_stage[k, :, :part] = output_grad[:, k * part : (k + 1) * part]
            tail_stage[k, :, part:] = jnp.zeros((width, 2 * LANES - part), BRAIN)
            last += outgoing(k, (2,))
        for copy in last:
            copy.start()
        for block in (1, 0):
            last += outgoing(block, (0, 1))
        for copy in last:
            copy.wait()


def layer(half, mixed, frames, cotangent, vectors, wides, backs):
    rows, width = frames.shape
    part = mixed[0].shape[0]
    deep = wides[0].shape[0]
    hidden = backs[0].shape[0]
    parts = portions(width, hidden)
    grads = [jax.ShapeDtypeStruct((2, width, p.columns), BRAIN) for p in parts]
    grid_spec = pltpu.PrefetchScalarGridSpec(
        num_scalar_prefetch=1,
        grid=(8,),
        in_specs=[whole((part, rows))] * 4
        + [whole((rows, width)), whole((rows, width)), whole(vectors.shape)]
        + [pl.BlockSpec(memory_space=pl.ANY)] * 9,
        out_specs=[whole((rows, width)), whole((rows, width))]
        + [whole((part, rows))] * 4
        + [whole((16, width))]
        + [pl.BlockSpec(memory_space=pl.ANY)] * 6,
        scratch_shapes=[
            pltpu.VMEM((4, deep, width), BRAIN),
            pltpu.VMEM((4, hidden, width), BRAIN),
            pltpu.VMEM((rows, width), BRAIN),
            pltpu.VMEM((rows, width), FLOAT),
            pltpu.VMEM((rows, width), BRAIN),
            pltpu.VMEM((width, rows), BRAIN),
            pltpu.VMEM((rows, width), FLOAT),
            pltpu.VMEM((rows, 1), FLOAT),
            pltpu.VMEM((4, rows, hidden), BRAIN),
            pltpu.VMEM((4, rows, hidden), FLOAT),
            pltpu.VMEM((rows, width), FLOAT),
            pltpu.VMEM((rows, width), BRAIN),
            pltpu.VMEM((width, rows), BRAIN),
            pltpu.VMEM((2, 2, width, hidden), BRAIN),
            pltpu.VMEM((4, width, 2 * LANES), BRAIN),
            pltpu.SemaphoreType.DMA((4, 3)),
            pltpu.SemaphoreType.DMA((2, 4)),
            pltpu.SemaphoreType.DMA((4, 2)),
        ],
    )
    return pl.pallas_call(
        functools.partial(layer_kernel, parts),
        grid_spec=grid_spec,
        out_shape=[
            jax.ShapeDtypeStruct((rows, width), BRAIN),
            jax.ShapeDtypeStruct((rows, width), FLOAT),
        ]
        + [jax.ShapeDtypeStruct((part, rows), BRAIN)] * 4
        + [jax.ShapeDtypeStruct((16, width), FLOAT)]
        + grads
        + grads,
        compiler_params=pltpu.CompilerParams(vmem_limit_bytes=VMEM_BYTES),
        cost_estimate=pl.CostEstimate(
            flops=2 * rows * width * (24 * hidden + 3 * width),
            bytes_accessed=40 << 20,
            transcendentals=8 * rows * hidden,
        ),
        name="layer",
    )(half, *mixed, frames, cotangent, vectors, *wides, *backs)


def frames_kernel(heads, *refs):
    t_ref, base_ref = refs[:2]
    pieces = refs[2 : 2 + 4 * heads]
    w_ref, out_ref, stack, weights = refs[2 + 4 * heads :]
    me = t_ref[0]
    cols = w_ref.shape[2]
    wide = stack.shape[1] // (4 * heads)
    for n in range(4 * heads):
        stack[:, n * wide : n * wide + cols] = pieces[n][...]
        stack[:, n * wide + cols : (n + 1) * wide] = jnp.zeros(
            (stack.shape[0], wide - cols), BRAIN
        )
        weights[n * wide : n * wide + cols] = w_ref[me ^ (n % 4), n // 4]
        weights[n * wide + cols : (n + 1) * wide] = jnp.zeros(
            (wide - cols, weights.shape[1]), BRAIN
        )
    out_ref[...] = base_ref[...] + dot(stack[...], weights[...])


def frames_back(me, base, pieces, weight):
    rows, width = base.shape
    heads, cols = weight.shape[1:3]
    deep = 4 * heads * 2 * LANES
    grid_spec = pltpu.PrefetchScalarGridSpec(
        num_scalar_prefetch=1,
        grid=(1,),
        in_specs=[whole((rows, width))]
        + [whole((rows, cols))] * (4 * heads)
        + [whole(weight.shape)],
        out_specs=whole((rows, width)),
        scratch_shapes=[pltpu.VMEM((rows, deep), BRAIN), pltpu.VMEM((deep, width), BRAIN)],
    )
    return pl.pallas_call(
        functools.partial(frames_kernel, heads),
        grid_spec=grid_spec,
        out_shape=jax.ShapeDtypeStruct((rows, width), FLOAT),
        compiler_params=pltpu.CompilerParams(vmem_limit_bytes=VMEM_BYTES),
        cost_estimate=pl.CostEstimate(
            flops=8 * heads * rows * cols * width, bytes_accessed=8 << 20, transcendentals=0
        ),
        name="frames_back",
    )(me, base, *pieces, weight)


def cut(value, bits, bit):
    at = bits.index(bit)
    front, (lead, rows, columns) = value.shape[:-3], value.shape[-3:]
    view = value.reshape(front + (2**at, 2, lead // 2 ** (at + 1), rows, columns))
    mine = (lax.axis_index("dp") // bit) % 2
    axis = len(front) + 1
    shape = front + (lead // 2, rows, columns)
    keep = lax.dynamic_index_in_dim(view, mine, axis, keepdims=False).reshape(shape)
    send = lax.dynamic_index_in_dim(view, 1 - mine, axis, keepdims=False).reshape(shape)
    return keep, send


def tie(first, second):
    return lax.optimization_barrier((first, second))[0]


class Halving:
    def __init__(self, value, bits, groups, tensor):
        self.value, self.bits, self.groups, self.tensor = value, list(bits), groups, tensor
        self.coming = None

    def send(self, step):
        if step == "tensor":
            self.keep, going = self.value[0], self.value[1]
            self.tensor = False
            self.coming = swap(going, "tensor", 4, 2)
        else:
            self.keep, going = cut(self.value, self.bits, step)
            self.bits = [b for b in self.bits if b != step]
            self.coming = swap(going, "dp", self.groups, step)

    def take(self, last=False):
        value = self.keep.astype(FLOAT) + self.coming.astype(FLOAT)
        self.value = value if last else value.astype(BRAIN)


def body(
    frames,
    segment_ids,
    project_weight,
    query_value_bias,
    output_weight,
    output_bias,
    first_gain,
    first_shift,
    expand_weight,
    expand_bias,
    reduce_weight,
    reduce_bias,
    second_gain,
    second_shift,
    cotangent,
    *,
    groups,
):
    rows, width = frames.shape
    cols = project_weight.shape[2]
    hidden = expand_weight.shape[1]
    heads = cols // HEAD_DIM
    length = 4 * rows
    me = lax.axis_index("tensor")
    scalar = jnp.full((1,), me, jnp.int32)
    half = lax.axis_index("dp") % 2
    other = functools.partial(swap, axis="tensor", size=4)

    far = other(frames, bits=2)
    near = other(frames, bits=1)

    blocks = segment_ids.reshape(4, rows)
    segs = jnp.concatenate([lax.dynamic_index_in_dim(blocks, me ^ k, 0) for k in range(4)], axis=1)
    ids = jnp.arange(IDS, dtype=jnp.int32)
    same = segs.reshape(1, length) == ids[:, None]
    qtail = jnp.pad(same.astype(BRAIN), ((0, HEAD_DIM - IDS), (0, 0)))
    differ = segs.reshape(length, 1) != ids[None, :]
    ktail = jnp.concatenate(
        [
            jnp.where(differ, -BIG, 0.0),
            jnp.full((length, 3), -1.0, FLOAT),
            jnp.zeros((length, LANES - IDS - 3), FLOAT),
        ],
        axis=1,
    )
    vectors = jnp.stack(
        [output_bias, first_gain, first_shift, reduce_bias, second_gain, second_shift]
    ).astype(FLOAT)
    vectors = jnp.pad(vectors, ((0, 2), (0, 0)))
    by_head = project_weight.reshape(3, width, heads, HEAD_DIM)
    turned = jnp.transpose(by_head[::-1], (2, 0, 3, 1)).reshape(heads, 3 * HEAD_DIM, width)
    upper = jnp.pad(by_head[:2], ((0, 0), (0, 0), (0, 0), (HEAD_DIM, 0)))
    lower = jnp.pad(by_head[2:], ((0, 0), (0, 0), (0, 0), (0, HEAD_DIM)))
    spread_weight = jnp.concatenate([upper, lower]).reshape(3, width, heads * LANES)
    bias = query_value_bias.astype(FLOAT).reshape(2, heads, HEAD_DIM)
    bias = jnp.stack(
        [
            jnp.pad(bias[0], ((0, 0), (HEAD_DIM, 0))).reshape(-1),
            jnp.pad(bias[1], ((0, 0), (0, HEAD_DIM))).reshape(-1),
        ]
    )
    wide = jnp.concatenate(
        [
            expand_weight,
            output_weight,
            jnp.pad(expand_bias[None], ((0, 31), (0, 0))),
        ]
    )
    deep = wide.shape[0]
    wide_half = lax.dynamic_index_in_dim(wide.reshape(2, deep // 2, -1), half, 0, False)
    near_wide = other(wide, bits=1)
    near_back = other(reduce_weight, bits=1)
    started = project(0, (frames, near), spread_weight, bias, ktail, qtail, ())

    far, started, turned, wide_half, near_wide, near_back = lax.optimization_barrier(
        (far, started, turned, wide_half, near_wide, near_back)
    )
    last = other(far, bits=1)

    got_wide = other(wide_half, bits=2)
    qt, ka, vt, qz, kt, va, xt = project(
        2, (far, last), spread_weight, bias, ktail, qtail, started
    )
    far_blocks = attend(qt, ka, vt, rows, (2, 3))
    reduce_later = tie(reduce_weight, got_wide)
    far_back = other(reduce_later, bits=2)
    relayed = swap(got_wide, "dp", groups, 1)
    qt_later = tie(qt, got_wide)
    near_blocks = attend(qt_later, ka, vt, rows, (0, 1))
    last_wide = other(jnp.concatenate([got_wide, relayed]), bits=1)
    last_back = other(far_back, bits=1)
    attended = near_blocks + far_blocks
    mixed = [attended[0][0]] + [other(attended[k][0], bits=k) for k in (1, 2, 3)]
    wt = lax.all_gather(tie(turned, far_back), "tensor")

    outs = layer(
        jnp.full((1,), half, jnp.int32),
        mixed,
        frames,
        cotangent,
        vectors,
        (wide, near_wide, got_wide, relayed, last_wide),
        (reduce_weight, near_back, far_back, last_back),
    )
    layer_out, grad_first = outs[:2]
    small = outs[6]
    keeps, sends = outs[7:10], outs[10:13]
    grad_heads = [outs[2]] + [other(outs[2 + k], bits=k) for k in (1, 2, 3)]

    everyone = lax.all_gather(small, ("dp", "tensor")).reshape(groups, 4, 16, width)
    vector_grads = jnp.sum(everyone[:, :, :6], axis=(0, 1))
    picked = [lax.dynamic_index_in_dim(everyone[:, s], 8 + (me ^ s), 1, False) for s in range(4)]
    expand_bias_grad = sum(jnp.sum(p, axis=0) for p in picked)

    bits = [2**n for n in reversed(range(groups.bit_length() - 1))]
    share = width // groups
    steps = ["tensor"] + bits[::-1]
    orders = [steps[n:3] + steps[:n] for n in range(3)]
    arrived = [other(send, bits=1) for send in sends]
    forms = (qt, ka, qz, kt, va, xt)
    exacts = [a[1] for a in attended]
    logs = [a[2] for a in attended]
    begun, query = attend_back_own(forms, grad_heads[0], exacts[0], logs[0])
    arrived, begun = lax.optimization_barrier((arrived, begun))
    sums = []
    for keep, come in zip(keeps, arrived):
        value = (keep.astype(FLOAT) + come.astype(FLOAT)).astype(BRAIN)
        sums.append(Halving(value.reshape(2, groups, share, -1), bits, groups, True))

    project_parts, pieces = [], []
    spread = 3 * HEAD_DIM // share
    for h in range(heads):
        for value, order in zip(sums, orders):
            value.send(order[h])
        begun = tie(begun, [value.keep for value in sums])
        res = attend_back(h, forms, grad_heads[1:], exacts[1:], logs[1:], begun, query)
        held = lax.optimization_barrier((res, [value.coming for value in sums]))
        res = held[0]
        for value, come in zip(sums, held[1]):
            value.coming = come
            value.take()
        pieces += [res[0]] + [other(res[k], bits=k) for k in (1, 2, 3)]
        bias_sum = jnp.broadcast_to(res[5].reshape(1, spread, share), (groups, spread, share))
        project_parts.append(
            jnp.concatenate(
                [
                    res[4].reshape(groups, share, 3 * HEAD_DIM),
                    jnp.swapaxes(bias_sum, 1, 2).astype(BRAIN),
                    jnp.zeros((groups, share, 2 * LANES - 3 * HEAD_DIM - spread), BRAIN),
                ],
                axis=2,
            )
        )
    rest = steps[3:]
    joined = Halving(
        jnp.concatenate([value.value for value in sums], axis=-1), rest[::-1], groups, False
    )
    for n, step in enumerate(rest):
        joined.send(step)
        joined.take(n == len(rest) - 1)
    tail = Halving(jnp.concatenate(project_parts, axis=-1), bits, groups, False)
    for n, step in enumerate(bits[::-1]):
        tail.send(step)
        tail.take(n == len(bits) - 1)
    frames_grad = frames_back(scalar, grad_first, pieces, wt)

    arrays = [[], [], []]
    at = 0
    for portion in portions(width, hidden):
        for array, _, count in portion.spans:
            arrays[array].append(joined.value[0][:, at : at + count])
            at += count
    expand_grad, reduce_grad, output_grad = [jnp.concatenate(a, axis=1) for a in arrays]
    reduce_grad = reduce_grad.T
    output_grad = output_grad[:, :cols].T

    summed = tail.value[0].reshape(share, heads, 2 * LANES)
    project_grad = jnp.stack(
        [
            summed[:, :, (2 - i) * HEAD_DIM : (3 - i) * HEAD_DIM].reshape(share, cols)
            for i in range(3)
        ]
    )
    bias_sums = jnp.transpose(summed[:, :, 3 * HEAD_DIM : 3 * HEAD_DIM + spread], (1, 2, 0))
    bias_sums = bias_sums.reshape(heads, 3, HEAD_DIM)
    attend_bias_grad = jnp.stack([bias_sums[:, i].reshape(cols) for i in (2, 0)])
    return (
        layer_out,
        frames_grad,
        project_grad,
        attend_bias_grad,
        output_grad,
        expand_grad,
        expand_bias_grad,
        reduce_grad,
        vector_grads,
    )


def solution(mesh):
    placed = (
        P(("dp", "tensor"), None),
        P("dp", None),
        P(None, None, "tensor"),
        P(None, "tensor"),
        P("tensor", None),
        P(),
        P(),
        P(),
        P(None, "tensor"),
        P("tensor"),
        P("tensor", None),
        P(),
        P(),
        P(),
        P(("dp", "tensor"), None),
    )
    return jax.shard_map(
        functools.partial(body, groups=mesh.shape["dp"]),
        mesh=mesh,
        in_specs=placed,
        out_specs=(
            P(("dp", "tensor"), None),
            P(("dp", "tensor"), None),
            P(None, "dp", "tensor"),
            P(None, "tensor"),
            P("tensor", "dp"),
            P("dp", "tensor"),
            P("tensor"),
            P("tensor", "dp"),
            P(),
        ),
        check_vma=False,
    )
```

```python
import functools

import jax
import jax.numpy as jnp
import numpy as np
from jax import lax
from jax.experimental import pallas as pl
from jax.experimental.pallas import tpu as pltpu
from jax.sharding import PartitionSpec as P

HEAD_DIM = 64
ROW_LEN = 2048
EPS = 1e-05
FLOAT = jnp.float32
BRAIN = jnp.bfloat16
BIG = 1e30
SCALE = HEAD_DIM ** (-0.5)
VMEM_BYTES = 60 << 20
IDS = 8
LANES = 128
CHUNK = 1024
BACK_CHUNK = 512

NN = (((1,), (0,)), ((), ()))
NT = (((1,), (1,)), ((), ()))


def dot(left, right, dims=NN):
    return lax.dot_general(left, right, dims, preferred_element_type=FLOAT)


def swap(value, axis, size, bits):
    return lax.ppermute(value, axis, [(i, i ^ bits) for i in range(size)])


def whole(shape):
    return pl.BlockSpec(shape, lambda *_: (0,) * len(shape), pipeline_mode=pl.Buffered(1))


def split_three(value):
    top = value.astype(BRAIN).astype(FLOAT)
    rest = value - top
    middle = rest.astype(BRAIN).astype(FLOAT)
    return top, middle, rest - middle


def project_kernel(heads, rows, *refs):
    x_refs = refs[:2]
    w_ref, bias_ref, ktail_ref, qtail_ref = refs[2:6]
    qt_ref, ka_ref, vt_ref, qz_ref, kt_ref, va_ref, xt_ref = refs[-8:-1]
    held = refs[-1]
    step = pl.program_id(0)
    for k in range(2):

        @pl.when(step == k)
        def _():
            held[...] = x_refs[k][...]

    x = held[...]
    xt_ref[...] = x.T
    lane = lax.broadcasted_iota(jnp.int32, (rows, LANES), 1)
    minus = jnp.where((lane >= HEAD_DIM) & (lane < HEAD_DIM + 3), -1.0, 0.0)
    query = (dot(x, w_ref[0]) + bias_ref[0:1]).astype(BRAIN).astype(FLOAT) * SCALE
    key = dot(x, w_ref[1])
    value = dot(x, w_ref[2]) + bias_ref[1:2]
    for h in range(heads):
        own = slice(h * LANES, (h + 1) * LANES)
        q, k_, v = query[:, own], key[:, own], value[:, own]
        qt_ref[h, :HEAD_DIM, :] = qtail_ref[...]
        qt_ref[h, HEAD_DIM:, :] = q.T[HEAD_DIM:].astype(BRAIN)
        kt_ref[h] = k_.T[HEAD_DIM:].astype(BRAIN)
        vt_ref[h] = v.T[:HEAD_DIM].astype(BRAIN)
        ka_ref[h] = (k_ + ktail_ref[...]).astype(BRAIN)
        va_ref[h] = (v + minus).astype(BRAIN)
        qz_ref[h, :HEAD_DIM, :] = jnp.zeros((HEAD_DIM, rows), BRAIN)
        qz_ref[h, HEAD_DIM:, :] = qt_ref[h, HEAD_DIM:, :]


def project(first, pieces, weight, bias, ktail, qtail, before):
    rows, width = pieces[0].shape
    heads = weight.shape[2] // LANES
    length = 4 * rows
    by_lane = lambda i: (0, 0, first + i)
    by_row = lambda i: (0, first + i, 0)
    shapes = [
        ((heads, LANES, length), (heads, LANES, rows), by_lane),
        ((heads, length, LANES), (heads, rows, LANES), by_row),
        ((heads, HEAD_DIM, length), (heads, HEAD_DIM, rows), by_lane),
        ((heads, LANES, length), (heads, LANES, rows), by_lane),
        ((heads, HEAD_DIM, length), (heads, HEAD_DIM, rows), by_lane),
        ((heads, length, LANES), (heads, rows, LANES), by_row),
        ((width, length), (width, rows), lambda i: (0, first + i)),
    ]
    return pl.pallas_call(
        functools.partial(project_kernel, heads, rows),
        grid=(2,),
        in_specs=[
            whole((rows, width)),
            whole((rows, width)),
            whole(weight.shape),
            whole(bias.shape),
            pl.BlockSpec((rows, LANES), lambda i: (first + i, 0)),
            pl.BlockSpec((HEAD_DIM, rows), lambda i: (0, first + i)),
        ]
        + [pl.BlockSpec(memory_space=pl.ANY)] * len(before),
        out_specs=[pl.BlockSpec(block, index) for _, block, index in shapes],
        out_shape=[jax.ShapeDtypeStruct(s, BRAIN) for s, _, _ in shapes],
        scratch_shapes=[pltpu.VMEM((rows, width), BRAIN)],
        input_output_aliases={6 + n: n for n in range(len(before))},
        compiler_params=pltpu.CompilerParams(vmem_limit_bytes=VMEM_BYTES),
        cost_estimate=pl.CostEstimate(
            flops=12 * rows * width * weight.shape[2], bytes_accessed=8 << 20, transcendentals=0
        ),
        name="project",
    )(*pieces, weight, bias, ktail, qtail, *before)


def attend_kernel(rows, count, *refs):
    qt_ref, ka_ref, vt_ref = refs[:3]
    out_refs, exact_ref, log_ref, held = refs[3:-3], refs[-3], refs[-2], refs[-1]
    length = ka_ref.shape[1]
    part, chunk = held.shape[2], min(CHUNK, length)
    chunks = [slice(at, at + chunk) for at in range(0, length, chunk)]
    items = [(n, at) for n in range(count) for at in range(0, rows, part)]

    def score(item, keys):
        n, at = items[item]
        first = n * rows + at
        scores = dot(ka_ref[0, keys], qt_ref[0, :, first : first + part])
        held[item % 2, keys] = scores
        return jnp.max(scores, axis=0, keepdims=True)

    highest = functools.reduce(jnp.maximum, [score(0, keys) for keys in chunks])
    for item, (n, at) in enumerate(items):
        tops, total, mixed = [], 0.0, 0.0
        for keys in chunks:
            if item + 1 < len(items):
                tops.append(score(item + 1, keys))
            raised = jnp.exp(held[item % 2, keys] - highest)
            total = total + jnp.sum(raised, axis=0, keepdims=True)
            mixed = mixed + dot(vt_ref[0, :, keys], raised.astype(BRAIN))
        mixed = mixed / total
        lanes = slice(at, at + part)
        if len(out_refs) == 1:
            out_refs[0][n, :, lanes] = mixed.astype(BRAIN)
        else:
            out_refs[n][0, :, lanes] = mixed.astype(BRAIN)
        exact_ref[n, :, lanes] = mixed
        log_ref[0, n : n + 1, lanes] = highest + jnp.log(total)
        if tops:
            highest = functools.reduce(jnp.maximum, tops)


def attend(qt, ka, vt, rows, first, count, parted):
    heads, _, length = qt.shape
    cols = heads * HEAD_DIM
    by_head = lambda h: (0, h, 0)
    sizes = [1] * count if parted else [count]
    outs = pl.pallas_call(
        functools.partial(attend_kernel, rows, count),
        grid=(heads,),
        in_specs=[
            pl.BlockSpec((1, LANES, count * rows), lambda h: (h, 0, first // count)),
            pl.BlockSpec((1, length, LANES), lambda h: (h, 0, 0)),
            pl.BlockSpec((1, HEAD_DIM, length), lambda h: (h, 0, 0)),
        ],
        out_specs=[pl.BlockSpec((n, HEAD_DIM, rows), by_head) for n in sizes]
        + [
            pl.BlockSpec((count, HEAD_DIM, rows), by_head),
            pl.BlockSpec((1, count, rows), lambda h: (h, 0, 0)),
        ],
        out_shape=[jax.ShapeDtypeStruct((n, cols, rows), BRAIN) for n in sizes]
        + [
            jax.ShapeDtypeStruct((count, cols, rows), FLOAT),
            jax.ShapeDtypeStruct((heads, count, rows), FLOAT),
        ],
        scratch_shapes=[pltpu.VMEM((2, length, rows // 2), FLOAT)],
        compiler_params=pltpu.CompilerParams(vmem_limit_bytes=VMEM_BYTES),
        cost_estimate=pl.CostEstimate(
            flops=8 * heads * length * count * rows * LANES,
            bytes_accessed=8 << 20,
            transcendentals=heads * length * count * rows,
        ),
        name="attend",
    )(qt, ka, vt)
    return outs[:-2], outs[-2], outs[-1]


def fill(slot, queries, grads, plain, qt, grad, exact, log):
    rows = queries.shape[2]
    low = lax.broadcasted_iota(jnp.int32, (8, rows), 0)

    def stacked(value):
        top, middle, bottom = split_three(value)
        return jnp.where(
            low == 0, top, jnp.where(low == 1, middle, jnp.where(low == 2, bottom, 0.0))
        )

    nothing = jnp.zeros((LANES - HEAD_DIM - 16, rows), BRAIN)
    delta = jnp.sum(grad.astype(FLOAT) * exact, axis=0, keepdims=True)
    ids = qt[:16].astype(FLOAT)[:IDS]
    queries[slot, :16] = jnp.concatenate([ids, stacked(log)], axis=0).astype(BRAIN)
    queries[slot, 16:] = qt[16:]
    grads[slot, :HEAD_DIM] = grad
    grads[slot, HEAD_DIM : HEAD_DIM + 16] = jnp.concatenate(
        [stacked(delta), jnp.zeros((8, rows), FLOAT)], axis=0
    ).astype(BRAIN)
    grads[slot, HEAD_DIM + 16 :] = nothing
    plain[slot, :HEAD_DIM] = grad
    plain[slot, HEAD_DIM:] = jnp.zeros((LANES - HEAD_DIM, rows), BRAIN)


def back_block(slot, queries, grads, plain, qz, ka_ref, kt_ref, va_ref, add):
    length = ka_ref.shape[1]
    chunk = min(BACK_CHUNK, length)
    grad_query = 0.0
    for at in range(0, length, chunk):
        keys = slice(at, at + chunk)
        probs = jnp.exp(dot(ka_ref[0, keys], queries[slot]))
        grad_scores = (probs * dot(va_ref[0, keys], grads[slot])).astype(BRAIN)
        add(keys, dot(probs.astype(BRAIN), plain[slot], NT) + dot(grad_scores, qz, NT))
        grad_query = grad_query + dot(kt_ref[0, :, keys], grad_scores)
    return (grad_query * SCALE).T.astype(BRAIN)


def attend_back_own_kernel(*refs):
    qt_ref, ka_ref, qz_ref, kt_ref, va_ref = refs[:5]
    grad_ref, exact_ref, log_ref = refs[5:8]
    total_ref, query_ref = refs[8:10]
    scratch = refs[10:]
    fill(0, *scratch, qt_ref[0], grad_ref[0], exact_ref[0], log_ref[0, 0:1])

    def add(keys, value):
        total_ref[0, keys] = value

    query_ref[0] = back_block(0, *scratch, qz_ref[0], ka_ref, kt_ref, va_ref, add)


def attend_back_own(forms, grad, exact, log):
    qt, ka, qz, kt, va, _ = forms
    heads, length = ka.shape[:2]
    rows = length // 4
    by_head = lambda h: (h, 0, 0)
    return pl.pallas_call(
        attend_back_own_kernel,
        grid=(heads,),
        in_specs=[
            pl.BlockSpec((1, LANES, rows), by_head),
            pl.BlockSpec((1, length, LANES), by_head),
            pl.BlockSpec((1, LANES, rows), by_head),
            pl.BlockSpec((1, HEAD_DIM, length), by_head),
            pl.BlockSpec((1, length, LANES), by_head),
            pl.BlockSpec((1, HEAD_DIM, rows), lambda h: (0, h, 0)),
            pl.BlockSpec((1, HEAD_DIM, rows), lambda h: (0, h, 0)),
            pl.BlockSpec((1, 2, rows), by_head),
        ],
        out_specs=[
            pl.BlockSpec((1, length, LANES), by_head),
            pl.BlockSpec((1, rows, HEAD_DIM), by_head),
        ],
        out_shape=[
            jax.ShapeDtypeStruct((heads, length, LANES), FLOAT),
            jax.ShapeDtypeStruct((heads, rows, HEAD_DIM), BRAIN),
        ],
        scratch_shapes=[pltpu.VMEM((1, LANES, rows), BRAIN)] * 3,
        compiler_params=pltpu.CompilerParams(vmem_limit_bytes=VMEM_BYTES),
        cost_estimate=pl.CostEstimate(
            flops=18 * length * length * LANES,
            bytes_accessed=8 << 20,
            transcendentals=length * length,
        ),
        name="attend_back_own",
    )(qt, ka, qz, kt, va, grad, exact, log)


def attend_back_kernel(rows, first, share, *refs):
    qt_ref, ka_ref, qz_ref, kt_ref, va_ref, xt_ref = refs[:6]
    grad_refs, exacts, logs = refs[6:9], refs[9:12], refs[12:14]
    begun_ref, query_ref = refs[14:16]
    own_ref, near_ref, far_ref, project_ref = refs[16:20]
    out_refs = (own_ref.at[0], near_ref.at[0], far_ref.at[0, 0], far_ref.at[0, 1])
    total, begun, xt = refs[20:23]
    scratch = refs[23:26]
    sem = refs[26]
    step = pl.program_id(0)
    begun_copy = pltpu.make_async_copy(begun_ref.at[first + step], begun, sem.at[0])
    xt_copy = pltpu.make_async_copy(xt_ref, xt, sem.at[1])
    begun_copy.start()
    pl.when(step == 0)(xt_copy.start)
    for k in range(3):
        at = pl.ds((k + 1) * rows, rows)
        log = logs[(k + 1) // 2][0, (k + 1) % 2 : (k + 1) % 2 + 1]
        fill(k, *scratch, qt_ref[0, :, at], grad_refs[k][0], exacts[k][0], log)
    out_refs[0][:, 2 * HEAD_DIM :] = query_ref[0]
    for k in range(3):

        def add(keys, value):
            if k == 0:
                total[keys] = value
            else:
                total[keys] += value

        qz = qz_ref[0, :, pl.ds((k + 1) * rows, rows)]
        grad_query = back_block(k, *scratch, qz, ka_ref, kt_ref, va_ref, add)
        out_refs[k + 1][:, 2 * HEAD_DIM :] = grad_query
    begun_copy.wait()
    pl.when(step == 0)(xt_copy.wait)
    cols = 3 * HEAD_DIM
    grad_project = jnp.zeros((project_ref.shape[1], cols), FLOAT)
    bias = jnp.zeros((1, cols), FLOAT)
    for k in range(4):
        at = pl.ds(k * rows, rows)
        out_refs[k][:, : 2 * HEAD_DIM] = (total[at] + begun[at]).astype(BRAIN)
        piece = out_refs[k][...]
        grad_project += dot(xt[:, at], piece)
        bias += jnp.sum(piece.astype(FLOAT), axis=0, keepdims=True)
    project_ref[0, :, :cols] = grad_project.astype(BRAIN)
    project_ref[0, :, cols:] = jnp.zeros((project_ref.shape[1], 2 * LANES - cols), BRAIN)
    if share % 16 == 0:
        spread = cols // share
        line = jnp.concatenate(
            [bias[:, n * share : (n + 1) * share] for n in range(spread)]
            + [jnp.zeros((8 - spread, share), FLOAT)],
            axis=0,
        ).T.astype(BRAIN)
        for at in range(0, project_ref.shape[1], share):
            project_ref[0, at : at + share, cols : cols + 8] = line
    else:
        refs[27][0] = bias


def attend_back(first, count, share, forms, grads, exacts, logs, begun, query):
    qt, ka, qz, kt, va, xt = forms
    length, width = ka.shape[1], xt.shape[0]
    rows = length // 4
    cols = 3 * HEAD_DIM
    own = lambda i: (first + i, 0, 0)
    by_block = lambda n: pl.BlockSpec((1, HEAD_DIM, rows), lambda i: (n, first + i, 0))
    each = lambda i: (i, 0, 0)
    out_specs = [
        pl.BlockSpec((1, rows, cols), each),
        pl.BlockSpec((1, rows, cols), each),
        pl.BlockSpec((1, 2, rows, cols), lambda i: (i, 0, 0, 0)),
        pl.BlockSpec((1, width, 2 * LANES), each),
    ]
    out_shape = [
        jax.ShapeDtypeStruct((count, rows, cols), BRAIN),
        jax.ShapeDtypeStruct((count, rows, cols), BRAIN),
        jax.ShapeDtypeStruct((count, 2, rows, cols), BRAIN),
        jax.ShapeDtypeStruct((count, width, 2 * LANES), BRAIN),
    ]
    scratch = (
        [
            pltpu.VMEM((length, LANES), FLOAT),
            pltpu.VMEM((length, LANES), FLOAT),
            pltpu.VMEM((width, length), BRAIN),
        ]
        + [pltpu.VMEM((3, LANES, rows), BRAIN)] * 3
        + [pltpu.SemaphoreType.DMA((2,))]
    )
    kernel = functools.partial(attend_back_kernel, rows, first, share)
    if share % 16:
        out_specs.append(pl.BlockSpec((1, 1, cols), each))
        out_shape.append(jax.ShapeDtypeStruct((count, 1, cols), FLOAT))
        kernel = lambda *refs: attend_back_kernel(
            rows, first, share, *refs[:20], *refs[21:], refs[20]
        )
    res = pl.pallas_call(
        kernel,
        grid=(count,),
        in_specs=[
            pl.BlockSpec((1, LANES, length), own),
            pl.BlockSpec((1, length, LANES), own),
            pl.BlockSpec((1, LANES, length), own),
            pl.BlockSpec((1, HEAD_DIM, length), own),
            pl.BlockSpec((1, length, LANES), own),
            pl.BlockSpec(memory_space=pl.ANY),
        ]
        + [by_block(0)] * 3
        + [by_block(1), by_block(0), by_block(1)]
        + [pl.BlockSpec((1, 2, rows), own)] * 2
        + [pl.BlockSpec(memory_space=pl.ANY), pl.BlockSpec((1, rows, HEAD_DIM), own)],
        out_specs=out_specs,
        out_shape=out_shape,
        scratch_shapes=scratch,
        compiler_params=pltpu.CompilerParams(vmem_limit_bytes=VMEM_BYTES),
        cost_estimate=pl.CostEstimate(
            flops=20 * count * length * length * LANES,
            bytes_accessed=8 << 20,
            transcendentals=count * length * length,
        ),
        name="attend_back",
    )(qt, ka, qz, kt, va, xt, *grads, exacts[0], exacts[1], exacts[1], *logs, begun, query)
    own_piece, near, far, project_grad = res[:4]
    project_grad = project_grad.reshape(count, width // share, share, 2 * LANES)
    if share % 16:
        spread = cols // share
        bias = jnp.swapaxes(res[4].reshape(count, 1, spread, share), 2, 3).astype(BRAIN)
        bias = jnp.broadcast_to(bias, (count, width // share, share, spread))
        project_grad = jnp.concatenate(
            [
                project_grad[..., :cols],
                bias,
                jnp.zeros(project_grad.shape[:3] + (2 * LANES - cols - spread,), BRAIN),
            ],
            axis=3,
        )
    return own_piece, near, far, project_grad


def gelu_parts(values):
    t = 1.0 / (1.0 + (0.3275911 * 0.7071067811865476) * jnp.abs(values))
    bell = jnp.exp(-0.5 * values * values)
    poly = 0.5 * 1.061405429
    for c in (-1.453152027, 1.421413741, -0.284496736, 0.254829592):
        poly = poly * t + 0.5 * c
    tail = poly * t * bell
    below = jnp.where(values >= 0, 1.0 - tail, tail)
    return values * below, below + values * bell * 0.3989422804014327


def mean_of(values):
    return jnp.mean(values, axis=-1, keepdims=True)


class Portion:
    def __init__(self, *spans):
        self.spans = spans
        self.columns = sum(span[2] for span in spans)


def portions(width, hidden):
    third = 5 * LANES
    if hidden == 6 * LANES:
        return (
            Portion((0, 0, third)),
            Portion((0, third, LANES), (1, 0, 4 * LANES)),
            Portion((1, 4 * LANES, 2 * LANES), (2, 0, 2 * LANES)),
        )
    return (Portion((0, 0, hidden)), Portion((1, 0, hidden)), Portion((2, 0, 2 * LANES)))


def layer_kernel(parts, hidden, *refs):
    t_ref = refs[0]
    mixed = refs[1:5]
    x_ref, cot_ref, vec_ref = refs[5:8]
    wide_refs, back_refs = refs[8:13], refs[13:18]
    out_ref, grad_first_ref = refs[18:20]
    d_refs = (refs[20].at[0], refs[21].at[0], refs[22].at[0], refs[22].at[1])
    small_ref = refs[23]
    keeps, sends = refs[24:27], refs[27:30]
    wet, wo, eb, back, orow, act, slope, dz, stage, tail_stage = refs[30:40]
    wide_sem, back_sem, out_sem = refs[40:]
    half, back_half = t_ref[0], t_ref[1]
    width = x_ref.shape[1]
    part = mixed[0].shape[1]
    bias_out, gain_one, shift_one, bias_red, gain_two, shift_two = (
        vec_ref[i : i + 1] for i in range(6)
    )

    split = hidden // 2 + part // 2 + 16

    def load_wide(k, n):
        if k < 2:
            source, first, which = wide_refs[k], n * split, n
        elif k == 2:
            source, first, which = wide_refs[2 + n], 0, (half, 1 - half)[n]
        else:
            source, first, which = wide_refs[4], n * split, (half, 1 - half)[n]
        found = []
        for m, (at, count, target, to) in enumerate(
            [
                (0, hidden // 2, wet, k * hidden + which * (hidden // 2)),
                (hidden // 2, part // 2, wo, k * part + which * (part // 2)),
                (hidden // 2 + part // 2, 16, eb.at[k], which * 16),
            ]
        ):
            to = to if isinstance(to, int) else pl.multiple_of(to, 16)
            found.append(
                pltpu.make_async_copy(
                    source.at[pl.ds(first + at, count)],
                    target.at[pl.ds(to, count)],
                    wide_sem.at[k, n, m],
                )
            )
        return found

    loads = [[load_wide(k, n) for n in range(2)] for k in range(4)]
    def load_back(k, n):
        if k < 2:
            source, first, which = back_refs[k], n * (hidden // 2), n
        elif k == 2:
            source, first, which = back_refs[2 + n], 0, (back_half, 1 - back_half)[n]
        else:
            source, first = back_refs[4], n * (hidden // 2)
            which = (back_half, 1 - back_half)[n]
        to = k * hidden + which * (hidden // 2)
        to = to if isinstance(to, int) else pl.multiple_of(to, 16)
        return pltpu.make_async_copy(
            source.at[pl.ds(first, hidden // 2)],
            back.at[pl.ds(to, hidden // 2)],
            back_sem.at[k, n],
        )

    back_loads = [load_back(k, n) for k in range(4) for n in range(2)]

    def each(kind, k=None):
        return [c[kind] for pair in (loads if k is None else [loads[k]]) for c in pair]

    for copy in each(1):
        copy.start()
    for k in range(4):
        for copy in each(0, k) + each(2, k):
            copy.start()
    for k, ref in enumerate(mixed):
        orow[:, k * part : (k + 1) * part] = ref[0].astype(FLOAT).T.astype(BRAIN)
    for copy in each(1):
        copy.wait()
    for copy in back_loads:
        copy.start()
    total = x_ref[...].astype(FLOAT) + bias_out + dot(orow[...], wo[...])
    center = total - mean_of(total)
    inverse_one = lax.rsqrt(mean_of(center * center) + EPS)
    unit_one = center * inverse_one
    normed = unit_one * gain_one + shift_one
    hb = normed.astype(BRAIN)
    hbt = normed.T.astype(BRAIN)

    owns = [slice(j * hidden, (j + 1) * hidden) for j in range(4)]
    for copy in each(0) + each(2):
        copy.wait()
    inner = dot(hb, wet[owns[0]], NT)
    for j in range(4):
        now = inner + eb[j, :16].astype(FLOAT)[:1]
        if j < 3:
            inner = dot(hb, wet[owns[j + 1]], NT)
        active, derivative = gelu_parts(now)
        act[:, owns[j]] = active.astype(BRAIN)
        slope[:, owns[j]] = derivative
    for copy in back_loads:
        copy.wait()
    total = normed + dot(act[...], back[...]) + bias_red
    center = total - mean_of(total)
    inverse = lax.rsqrt(mean_of(center * center) + EPS)
    unit = center * inverse
    out_ref[...] = (unit * gain_two + shift_two).astype(BRAIN)
    cot = cot_ref[...].astype(FLOAT)
    scaled = cot * gain_two
    grad = inverse * (scaled - mean_of(scaled) - unit * mean_of(scaled * unit))
    small_ref[3:4] = jnp.sum(grad, axis=0, keepdims=True)
    small_ref[4:5] = jnp.sum(cot * unit, axis=0, keepdims=True)
    small_ref[5:6] = jnp.sum(cot, axis=0, keepdims=True)
    dfb = grad.astype(BRAIN)
    dfbt = grad.T.astype(BRAIN)

    def outgoing(block, array, first_sem):
        found = []
        for ref, portion in zip(keeps if block in (0, 2) else sends, parts):
            at = 0
            for held, first, count in portion.spans:
                if held == array:
                    source = tail_stage.at[block] if array == 2 else stage.at[block, array]
                    found.append(
                        pltpu.make_async_copy(
                            source.at[:, pl.ds(first, count)],
                            ref.at[block // 2, :, pl.ds(at, count)],
                            out_sem.at[block, first_sem + len(found)],
                        )
                    )
                at += count
        return found

    order = (1, 3, 0, 2)
    started = []
    for j in order:
        stage[j, 1] = dot(dfbt, act[:, owns[j]]).astype(BRAIN)
        copies = outgoing(j, 1, 2)
        for copy in copies:
            copy.start()
        started += copies
    grad_active = dot(dfb, back[owns[order[0]]], NT)
    for n, j in enumerate(order):
        now = grad_active
        if n < 3:
            grad_active = dot(dfb, back[owns[order[n + 1]]], NT)
        grad_inner = (now * slope[:, owns[j]]).astype(BRAIN)
        dz[:, owns[j]] = grad_inner
        small_ref[8 + j : 9 + j] = jnp.sum(grad_inner.astype(FLOAT), axis=0, keepdims=True)
        stage[j, 0] = dot(hbt, grad_inner).astype(BRAIN)
        copies = outgoing(j, 0, 0)
        for copy in copies:
            copy.start()
        started += copies
    grad = grad + dot(dz[...], wet[...])
    small_ref[1:2] = jnp.sum(grad * unit_one, axis=0, keepdims=True)
    small_ref[2:3] = jnp.sum(grad, axis=0, keepdims=True)
    scaled = grad * gain_one
    first = inverse_one * (scaled - mean_of(scaled) - unit_one * mean_of(scaled * unit_one))
    small_ref[0:1] = jnp.sum(first, axis=0, keepdims=True)
    small_ref[6:8] = jnp.zeros((2, width), FLOAT)
    small_ref[12:] = jnp.zeros((4, width), FLOAT)
    grad_first_ref[...] = first
    grad_mixed = dot(wo[...], first.astype(BRAIN), NT).astype(BRAIN)
    for k, ref in enumerate(d_refs):
        ref[...] = grad_mixed[k * part : (k + 1) * part]
    output_grad = dot(first.T.astype(BRAIN), orow[...]).astype(BRAIN)
    for k in range(4):
        tail_stage[k, :, :part] = output_grad[:, k * part : (k + 1) * part]
        tail_stage[k, :, part:] = jnp.zeros((width, 2 * LANES - part), BRAIN)
        copies = outgoing(k, 2, 4)
        for copy in copies:
            copy.start()
        started += copies
    for copy in started:
        copy.wait()


def layer(halves, mixed, frames, cotangent, vectors, wides, backs):
    rows, width = frames.shape
    part = mixed[0].shape[1]
    hidden = backs[0].shape[0]
    parts = portions(width, hidden)
    grads = [jax.ShapeDtypeStruct((2, width, p.columns), BRAIN) for p in parts]
    grid_spec = pltpu.PrefetchScalarGridSpec(
        num_scalar_prefetch=1,
        grid=(1,),
        in_specs=[whole((1, part, rows))] * 4
        + [whole((rows, width)), whole((rows, width)), whole(vectors.shape)]
        + [pl.BlockSpec(memory_space=pl.ANY)] * 10,
        out_specs=[whole((rows, width)), whole((rows, width))]
        + [whole((n, part, rows)) for n in (1, 1, 2)]
        + [whole((16, width))]
        + [pl.BlockSpec(memory_space=pl.ANY)] * 6,
        scratch_shapes=[
            pltpu.VMEM((4 * hidden, width), BRAIN),
            pltpu.VMEM((4 * part, width), BRAIN),
            pltpu.VMEM((4, 32, width), BRAIN),
            pltpu.VMEM((4 * hidden, width), BRAIN),
            pltpu.VMEM((rows, width), BRAIN),
            pltpu.VMEM((rows, 4 * hidden), BRAIN),
            pltpu.VMEM((rows, 4 * hidden), FLOAT),
            pltpu.VMEM((rows, 4 * hidden), BRAIN),
            pltpu.VMEM((4, 2, width, hidden), BRAIN),
            pltpu.VMEM((4, width, 2 * LANES), BRAIN),
            pltpu.SemaphoreType.DMA((4, 2, 3)),
            pltpu.SemaphoreType.DMA((4, 2)),
            pltpu.SemaphoreType.DMA((4, 6)),
        ],
    )
    return pl.pallas_call(
        functools.partial(layer_kernel, parts, hidden),
        grid_spec=grid_spec,
        out_shape=[
            jax.ShapeDtypeStruct((rows, width), BRAIN),
            jax.ShapeDtypeStruct((rows, width), FLOAT),
        ]
        + [jax.ShapeDtypeStruct((n, part, rows), BRAIN) for n in (1, 1, 2)]
        + [jax.ShapeDtypeStruct((16, width), FLOAT)]
        + grads
        + grads,
        compiler_params=pltpu.CompilerParams(vmem_limit_bytes=VMEM_BYTES),
        cost_estimate=pl.CostEstimate(
            flops=2 * rows * width * (24 * hidden + 3 * width),
            bytes_accessed=40 << 20,
            transcendentals=8 * rows * hidden,
        ),
        name="layer",
    )(halves, *mixed, frames, cotangent, vectors, *wides, *backs)


def frames_kernel(count, *refs):
    t_ref, base_ref = refs[:2]
    pieces = refs[2:6]
    w_ref, out_ref, stack, weights = refs[6:]
    me = t_ref[0]
    cols = w_ref.shape[2]
    wide = 2 * LANES
    nothing = jnp.zeros((stack.shape[0], wide - cols), BRAIN)
    below = jnp.zeros((wide - cols, weights.shape[1]), BRAIN)
    for h in range(count):
        for k in range(4):
            at = (4 * h + k) * wide
            piece = pieces[k][h, 0] if k == 2 else pieces[k][h]
            stack[:, at : at + cols] = piece
            stack[:, at + cols : at + wide] = nothing
            weights[at : at + cols] = w_ref[me ^ k, h]
            weights[at + cols : at + wide] = below
    out_ref[...] = base_ref[...] + dot(stack[...], weights[...])


def frames_back(me, base, pieces, weight, first):
    rows, width = base.shape
    count, cols = pieces[0].shape[0], weight.shape[2]
    deep = 4 * count * 2 * LANES
    grid_spec = pltpu.PrefetchScalarGridSpec(
        num_scalar_prefetch=1,
        grid=(1,),
        in_specs=[whole((rows, width))]
        + [
            pl.BlockSpec((count, 1, rows, cols), lambda i, t: (0, 0, 0, 0))
            if p.ndim == 4
            else whole(p.shape)
            for p in pieces
        ]
        + [
            pl.BlockSpec(
                (4, count, cols, width),
                lambda i, t: (0, first // count, 0, 0),
                pipeline_mode=pl.Buffered(1),
            )
        ],
        out_specs=whole((rows, width)),
        scratch_shapes=[pltpu.VMEM((rows, deep), BRAIN), pltpu.VMEM((deep, width), BRAIN)],
    )
    return pl.pallas_call(
        functools.partial(frames_kernel, count),
        grid_spec=grid_spec,
        out_shape=jax.ShapeDtypeStruct((rows, width), FLOAT),
        compiler_params=pltpu.CompilerParams(vmem_limit_bytes=VMEM_BYTES),
        cost_estimate=pl.CostEstimate(
            flops=8 * count * rows * cols * width, bytes_accessed=8 << 20, transcendentals=0
        ),
        name="frames_back",
    )(me, base, *pieces, weight)


def merge_kernel(count, joined, mine_ref, *refs):
    ins, outs = refs[: 4 * count], refs[4 * count :]
    at = 0
    for n in range(count):
        for which in range(2):
            value = ins[4 * n + which][...].astype(FLOAT) + ins[4 * n + 2 + which][...].astype(FLOAT)
            value = value.astype(BRAIN).reshape(
                [d for i, d in enumerate(ins[4 * n].shape) if i != 1]
            )
            if joined:
                outs[which][:, :, :, at : at + value.shape[-1]] = value
            else:
                outs[2 * n + which][...] = value
        at += ins[4 * n].shape[-1]


def merge(mine, parts, places, steps, joined=False):
    ins, in_specs, outs, out_specs = [], [], [], []
    for (keep, come, outer, inner), place in zip(parts, places):
        rows, columns = keep.shape[-2:]
        size = outer * inner // steps
        if inner >= size:
            block, per = (1, size), inner // size
        else:
            block, per = (size // inner, inner), 1

        def index(which, g, m, place=place, per=per):
            return (g // per, m[place] if which == 0 else 1 - m[place], g % per, 0, 0)

        for array in (keep, come):
            for which in range(2):
                ins.append(array.reshape(outer, 2, inner, rows, columns))
                in_specs.append(
                    pl.BlockSpec(
                        (block[0], 1, block[1], rows, columns), functools.partial(index, which)
                    )
                )
        for which in range(2):
            outs.append(jax.ShapeDtypeStruct((outer, inner, rows, columns), BRAIN))
            out_specs.append(
                pl.BlockSpec(
                    block + (rows, columns), lambda g, m, per=per: (g // per, g % per, 0, 0)
                )
            )
    if joined:
        whole_columns = sum(o.shape[-1] for o in outs) // 2
        shape = outs[0].shape[:-1] + (whole_columns,)
        outs = [jax.ShapeDtypeStruct(shape, BRAIN)] * 2
        spec = pl.BlockSpec(
            out_specs[0].block_shape[:-1] + (whole_columns,), out_specs[0].index_map
        )
        out_specs = [spec] * 2
    res = pl.pallas_call(
        functools.partial(merge_kernel, len(parts), joined),
        grid_spec=pltpu.PrefetchScalarGridSpec(
            num_scalar_prefetch=1, grid=(steps,), in_specs=in_specs, out_specs=out_specs
        ),
        out_shape=outs,
        compiler_params=pltpu.CompilerParams(vmem_limit_bytes=VMEM_BYTES),
        cost_estimate=pl.CostEstimate(flops=1 << 22, bytes_accessed=8 << 20, transcendentals=0),
        name="merge",
    )(mine, *ins)
    flat = [r.reshape((-1,) + r.shape[2:]) for r in res]
    return [(flat[2 * n], flat[2 * n + 1]) for n in range(len(flat) // 2)]


def fence(*values):
    return lax.optimization_barrier(values)


def tie(first, second):
    return fence(first, second)[0]


def body(
    frames,
    segment_ids,
    project_weight,
    query_value_bias,
    output_weight,
    output_bias,
    first_gain,
    first_shift,
    expand_weight,
    expand_bias,
    reduce_weight,
    reduce_bias,
    second_gain,
    second_shift,
    cotangent,
    *,
    groups,
):
    rows, width = frames.shape
    cols = project_weight.shape[2]
    hidden = expand_weight.shape[1]
    heads = cols // HEAD_DIM
    length = 4 * rows
    me = lax.axis_index("tensor")
    scalar = jnp.full((1,), me, jnp.int32)
    half = lax.axis_index("dp") % 2
    half_two = (lax.axis_index("dp") // 2) % 2
    other = functools.partial(swap, axis="tensor", size=4)

    far = other(frames, bits=2)
    near = other(frames, bits=1)

    blocks = segment_ids.reshape(4, rows)
    segs = jnp.concatenate([lax.dynamic_index_in_dim(blocks, me ^ k, 0) for k in range(4)], axis=1)
    ids = jnp.arange(IDS, dtype=jnp.int32)
    same = segs.reshape(1, length) == ids[:, None]
    qtail = jnp.pad(same.astype(BRAIN), ((0, HEAD_DIM - IDS), (0, 0)))
    differ = segs.reshape(length, 1) != ids[None, :]
    ktail = jnp.concatenate(
        [
            jnp.where(differ, -BIG, 0.0),
            jnp.full((length, 3), -1.0, FLOAT),
            jnp.zeros((length, LANES - IDS - 3), FLOAT),
        ],
        axis=1,
    )
    vectors = jnp.stack(
        [output_bias, first_gain, first_shift, reduce_bias, second_gain, second_shift]
    ).astype(FLOAT)
    vectors = jnp.pad(vectors, ((0, 2), (0, 0)))
    by_head = project_weight.reshape(3, width, heads, HEAD_DIM)
    turned = jnp.transpose(by_head[::-1], (2, 0, 3, 1)).reshape(heads, 3 * HEAD_DIM, width)
    upper = jnp.pad(by_head[:2], ((0, 0), (0, 0), (0, 0), (HEAD_DIM, 0)))
    lower = jnp.pad(by_head[2:], ((0, 0), (0, 0), (0, 0), (0, HEAD_DIM)))
    spread_weight = jnp.concatenate([upper, lower]).reshape(3, width, heads * LANES)
    bias = query_value_bias.astype(FLOAT).reshape(2, heads, HEAD_DIM)
    bias = jnp.stack(
        [
            jnp.pad(bias[0], ((0, 0), (HEAD_DIM, 0))).reshape(-1),
            jnp.pad(bias[1], ((0, 0), (0, HEAD_DIM))).reshape(-1),
        ]
    )
    wide_halves = jnp.concatenate(
        [
            expand_weight.T.reshape(2, hidden // 2, width),
            output_weight.reshape(2, cols // 2, width),
            jnp.broadcast_to(
                jnp.pad(expand_bias[None], ((0, 15), (0, width - hidden))), (2, 16, width)
            ),
        ],
        axis=1,
    )
    wide = wide_halves.reshape(-1, width)
    wide_half = lax.dynamic_index_in_dim(wide_halves, half, 0, False)
    back_half = lax.dynamic_index_in_dim(
        reduce_weight.reshape(2, hidden // 2, width), half_two, 0, False
    )
    near_wide = other(wide, bits=1)
    near_back = other(reduce_weight, bits=1)
    started = project(0, (frames, near), spread_weight, bias, ktail, qtail, ())

    far, started, turned, wide_half, back_half, near_wide, near_back = fence(
        far, started, turned, wide_half, back_half, near_wide, near_back
    )
    last = other(far, bits=1)

    got_wide = other(wide_half, bits=2)
    qt, ka, vt, qz, kt, va, xt = project(
        2, (far, last), spread_weight, bias, ktail, qtail, started
    )
    far_blocks = attend(qt, ka, vt, rows, 2, 2, False)
    far_blocks, got_wide, back_half, qt_later = fence(far_blocks, got_wide, back_half, qt)
    got_back = other(back_half, bits=2)
    relayed = swap(got_wide, "dp", groups, 1)
    far_mixed = other(far_blocks[0][0], bits=2)
    near_blocks = attend(qt_later, ka, vt, rows, 0, 2, True)
    near_blocks, got_back, relayed, far_mixed = fence(near_blocks, got_back, relayed, far_mixed)
    relayed_back = swap(got_back, "dp", groups, 2)
    near_mixed = other(near_blocks[0][1], bits=1)
    last_wide = other(jnp.concatenate([got_wide, relayed]), bits=1)
    last_mixed = other(far_mixed[1:], bits=1)
    last_back = other(jnp.concatenate([got_back, relayed_back]), bits=1)
    mixed = [near_blocks[0][0], near_mixed, far_mixed, last_mixed]
    wt = lax.all_gather(tie(turned, last_back), "tensor")

    outs = layer(
        jnp.stack([half, half_two]).astype(jnp.int32),
        mixed,
        frames,
        cotangent,
        vectors,
        (wide, near_wide, got_wide, relayed, last_wide),
        (reduce_weight, near_back, got_back, relayed_back, last_back),
    )
    outs, wt = fence(outs, wt)
    layer_out, grad_first = outs[:2]
    own_grad, near_grad, far_grad, small = outs[2:6]
    keeps, sends = outs[6:9], outs[9:12]
    far_grad = other(far_grad, bits=2)
    near_grad = other(near_grad, bits=1)

    everyone = lax.all_gather(small, ("dp", "tensor")).reshape(groups, 4, 16, width)

    bits = [2**n for n in reversed(range(groups.bit_length() - 1))]
    share = width // groups
    steps = [0] + bits[::-1]
    orders = [steps[n:3] + steps[:n] for n in range(3)]
    arrived = [other(send, bits=1) for send in sends]
    forms = (qt, ka, qz, kt, va, xt)
    exacts = [near_blocks[1], far_blocks[1]]
    logs = [near_blocks[2], far_blocks[2]]
    begun, query = attend_back_own(forms, own_grad, exacts[0], logs[0])
    arrived, begun, far_grad, near_grad = fence(arrived, begun, far_grad, near_grad)
    grad_heads = [near_grad, far_grad, other(far_grad[1:], bits=1)]
    mine = jnp.stack([jnp.zeros_like(half)] + [(lax.axis_index("dp") // b) % 2 for b in bits])
    mine = mine.astype(jnp.int32)
    axes = [0] + bits
    left = [list(axes) for _ in orders]
    values = [
        (keep.reshape(2 * groups, share, -1), come.reshape(2 * groups, share, -1))
        for keep, come in zip(keeps, arrived)
    ]

    def divide(values, chosen, steps, joined=False):
        parts = []
        for n, ((keep, come), axis) in enumerate(zip(values, chosen)):
            at = left[n].index(axis)
            parts.append((keep, come, 2**at, 2 ** (len(left[n]) - at - 1)))
            left[n] = [b for b in left[n] if b != axis]
        return merge(mine, parts, [axes.index(axis) for axis in chosen], steps, joined)

    def go(value, axis):
        return other(value, bits=2) if axis == 0 else swap(value, "dp", groups, axis)

    def sent_half(value, axis):
        count, lead = value.shape[:2]
        at = tail_left.index(axis)
        view = value.reshape((count, 2**at, 2, lead // 2 ** (at + 1)) + value.shape[2:])
        bit = (lax.axis_index("dp") // axis) % 2
        shape = (count, lead // 2) + value.shape[2:]
        keep_ = lax.dynamic_index_in_dim(view, bit, 2, keepdims=False).reshape(shape)
        send = lax.dynamic_index_in_dim(view, 1 - bit, 2, keepdims=False).reshape(shape)
        return keep_, swap(send, "dp", groups, axis)

    def added(pair):
        return (pair[0].astype(FLOAT) + pair[1].astype(FLOAT)).astype(BRAIN)

    def phase(values, number, steps):
        order = [o[number] for o in orders]
        halves = divide(values, order, steps)
        return [(half_[0], go(half_[1], axis)) for half_, axis in zip(halves, order)]

    def keeps_of(values):
        return [value[0] for value in values]

    tail_left = list(bits)
    values = phase(values, 0, 4)
    begun = tie(begun, keeps_of(values))
    head_args = (share, forms, grad_heads, exacts, logs)
    most = attend_back(0, heads - 1, *head_args, begun, query)
    most, values = fence(most, values)

    values = phase(values, 1, 2)
    far_most = other(most[2], bits=2)
    early = sent_half(most[3], 1)
    begun = tie(begun, (keeps_of(values), early[0]))
    final = attend_back(heads - 1, 1, *head_args, begun, query)
    final, values, far_most, early = fence(final, values, far_most, early)

    values = phase(values, 2, 1)
    late = sent_half(final[3], 1)
    far_final = other(final[2], bits=2)
    tail_left.remove(1)
    near_most = other(most[1], bits=1)
    last_most = other(far_most[:, 1], bits=1)
    frames_grad = frames_back(
        scalar, grad_first, (most[0], near_most, far_most, last_most), wt, 0
    )
    tail = jnp.concatenate([added(early), added(late)])
    for axis in bits[::-1][1:-1]:
        pair = sent_half(tail, axis)
        tail_left.remove(axis)
        if axis != bits[1]:
            tail = added(pair)
    frames_grad, values, pair, far_final = fence(frames_grad, values, pair, far_final)
    near_final = other(final[1], bits=1)
    last_final = other(far_final[:, 1], bits=1)
    rest = steps[3:]
    while len(rest) > 1:
        values = [
            (half_[0], go(half_[1], rest[0])) for half_ in divide(values, [rest[0]] * 3, 1)
        ]
        rest = rest[1:]
    ((kept, sent),) = divide(values, [rest[0]] * 3, 1, True)
    tail_keep, tail_come = sent_half(added(pair), rest[0])
    come = go(sent, rest[0])
    frames_grad = frames_back(
        scalar, frames_grad, (final[0], near_final, far_final, last_final), wt, heads - 1
    )
    tail = tail_keep[:, 0].astype(FLOAT) + tail_come[:, 0].astype(FLOAT)
    joined = (kept.astype(FLOAT) + come.astype(FLOAT))[0]

    vector_grads = jnp.sum(everyone[:, :, :6], axis=(0, 1))
    picked = [lax.dynamic_index_in_dim(everyone[:, s], 8 + (me ^ s), 1, False) for s in range(4)]
    expand_bias_grad = sum(jnp.sum(p, axis=0) for p in picked)

    arrays = [[], [], []]
    at = 0
    for portion in portions(width, hidden):
        for array, _, count in portion.spans:
            arrays[array].append(joined[:, at : at + count])
            at += count
    expand_grad, reduce_grad, output_grad = [jnp.concatenate(a, axis=1) for a in arrays]
    reduce_grad = reduce_grad.T
    output_grad = output_grad[:, :cols].T

    project_grad = jnp.stack(
        [
            jnp.swapaxes(tail[:, :, (2 - i) * HEAD_DIM : (3 - i) * HEAD_DIM], 0, 1).reshape(
                share, cols
            )
            for i in range(3)
        ]
    )
    spread = 3 * HEAD_DIM // share
    bias_sums = jnp.swapaxes(tail[:, :, 3 * HEAD_DIM : 3 * HEAD_DIM + spread], 1, 2)
    bias_sums = bias_sums.reshape(heads, 3, HEAD_DIM)
    attend_bias_grad = jnp.stack([bias_sums[:, i].reshape(cols) for i in (2, 0)])
    return (
        layer_out,
        frames_grad,
        project_grad,
        attend_bias_grad,
        output_grad,
        expand_grad,
        expand_bias_grad,
        reduce_grad,
        vector_grads,
    )


def solution(mesh):
    placed = (
        P(("dp", "tensor"), None),
        P("dp", None),
        P(None, None, "tensor"),
        P(None, "tensor"),
        P("tensor", None),
        P(),
        P(),
        P(),
        P(None, "tensor"),
        P("tensor"),
        P("tensor", None),
        P(),
        P(),
        P(),
        P(("dp", "tensor"), None),
    )
    return jax.shard_map(
        functools.partial(body, groups=mesh.shape["dp"]),
        mesh=mesh,
        in_specs=placed,
        out_specs=(
            P(("dp", "tensor"), None),
            P(("dp", "tensor"), None),
            P(None, "dp", "tensor"),
            P(None, "tensor"),
            P("tensor", "dp"),
            P("dp", "tensor"),
            P("tensor"),
            P("tensor", "dp"),
            P(),
        ),
        check_vma=False,
    )
```

```python
import functools

import jax
import jax.numpy as jnp
import numpy as np
from jax import lax
from jax.experimental import pallas as pl
from jax.experimental.pallas import tpu as pltpu
from jax.sharding import PartitionSpec as P

HEAD_DIM = 64
ROW_LEN = 2048
EPS = 1e-05
FLOAT = jnp.float32
BRAIN = jnp.bfloat16
BIG = 1e30
SCALE = HEAD_DIM ** (-0.5)
VMEM_BYTES = 60 << 20
IDS = 8
LANES = 128
CHUNK = 1024
BACK_CHUNK = 512
SLOTS = 64

NN = (((1,), (0,)), ((), ()))
NT = (((1,), (1,)), ((), ()))


def dot(left, right, dims=NN):
    return lax.dot_general(left, right, dims, preferred_element_type=FLOAT)


def swap(value, axis, size, bits):
    return lax.ppermute(value, axis, [(i, i ^ bits) for i in range(size)])


def whole(shape):
    return pl.BlockSpec(shape, lambda *_: (0,) * len(shape), pipeline_mode=pl.Buffered(1))


def split_three(value):
    top = value.astype(BRAIN).astype(FLOAT)
    rest = value - top
    middle = rest.astype(BRAIN).astype(FLOAT)
    return top, middle, rest - middle


def project_kernel(heads, rows, first, *refs):
    x_refs = refs[:2]
    w_ref, bias_ref, segs_ref = refs[2:5]
    if first:
        held = refs[-1]
        spread = refs[-2]
        forms = refs[-9:-2]
    else:
        held = refs[-1]
        spread = w_ref
        forms = refs[-8:-1]
    qt_ref, ka_ref, vt_ref, qz_ref, kt_ref, va_ref, xt_ref = forms
    step = pl.program_id(0)
    for k in range(2):

        @pl.when(step == k)
        def _():
            held[...] = x_refs[k][...]

    if first:

        @pl.when(step == 0)
        def _():
            nothing = jnp.zeros((w_ref.shape[1], HEAD_DIM), BRAIN)
            for i in range(3):
                for h in range(heads):
                    own = w_ref[i, :, h * HEAD_DIM : (h + 1) * HEAD_DIM]
                    pair = [own, nothing] if i == 2 else [nothing, own]
                    spread[i, :, h * LANES : (h + 1) * LANES] = jnp.concatenate(pair, axis=1)

    x = held[...]
    xt_ref[...] = x.T
    segs = segs_ref[...].astype(FLOAT)
    number = lax.broadcasted_iota(jnp.int32, (HEAD_DIM, rows), 0).astype(FLOAT)
    qtail = jnp.where(jnp.broadcast_to(segs, (HEAD_DIM, rows)) == number, 1.0, 0.0).astype(BRAIN)
    lane = lax.broadcasted_iota(jnp.int32, (rows, LANES), 1)
    differ = jnp.broadcast_to(segs, (LANES, rows)).T != lane.astype(FLOAT)
    ktail = jnp.where(lane < IDS, jnp.where(differ, -BIG, 0.0), jnp.where(lane < IDS + 3, -1.0, 0.0))
    minus = jnp.where((lane >= HEAD_DIM) & (lane < HEAD_DIM + 3), -1.0, 0.0)
    query = (dot(x, spread[0]) + bias_ref[0:1]).astype(BRAIN).astype(FLOAT) * SCALE
    key = dot(x, spread[1])
    value = dot(x, spread[2]) + bias_ref[1:2]
    for h in range(heads):
        own = slice(h * LANES, (h + 1) * LANES)
        q, k_, v = query[:, own], key[:, own], value[:, own]
        qt_ref[h, :HEAD_DIM, :] = qtail
        qt_ref[h, HEAD_DIM:, :] = q.T[HEAD_DIM:].astype(BRAIN)
        kt_ref[h] = k_.T.astype(BRAIN)
        vt_ref[h] = v.T[:HEAD_DIM].astype(BRAIN)
        ka_ref[h] = (k_ + ktail).astype(BRAIN)
        va_ref[h] = (v + minus).astype(BRAIN)
        qz_ref[h, :HEAD_DIM, :] = jnp.zeros((HEAD_DIM, rows), BRAIN)
        qz_ref[h, HEAD_DIM:, :] = qt_ref[h, HEAD_DIM:, :]


def project(first, pieces, weight, bias, segs, before):
    rows, width = pieces[0].shape
    heads = bias.shape[1] // LANES
    length = 4 * rows
    by_lane = lambda i: (0, 0, first + i)
    by_row = lambda i: (0, first + i, 0)
    shapes = [
        ((heads, LANES, length), (heads, LANES, rows), by_lane),
        ((heads, length, LANES), (heads, rows, LANES), by_row),
        ((heads, HEAD_DIM, length), (heads, HEAD_DIM, rows), by_lane),
        ((heads, LANES, length), (heads, LANES, rows), by_lane),
        ((heads, LANES, length), (heads, LANES, rows), by_lane),
        ((heads, length, LANES), (heads, rows, LANES), by_row),
        ((width, length), (width, rows), lambda i: (0, first + i)),
    ]
    out_specs = [pl.BlockSpec(block, index) for _, block, index in shapes]
    if not before:
        shapes.append(((3, width, heads * LANES), None, None))
        out_specs.append(whole(shapes[-1][0]))
    return pl.pallas_call(
        functools.partial(project_kernel, heads, rows, not before),
        grid=(2,),
        in_specs=[
            whole((rows, width)),
            whole((rows, width)),
            whole(weight.shape),
            whole(bias.shape),
            pl.BlockSpec((1, rows), lambda i: (0, first + i)),
        ]
        + [pl.BlockSpec(memory_space=pl.ANY)] * len(before),
        out_specs=out_specs,
        out_shape=[jax.ShapeDtypeStruct(s[0], BRAIN) for s in shapes],
        scratch_shapes=[pltpu.VMEM((rows, width), BRAIN)],
        input_output_aliases={5 + n: n for n in range(len(before))},
        compiler_params=pltpu.CompilerParams(vmem_limit_bytes=VMEM_BYTES),
        cost_estimate=pl.CostEstimate(
            flops=12 * rows * width * heads * LANES, bytes_accessed=8 << 20, transcendentals=0
        ),
        name="project",
    )(*pieces, weight, bias, segs, *before)


def attend_kernel(rows, count, *refs):
    qt_ref, ka_ref, vt_ref = refs[:3]
    out_refs, exact_ref, log_ref, held = refs[3:-3], refs[-3], refs[-2], refs[-1]
    length = ka_ref.shape[1]
    part, chunk = held.shape[2], min(CHUNK, length)
    chunks = [slice(at, at + chunk) for at in range(0, length, chunk)]
    items = [(n, at) for n in range(count) for at in range(0, rows, part)]

    def score(item, keys):
        n, at = items[item]
        first = n * rows + at
        scores = dot(ka_ref[0, keys], qt_ref[0, :, first : first + part])
        held[item % 2, keys] = scores
        return jnp.max(scores, axis=0, keepdims=True)

    highest = functools.reduce(jnp.maximum, [score(0, keys) for keys in chunks])
    for item, (n, at) in enumerate(items):
        tops, total, mixed = [], 0.0, 0.0
        for keys in chunks:
            if item + 1 < len(items):
                tops.append(score(item + 1, keys))
            raised = jnp.exp(held[item % 2, keys] - highest)
            total = total + jnp.sum(raised, axis=0, keepdims=True)
            mixed = mixed + dot(vt_ref[0, :, keys], raised.astype(BRAIN))
        mixed = mixed / total
        lanes = slice(at, at + part)
        if len(out_refs) == 1:
            out_refs[0][n, :, lanes] = mixed.astype(BRAIN)
        else:
            out_refs[n][0, :, lanes] = mixed.astype(BRAIN)
        exact_ref[n, :, lanes] = mixed
        log_ref[0, n : n + 1, lanes] = highest + jnp.log(total)
        if tops:
            highest = functools.reduce(jnp.maximum, tops)


def attend(qt, ka, vt, rows, first, count, parted):
    heads, _, length = qt.shape
    cols = heads * HEAD_DIM
    by_head = lambda h: (0, h, 0)
    sizes = [1] * count if parted else [count]
    outs = pl.pallas_call(
        functools.partial(attend_kernel, rows, count),
        grid=(heads,),
        in_specs=[
            pl.BlockSpec((1, LANES, count * rows), lambda h: (h, 0, first // count)),
            pl.BlockSpec((1, length, LANES), lambda h: (h, 0, 0)),
            pl.BlockSpec((1, HEAD_DIM, length), lambda h: (h, 0, 0)),
        ],
        out_specs=[pl.BlockSpec((n, HEAD_DIM, rows), by_head) for n in sizes]
        + [
            pl.BlockSpec((count, HEAD_DIM, rows), by_head),
            pl.BlockSpec((1, count, rows), lambda h: (h, 0, 0)),
        ],
        out_shape=[jax.ShapeDtypeStruct((n, cols, rows), BRAIN) for n in sizes]
        + [
            jax.ShapeDtypeStruct((count, cols, rows), FLOAT),
            jax.ShapeDtypeStruct((heads, count, rows), FLOAT),
        ],
        scratch_shapes=[pltpu.VMEM((2, length, rows // 2), FLOAT)],
        compiler_params=pltpu.CompilerParams(vmem_limit_bytes=VMEM_BYTES),
        cost_estimate=pl.CostEstimate(
            flops=8 * heads * length * count * rows * LANES,
            bytes_accessed=8 << 20,
            transcendentals=heads * length * count * rows,
        ),
        name="attend",
    )(qt, ka, vt)
    return outs[:-2], outs[-2], outs[-1]


def fill(slot, queries, grads, plain, qt, grad, exact, log):
    rows = queries.shape[2]
    low = lax.broadcasted_iota(jnp.int32, (8, rows), 0)

    def stacked(value):
        top, middle, bottom = split_three(value)
        return jnp.where(
            low == 0, top, jnp.where(low == 1, middle, jnp.where(low == 2, bottom, 0.0))
        )

    nothing = jnp.zeros((LANES - HEAD_DIM - 16, rows), BRAIN)
    delta = jnp.sum(grad.astype(FLOAT) * exact, axis=0, keepdims=True)
    ids = qt[:16].astype(FLOAT)[:IDS]
    queries[slot, :16] = jnp.concatenate([ids, stacked(log)], axis=0).astype(BRAIN)
    queries[slot, 16:] = qt[16:]
    grads[slot, :HEAD_DIM] = grad
    grads[slot, HEAD_DIM : HEAD_DIM + 16] = jnp.concatenate(
        [stacked(delta), jnp.zeros((8, rows), FLOAT)], axis=0
    ).astype(BRAIN)
    grads[slot, HEAD_DIM + 16 :] = nothing
    plain[slot, :HEAD_DIM] = grad
    plain[slot, HEAD_DIM:] = jnp.zeros((LANES - HEAD_DIM, rows), BRAIN)


def back_block(slot, queries, grads, plain, qz, ka_ref, kt_ref, va_ref, add):
    length = ka_ref.shape[1]
    chunk = min(BACK_CHUNK, length)
    grad_query = 0.0
    for at in range(0, length, chunk):
        keys = slice(at, at + chunk)
        probs = jnp.exp(dot(ka_ref[0, keys], queries[slot]))
        grad_scores = (probs * dot(va_ref[0, keys], grads[slot])).astype(BRAIN)
        add(keys, dot(probs.astype(BRAIN), plain[slot], NT) + dot(grad_scores, qz, NT))
        grad_query = grad_query + dot(kt_ref[0, :, keys], grad_scores)
    return (grad_query * SCALE).T.astype(BRAIN)


def attend_back_own_kernel(*refs):
    qt_ref, ka_ref, qz_ref, kt_ref, va_ref = refs[:5]
    grad_ref, exact_ref, log_ref = refs[5:8]
    total_ref, query_ref = refs[8:10]
    scratch = refs[10:]
    fill(0, *scratch, qt_ref[0], grad_ref[0], exact_ref[0], log_ref[0, 0:1])

    def add(keys, value):
        total_ref[0, keys] = value

    query_ref[0] = back_block(0, *scratch, qz_ref[0], ka_ref, kt_ref, va_ref, add)


def attend_back_own(forms, grad, exact, log):
    qt, ka, qz, kt, va, _ = forms
    heads, length = ka.shape[:2]
    rows = length // 4
    by_head = lambda h: (h, 0, 0)
    return pl.pallas_call(
        attend_back_own_kernel,
        grid=(heads,),
        in_specs=[
            pl.BlockSpec((1, LANES, rows), by_head),
            pl.BlockSpec((1, length, LANES), by_head),
            pl.BlockSpec((1, LANES, rows), by_head),
            pl.BlockSpec((1, LANES, length), by_head),
            pl.BlockSpec((1, length, LANES), by_head),
            pl.BlockSpec((1, HEAD_DIM, rows), lambda h: (0, h, 0)),
            pl.BlockSpec((1, HEAD_DIM, rows), lambda h: (0, h, 0)),
            pl.BlockSpec((1, 2, rows), by_head),
        ],
        out_specs=[
            pl.BlockSpec((1, length, LANES), by_head),
            pl.BlockSpec((1, rows, LANES), by_head),
        ],
        out_shape=[
            jax.ShapeDtypeStruct((heads, length, LANES), FLOAT),
            jax.ShapeDtypeStruct((heads, rows, LANES), BRAIN),
        ],
        scratch_shapes=[pltpu.VMEM((1, LANES, rows), BRAIN)] * 3,
        compiler_params=pltpu.CompilerParams(vmem_limit_bytes=VMEM_BYTES),
        cost_estimate=pl.CostEstimate(
            flops=18 * length * length * LANES,
            bytes_accessed=8 << 20,
            transcendentals=length * length,
        ),
        name="attend_back_own",
    )(qt, ka, qz, kt, va, grad, exact, log)


def attend_back_kernel(rows, first, share, *refs):
    qt_ref, ka_ref, qz_ref, kt_ref, va_ref, xt_ref = refs[:6]
    grad_refs, exacts, logs = refs[6:9], refs[9:12], refs[12:14]
    begun_ref, query_ref = refs[14:16]
    out_ref, project_ref = refs[16:18]
    total, begun, xt = refs[18:21]
    scratch = refs[21:24]
    sem = refs[24]
    step = pl.program_id(0)
    begun_copy = pltpu.make_async_copy(begun_ref.at[first + step], begun, sem.at[0])
    xt_copy = pltpu.make_async_copy(xt_ref, xt, sem.at[1])
    begun_copy.start()
    pl.when(step == 0)(xt_copy.start)
    for k in range(3):
        at = pl.ds((k + 1) * rows, rows)
        log = logs[(k + 1) // 2][0, (k + 1) % 2 : (k + 1) % 2 + 1]
        fill(k, *scratch, qt_ref[0, :, at], grad_refs[k][0], exacts[k][0], log)
    out_ref[0, :rows, LANES:] = query_ref[0]
    for k in range(3):

        def add(keys, value):
            if k == 0:
                total[keys] = value
            else:
                total[keys] += value

        at = pl.ds((k + 1) * rows, rows)
        qz = qz_ref[0, :, at]
        out_ref[0, at, LANES:] = back_block(k, *scratch, qz, ka_ref, kt_ref, va_ref, add)
    begun_copy.wait()
    pl.when(step == 0)(xt_copy.wait)
    out_ref[0, :, :LANES] = (total[...] + begun[...]).astype(BRAIN)
    pieces = out_ref[0]
    project_ref[0] = dot(xt[...], pieces).astype(BRAIN)
    bias = jnp.sum(pieces.astype(FLOAT), axis=0, keepdims=True)
    if share % 16 == 0:
        bias = jnp.concatenate([bias[:, :LANES], bias[:, LANES + HEAD_DIM :]], axis=1)
        spread = 3 * HEAD_DIM // share
        line = jnp.concatenate(
            [bias[:, n * share : (n + 1) * share] for n in range(spread)]
            + [jnp.zeros((8 - spread, share), FLOAT)],
            axis=0,
        ).T.astype(BRAIN)
        for at in range(0, project_ref.shape[1], share):
            project_ref[0, at : at + share, LANES : LANES + 8] = line
    else:
        refs[25][0] = bias


def attend_back(first, count, share, forms, grads, exacts, logs, begun, query):
    qt, ka, qz, kt, va, xt = forms
    length, width = ka.shape[1], xt.shape[0]
    rows = length // 4
    cols = 2 * LANES
    own = lambda i: (first + i, 0, 0)
    by_block = lambda n: pl.BlockSpec((1, HEAD_DIM, rows), lambda i: (n, first + i, 0))
    each = lambda i: (i, 0, 0)
    out_specs = [pl.BlockSpec((1, length, cols), each), pl.BlockSpec((1, width, cols), each)]
    out_shape = [
        jax.ShapeDtypeStruct((count, length, cols), BRAIN),
        jax.ShapeDtypeStruct((count, width, cols), BRAIN),
    ]
    scratch = (
        [
            pltpu.VMEM((length, LANES), FLOAT),
            pltpu.VMEM((length, LANES), FLOAT),
            pltpu.VMEM((width, length), BRAIN),
        ]
        + [pltpu.VMEM((3, LANES, rows), BRAIN)] * 3
        + [pltpu.SemaphoreType.DMA((2,))]
    )
    kernel = functools.partial(attend_back_kernel, rows, first, share)
    if share % 16:
        out_specs.append(pl.BlockSpec((1, 1, cols), each))
        out_shape.append(jax.ShapeDtypeStruct((count, 1, cols), FLOAT))
        kernel = lambda *refs: attend_back_kernel(
            rows, first, share, *refs[:18], *refs[19:], refs[18]
        )
    res = pl.pallas_call(
        kernel,
        grid=(count,),
        in_specs=[
            pl.BlockSpec((1, LANES, length), own),
            pl.BlockSpec((1, length, LANES), own),
            pl.BlockSpec((1, LANES, length), own),
            pl.BlockSpec((1, LANES, length), own),
            pl.BlockSpec((1, length, LANES), own),
            pl.BlockSpec(memory_space=pl.ANY),
        ]
        + [by_block(0)] * 3
        + [by_block(1), by_block(0), by_block(1)]
        + [pl.BlockSpec((1, 2, rows), own)] * 2
        + [pl.BlockSpec(memory_space=pl.ANY), pl.BlockSpec((1, rows, LANES), own)],
        out_specs=out_specs,
        out_shape=out_shape,
        scratch_shapes=scratch,
        compiler_params=pltpu.CompilerParams(vmem_limit_bytes=VMEM_BYTES),
        cost_estimate=pl.CostEstimate(
            flops=20 * count * length * length * LANES,
            bytes_accessed=8 << 20,
            transcendentals=count * length * length,
        ),
        name="attend_back",
    )(qt, ka, qz, kt, va, xt, *grads, exacts[0], exacts[1], exacts[1], *logs, begun, query)
    project_grad = res[1].reshape(count, width // share, share, cols)
    if share % 16:
        spread = 3 * HEAD_DIM // share
        bias = jnp.concatenate([res[2][..., :LANES], res[2][..., LANES + HEAD_DIM :]], axis=2)
        bias = jnp.swapaxes(bias.reshape(count, 1, spread, share), 2, 3).astype(BRAIN)
        bias = jnp.broadcast_to(bias, (count, width // share, share, spread))
        project_grad = jnp.concatenate(
            [
                project_grad[..., :LANES],
                bias,
                project_grad[..., LANES + spread :],
            ],
            axis=3,
        )
    return res[0], project_grad


def gelu_parts(values):
    t = 1.0 / (1.0 + (0.3275911 * 0.7071067811865476) * jnp.abs(values))
    bell = jnp.exp(-0.5 * values * values)
    poly = 0.5 * 1.061405429
    for c in (-1.453152027, 1.421413741, -0.284496736, 0.254829592):
        poly = poly * t + 0.5 * c
    tail = poly * t * bell
    below = jnp.where(values >= 0, 1.0 - tail, tail)
    return values * below, below + values * bell * 0.3989422804014327


def mean_of(values):
    return jnp.mean(values, axis=-1, keepdims=True)


class Portion:
    def __init__(self, *spans):
        self.spans = spans
        self.columns = sum(span[2] for span in spans)


def portions(width, hidden):
    if hidden == 6 * LANES:
        return (
            Portion((0, 0, 4 * LANES)),
            Portion((0, 4 * LANES, 2 * LANES), (1, 0, 3 * LANES)),
            Portion((1, 3 * LANES, 3 * LANES), (2, 0, 2 * LANES)),
        )
    return (Portion((0, 0, hidden)), Portion((1, 0, hidden)), Portion((2, 0, 2 * LANES)))


def layer_kernel(parts, hidden, riding, *refs):
    t_ref = refs[0]
    mixed = refs[1:5]
    x_ref, cot_ref, vec_ref = refs[5:8]
    wide_refs, back_refs = refs[8:14], refs[14:20]
    out_ref, grad_first_ref = refs[20:22]
    d_refs = (refs[22].at[0], refs[23].at[0], refs[24].at[0], refs[24].at[1])
    small_ref = refs[25]
    keeps, sends = refs[26:29], refs[29:32]
    wet, wo, eb, back, orow, act, slope, dz, stage, tail_stage = refs[32:42]
    wide_sem, back_sem, out_sem = refs[42:]
    half, back_half = t_ref[0], t_ref[1]
    width = x_ref.shape[1]
    part = mixed[0].shape[1]
    bias_out, gain_one, shift_one, bias_red, gain_two, shift_two = (
        vec_ref[i : i + 1] for i in range(6)
    )

    split = hidden // 2 + part // 2 + 16

    def load_wide(k, n):
        if k < 2:
            source, first, which = wide_refs[k], n * split, n
        else:
            source, first, which = wide_refs[2 * k - 2 + n], 0, (half, 1 - half)[n]
        found = []
        for m, (at, count, target, to) in enumerate(
            [
                (0, hidden // 2, wet, k * hidden + which * (hidden // 2)),
                (hidden // 2, part // 2, wo, k * part + which * (part // 2)),
                (hidden // 2 + part // 2, 16, eb.at[k], which * 16),
            ]
        ):
            to = to if isinstance(to, int) else pl.multiple_of(to, 16)
            found.append(
                pltpu.make_async_copy(
                    source.at[pl.ds(first + at, count)],
                    target.at[pl.ds(to, count)],
                    wide_sem.at[k, n, m],
                )
            )
        return found

    loads = [[load_wide(k, n) for n in range(2)] for k in range(4)]
    def load_back(k, n):
        if k < 2:
            source, first, which = back_refs[k], n * (hidden // 2), n
        else:
            source, first, which = back_refs[2 * k - 2 + n], 0, (back_half, 1 - back_half)[n]
        to = k * hidden + which * (hidden // 2)
        to = to if isinstance(to, int) else pl.multiple_of(to, 16)
        return pltpu.make_async_copy(
            source.at[pl.ds(first, hidden // 2)],
            back.at[pl.ds(to, hidden // 2)],
            back_sem.at[k, n],
        )

    back_loads = [load_back(k, n) for k in range(4) for n in range(2)]

    def each(kind, k=None):
        return [c[kind] for pair in (loads if k is None else [loads[k]]) for c in pair]

    for copy in each(1):
        copy.start()
    for k in range(4):
        for copy in each(0, k) + each(2, k):
            copy.start()
    for k, ref in enumerate(mixed):
        orow[:, k * part : (k + 1) * part] = ref[0].astype(FLOAT).T.astype(BRAIN)
    for copy in each(1):
        copy.wait()
    for copy in back_loads:
        copy.start()
    total = x_ref[...].astype(FLOAT) + bias_out + dot(orow[...], wo[...])
    center = total - mean_of(total)
    inverse_one = lax.rsqrt(mean_of(center * center) + EPS)
    unit_one = center * inverse_one
    normed = unit_one * gain_one + shift_one
    hb = normed.astype(BRAIN)
    hbt = normed.T.astype(BRAIN)

    owns = [slice(j * hidden, (j + 1) * hidden) for j in range(4)]
    for copy in each(0) + each(2):
        copy.wait()
    inner = dot(hb, wet[owns[0]], NT)
    for j in range(4):
        now = inner + eb[j, :16].astype(FLOAT)[:1]
        if j < 3:
            inner = dot(hb, wet[owns[j + 1]], NT)
        active, derivative = gelu_parts(now)
        act[:, owns[j]] = active.astype(BRAIN)
        slope[:, owns[j]] = derivative
    for copy in back_loads:
        copy.wait()
    total = normed + dot(act[...], back[...]) + bias_red
    center = total - mean_of(total)
    inverse = lax.rsqrt(mean_of(center * center) + EPS)
    unit = center * inverse
    out_ref[...] = (unit * gain_two + shift_two).astype(BRAIN)
    cot = cot_ref[...].astype(FLOAT)
    scaled = cot * gain_two
    grad = inverse * (scaled - mean_of(scaled) - unit * mean_of(scaled * unit))
    small_ref[3:4] = jnp.sum(grad, axis=0, keepdims=True)
    small_ref[4:5] = jnp.sum(cot * unit, axis=0, keepdims=True)
    small_ref[5:6] = jnp.sum(cot, axis=0, keepdims=True)
    dfb = grad.astype(BRAIN)
    dfbt = grad.T.astype(BRAIN)

    def outgoing(block, array, first_sem):
        found = []
        for ref, portion in zip(keeps if block in (0, 2) else sends, parts):
            at = 0
            for held, first, count in portion.spans:
                if held == array:
                    source = tail_stage.at[block] if array == 2 else stage.at[block, array]
                    found.append(
                        pltpu.make_async_copy(
                            source.at[:, pl.ds(first, count)],
                            ref.at[block // 2, :, pl.ds(at, count)],
                            out_sem.at[block, first_sem + len(found)],
                        )
                    )
                at += count
        return found

    order = (1, 3, 0, 2)
    started = []
    for j in order:
        stage[j, 1] = dot(dfbt, act[:, owns[j]]).astype(BRAIN)
        copies = outgoing(j, 1, 2)
        for copy in copies:
            copy.start()
        started += copies
    grad_active = dot(dfb, back[owns[order[0]]], NT)
    for n, j in enumerate(order):
        now = grad_active
        if n < 3:
            grad_active = dot(dfb, back[owns[order[n + 1]]], NT)
        grad_inner = (now * slope[:, owns[j]]).astype(BRAIN)
        dz[:, owns[j]] = grad_inner
        small_ref[8 + j : 9 + j] = jnp.sum(grad_inner.astype(FLOAT), axis=0, keepdims=True)
        stage[j, 0] = dot(hbt, grad_inner).astype(BRAIN)
        copies = outgoing(j, 0, 0)
        for copy in copies:
            copy.start()
        started += copies
    grad = grad + dot(dz[...], wet[...])
    small_ref[1:2] = jnp.sum(grad * unit_one, axis=0, keepdims=True)
    small_ref[2:3] = jnp.sum(grad, axis=0, keepdims=True)
    scaled = grad * gain_one
    first = inverse_one * (scaled - mean_of(scaled) - unit_one * mean_of(scaled * unit_one))
    small_ref[0:1] = jnp.sum(first, axis=0, keepdims=True)
    small_ref[6:8] = jnp.zeros((2, width), FLOAT)
    small_ref[12:] = jnp.zeros((4, width), FLOAT)
    grad_first_ref[...] = first
    grad_mixed = dot(wo[...], first.astype(BRAIN), NT).astype(BRAIN)
    for k, ref in enumerate(d_refs):
        ref[...] = grad_mixed[k * part : (k + 1) * part]
    output_grad = dot(first.T.astype(BRAIN), orow[...]).astype(BRAIN)
    places = SLOTS // 8
    share = width // places
    sums = small_ref[...]
    for k in range(4):
        tail_stage[k, :, :part] = output_grad[:, k * part : (k + 1) * part]
        if riding:
            rows_k = jnp.concatenate([sums[:6], sums[8 + k : 9 + k], sums[6:7]], axis=0)
            lines = jnp.concatenate(
                [rows_k[:, c * share : (c + 1) * share] for c in range(places)], axis=0
            ).T.astype(BRAIN)
            tail_stage[k, :, part:] = jnp.concatenate([lines] * places, axis=0)
        else:
            tail_stage[k, :, part:] = jnp.zeros((width, 2 * LANES - part), BRAIN)
        copies = outgoing(k, 2, 4)
        for copy in copies:
            copy.start()
        started += copies
    for copy in started:
        copy.wait()


def layer(halves, mixed, frames, cotangent, vectors, wides, backs, riding):
    rows, width = frames.shape
    part = mixed[0].shape[1]
    hidden = backs[0].shape[0]
    parts = portions(width, hidden)
    grads = [jax.ShapeDtypeStruct((2, width, p.columns), BRAIN) for p in parts]
    grid_spec = pltpu.PrefetchScalarGridSpec(
        num_scalar_prefetch=1,
        grid=(1,),
        in_specs=[whole((1, part, rows))] * 4
        + [whole((rows, width)), whole((rows, width)), whole(vectors.shape)]
        + [pl.BlockSpec(memory_space=pl.ANY)] * 12,
        out_specs=[whole((rows, width)), whole((rows, width))]
        + [whole((n, part, rows)) for n in (1, 1, 2)]
        + [whole((16, width))]
        + [pl.BlockSpec(memory_space=pl.ANY)] * 6,
        scratch_shapes=[
            pltpu.VMEM((4 * hidden, width), BRAIN),
            pltpu.VMEM((4 * part, width), BRAIN),
            pltpu.VMEM((4, 32, width), BRAIN),
            pltpu.VMEM((4 * hidden, width), BRAIN),
            pltpu.VMEM((rows, width), BRAIN),
            pltpu.VMEM((rows, 4 * hidden), BRAIN),
            pltpu.VMEM((rows, 4 * hidden), FLOAT),
            pltpu.VMEM((rows, 4 * hidden), BRAIN),
            pltpu.VMEM((4, 2, width, hidden), BRAIN),
            pltpu.VMEM((4, width, 2 * LANES), BRAIN),
            pltpu.SemaphoreType.DMA((4, 2, 3)),
            pltpu.SemaphoreType.DMA((4, 2)),
            pltpu.SemaphoreType.DMA((4, 6)),
        ],
    )
    return pl.pallas_call(
        functools.partial(layer_kernel, parts, hidden, riding),
        grid_spec=grid_spec,
        out_shape=[
            jax.ShapeDtypeStruct((rows, width), BRAIN),
            jax.ShapeDtypeStruct((rows, width), FLOAT),
        ]
        + [jax.ShapeDtypeStruct((n, part, rows), BRAIN) for n in (1, 1, 2)]
        + [jax.ShapeDtypeStruct((16, width), FLOAT)]
        + grads
        + grads,
        compiler_params=pltpu.CompilerParams(vmem_limit_bytes=VMEM_BYTES),
        cost_estimate=pl.CostEstimate(
            flops=2 * rows * width * (24 * hidden + 3 * width),
            bytes_accessed=40 << 20,
            transcendentals=8 * rows * hidden,
        ),
        name="layer",
    )(halves, *mixed, frames, cotangent, vectors, *wides, *backs)


def frames_kernel(based, most_ref, last_ref, w_ref, *refs):
    if based:
        base_ref, first_ref, second_ref, stack, weights = refs
    else:
        out_ref, stack, weights = refs
    step = pl.program_id(0)
    heads = w_ref.shape[2] // LANES
    wide = 2 * LANES

    @pl.when(step == 0)
    def _():
        for h in range(heads):
            own = slice(h * LANES, (h + 1) * LANES)
            at = h * wide
            weights[:, at : at + LANES] = w_ref[1, :, own] + w_ref[2, :, own]
            weights[:, at + LANES : at + wide] = w_ref[0, :, own]

    for h in range(heads - 1):
        stack[:, h * wide : (h + 1) * wide] = most_ref[h]
    stack[:, (heads - 1) * wide :] = last_ref[0]
    value = dot(stack[...], weights[...], NT)
    if based:

        @pl.when(step == 0)
        def _():
            first_ref[...] = base_ref[...] + value

        @pl.when(step == 1)
        def _():
            second_ref[...] = value
    else:
        out_ref[0] = value.astype(BRAIN)


def frames_back(most, last, weight, base=None):
    heads = most.shape[0] + 1
    width = weight.shape[1]
    rows = most.shape[1] // 4
    shift = 1 if base is None else 0
    cols = 2 * LANES
    ins = [most, last, weight]
    in_specs = [
        pl.BlockSpec((heads - 1, rows, cols), lambda i: (0, 2 * i + shift, 0)),
        pl.BlockSpec((1, rows, cols), lambda i: (0, 2 * i + shift, 0)),
        whole(weight.shape),
    ]
    if base is None:
        out_specs = pl.BlockSpec((1, rows, width), lambda i: (i, 0, 0))
        out_shape = jax.ShapeDtypeStruct((2, rows, width), BRAIN)
    else:
        ins.append(base)
        in_specs.append(whole((rows, width)))
        out_specs = [whole((rows, width))] * 2
        out_shape = [jax.ShapeDtypeStruct((rows, width), FLOAT)] * 2
    return pl.pallas_call(
        functools.partial(frames_kernel, base is not None),
        grid=(2,),
        in_specs=in_specs,
        out_specs=out_specs,
        out_shape=out_shape,
        scratch_shapes=[
            pltpu.VMEM((rows, heads * cols), BRAIN),
            pltpu.VMEM((width, heads * cols), BRAIN),
        ],
        compiler_params=pltpu.CompilerParams(vmem_limit_bytes=VMEM_BYTES),
        cost_estimate=pl.CostEstimate(
            flops=4 * rows * heads * cols * width, bytes_accessed=8 << 20, transcendentals=0
        ),
        name="frames_back",
    )(*ins)


def merge_kernel(count, joined, mine_ref, *refs):
    ins, outs = refs[: 4 * count], refs[4 * count :]
    at = 0
    for n in range(count):
        for which in range(2):
            value = ins[4 * n + which][...] + ins[4 * n + 2 + which][...]
            value = value.reshape(
                [d for i, d in enumerate(ins[4 * n].shape) if i != 1]
            )
            if joined:
                outs[which][:, :, :, at : at + value.shape[-1]] = value
            else:
                outs[2 * n + which][...] = value
        at += ins[4 * n].shape[-1]


def merge(mine, parts, places, steps, joined=False):
    ins, in_specs, outs, out_specs = [], [], [], []
    for (keep, come, outer, inner), place in zip(parts, places):
        rows, columns = keep.shape[-2:]
        size = outer * inner // steps
        if inner >= size:
            block, per = (1, size), inner // size
        else:
            block, per = (size // inner, inner), 1

        def index(which, g, m, place=place, per=per):
            return (g // per, m[place] if which == 0 else 1 - m[place], g % per, 0, 0)

        for array in (keep, come):
            for which in range(2):
                ins.append(array.reshape(outer, 2, inner, rows, columns))
                in_specs.append(
                    pl.BlockSpec(
                        (block[0], 1, block[1], rows, columns), functools.partial(index, which)
                    )
                )
        for which in range(2):
            outs.append(jax.ShapeDtypeStruct((outer, inner, rows, columns), BRAIN))
            out_specs.append(
                pl.BlockSpec(
                    block + (rows, columns), lambda g, m, per=per: (g // per, g % per, 0, 0)
                )
            )
    if joined:
        whole_columns = sum(o.shape[-1] for o in outs) // 2
        shape = outs[0].shape[:-1] + (whole_columns,)
        outs = [jax.ShapeDtypeStruct(shape, BRAIN)] * 2
        spec = pl.BlockSpec(
            out_specs[0].block_shape[:-1] + (whole_columns,), out_specs[0].index_map
        )
        out_specs = [spec] * 2
    res = pl.pallas_call(
        functools.partial(merge_kernel, len(parts), joined),
        grid_spec=pltpu.PrefetchScalarGridSpec(
            num_scalar_prefetch=1, grid=(steps,), in_specs=in_specs, out_specs=out_specs
        ),
        out_shape=outs,
        compiler_params=pltpu.CompilerParams(vmem_limit_bytes=VMEM_BYTES),
        cost_estimate=pl.CostEstimate(flops=1 << 22, bytes_accessed=8 << 20, transcendentals=0),
        name="merge",
    )(mine, *ins)
    flat = [r.reshape((-1,) + r.shape[2:]) for r in res]
    return [(flat[2 * n], flat[2 * n + 1]) for n in range(len(flat) // 2)]


def project_end_kernel(keep_ref, come_ref, out_ref, bias_ref):
    heads = keep_ref.shape[0]
    for h in range(heads):
        value = keep_ref[h].astype(FLOAT) + come_ref[h].astype(FLOAT)
        own = slice(h * HEAD_DIM, (h + 1) * HEAD_DIM)
        for i, at in enumerate((LANES + HEAD_DIM, HEAD_DIM, 0)):
            out_ref[i, :, own] = value[:, at : at + HEAD_DIM]
        bias_ref[h] = value[:, LANES : LANES + HEAD_DIM]


def project_end(keep, come):
    heads, share, _ = keep.shape
    return pl.pallas_call(
        project_end_kernel,
        out_shape=[
            jax.ShapeDtypeStruct((3, share, heads * HEAD_DIM), FLOAT),
            jax.ShapeDtypeStruct((heads, share, HEAD_DIM), FLOAT),
        ],
        cost_estimate=pl.CostEstimate(flops=1 << 18, bytes_accessed=1 << 20, transcendentals=0),
        name="project_end",
    )(keep, come)


def fence(*values):
    return lax.optimization_barrier(values)


def tie(first, second):
    return fence(first, second)[0]


def body(
    frames,
    segment_ids,
    project_weight,
    query_value_bias,
    output_weight,
    output_bias,
    first_gain,
    first_shift,
    expand_weight,
    expand_bias,
    reduce_weight,
    reduce_bias,
    second_gain,
    second_shift,
    cotangent,
    *,
    groups,
):
    rows, width = frames.shape
    cols = project_weight.shape[2]
    hidden = expand_weight.shape[1]
    heads = cols // HEAD_DIM
    length = 4 * rows
    me = lax.axis_index("tensor")
    half = lax.axis_index("dp") % 2
    half_two = (lax.axis_index("dp") // 2) % 2
    other = functools.partial(swap, axis="tensor", size=4)

    far = other(frames, bits=2)
    near = other(frames, bits=1)

    blocks = segment_ids.reshape(4, rows)
    segs = jnp.concatenate([lax.dynamic_index_in_dim(blocks, me ^ k, 0) for k in range(4)], axis=1)
    vectors = jnp.stack(
        [output_bias, first_gain, first_shift, reduce_bias, second_gain, second_shift]
    ).astype(FLOAT)
    vectors = jnp.pad(vectors, ((0, 2), (0, 0)))
    bias = query_value_bias.astype(FLOAT).reshape(2, heads, HEAD_DIM)
    bias = jnp.stack(
        [
            jnp.pad(bias[0], ((0, 0), (HEAD_DIM, 0))).reshape(-1),
            jnp.pad(bias[1], ((0, 0), (0, HEAD_DIM))).reshape(-1),
        ]
    )
    wide_halves = jnp.concatenate(
        [
            expand_weight.T.reshape(2, hidden // 2, width),
            output_weight.reshape(2, cols // 2, width),
            jnp.broadcast_to(
                jnp.pad(expand_bias[None], ((0, 15), (0, width - hidden))), (2, 16, width)
            ),
        ],
        axis=1,
    )
    wide = wide_halves.reshape(-1, width)
    wide_half = lax.dynamic_index_in_dim(wide_halves, half, 0, False)
    back_half = lax.dynamic_index_in_dim(
        reduce_weight.reshape(2, hidden // 2, width), half_two, 0, False
    )
    wide_later, back_later = tie((wide, reduce_weight), near)
    near_wide = other(wide_later, bits=1)
    near_back = other(back_later, bits=1)
    *started, spread_weight = project(0, (frames, near), project_weight, bias, segs, ())

    far, started, wide_half, back_half, near_wide, near_back = fence(
        far, started, wide_half, back_half, near_wide, near_back
    )
    last = other(far, bits=1)

    got_wide = other(wide_half, bits=2)
    got_back = other(back_half, bits=2)
    qt, ka, vt, qz, kt, va, xt = project(
        2, (far, last), spread_weight, bias, segs, started
    )
    far_blocks = attend(qt, ka, vt, rows, 2, 2, False)
    far_blocks, got_wide, got_back, qt_later = fence(far_blocks, got_wide, got_back, qt)
    relayed = swap(got_wide, "dp", groups, 1)
    relayed_back = swap(got_back, "dp", groups, 2)
    far_mixed = other(far_blocks[0][0], bits=2)
    last_wide = other(got_wide, bits=1)
    last_back = other(got_back, bits=1)
    near_blocks = attend(qt_later, ka, vt, rows, 0, 2, True)
    near_blocks, relayed, relayed_back, far_mixed, last_wide, last_back = fence(
        near_blocks, relayed, relayed_back, far_mixed, last_wide, last_back
    )
    near_mixed = other(near_blocks[0][1], bits=1)
    last_mixed = other(far_mixed[1:], bits=1)
    mixed = [near_blocks[0][0], near_mixed, far_mixed, last_mixed]

    riding = groups * 8 == SLOTS and 2 * LANES - cols == SLOTS and (width // groups) % 16 == 0
    outs = layer(
        jnp.stack([half, half_two]).astype(jnp.int32),
        mixed,
        frames,
        cotangent,
        vectors,
        (wide, near_wide, got_wide, relayed, last_wide, other(relayed, bits=1)),
        (reduce_weight, near_back, got_back, relayed_back, last_back, other(relayed_back, bits=1)),
        riding,
    )
    layer_out, grad_first = outs[:2]
    own_grad, near_grad, far_grad, small = outs[2:6]
    keeps, sends = outs[6:9], outs[9:12]
    far_grad = other(far_grad, bits=2)
    near_grad = other(near_grad, bits=1)

    bits = [2**n for n in reversed(range(groups.bit_length() - 1))]
    share = width // groups
    steps = [0] + bits[::-1]
    orders = [steps[n:3] + steps[:n] for n in range(3)]
    arrived = [other(send, bits=1) for send in sends]
    forms = (qt, ka, qz, kt, va, xt)
    exacts = [near_blocks[1], far_blocks[1]]
    logs = [near_blocks[2], far_blocks[2]]
    begun, query = attend_back_own(forms, own_grad, exacts[0], logs[0])
    arrived, begun, far_grad, near_grad = fence(arrived, begun, far_grad, near_grad)
    grad_heads = [near_grad, far_grad, other(far_grad[1:], bits=1)]
    mine = jnp.stack([jnp.zeros_like(half)] + [(lax.axis_index("dp") // b) % 2 for b in bits])
    mine = mine.astype(jnp.int32)
    axes = [0] + bits
    left = [list(axes) for _ in orders]
    values = [
        (keep.reshape(2 * groups, share, -1), come.reshape(2 * groups, share, -1))
        for keep, come in zip(keeps, arrived)
    ]

    def divide(values, chosen, steps, joined=False):
        parts = []
        for n, ((keep, come), axis) in enumerate(zip(values, chosen)):
            at = left[n].index(axis)
            parts.append((keep, come, 2**at, 2 ** (len(left[n]) - at - 1)))
            left[n] = [b for b in left[n] if b != axis]
        return merge(mine, parts, [axes.index(axis) for axis in chosen], steps, joined)

    def go(value, axis):
        return other(value, bits=2) if axis == 0 else swap(value, "dp", groups, axis)

    def sent_half(value, axis):
        count, lead = value.shape[:2]
        at = tail_left.index(axis)
        view = value.reshape((count, 2**at, 2, lead // 2 ** (at + 1)) + value.shape[2:])
        bit = (lax.axis_index("dp") // axis) % 2
        shape = (count, lead // 2) + value.shape[2:]
        keep_ = lax.dynamic_index_in_dim(view, bit, 2, keepdims=False).reshape(shape)
        send = lax.dynamic_index_in_dim(view, 1 - bit, 2, keepdims=False).reshape(shape)
        return keep_, swap(send, "dp", groups, axis)

    def added(pair):
        return (pair[0].astype(FLOAT) + pair[1].astype(FLOAT)).astype(BRAIN)

    def phase(values, number, steps):
        order = [o[number] for o in orders]
        halves = divide(values, order, steps)
        return [(half_[0], go(half_[1], axis)) for half_, axis in zip(halves, order)]

    def keeps_of(values):
        return [value[0] for value in values]

    tail_left = list(bits)
    values = phase(values, 0, 4)
    begun = tie(begun, keeps_of(values))
    head_args = (share, forms, grad_heads, exacts, logs)
    most = attend_back(0, heads - 1, *head_args, begun, query)
    most, values = fence(most, values)

    values = phase(values, 1, 2)
    early = sent_half(most[1], 1)
    begun = tie(begun, (keeps_of(values), early[0]))
    final = attend_back(heads - 1, 1, *head_args, begun, query)
    final, values = fence(final, values)

    values = phase(values, 2, 1)
    late = sent_half(final[1], 1)
    most_rows, final_rows, grad_first = tie(
        (most[0], final[0], grad_first), (keeps_of(values), late[0])
    )
    sent = frames_back(most_rows, final_rows, spread_weight)
    sent, values = fence(sent, values)
    got = other(sent, bits=1)
    rest = steps[3:]
    while len(rest) > 1:
        values = [
            (half_[0], go(half_[1], rest[0])) for half_ in divide(values, [rest[0]] * 3, 1)
        ]
        rest = rest[1:]
    ((kept, going),) = divide(values, [rest[0]] * 3, 1, True)
    come = go(going, rest[0])
    most_rows, final_rows, grad_first = tie((most_rows, final_rows, grad_first), (sent, kept))
    own_sum, far_sum = frames_back(most_rows, final_rows, spread_weight, grad_first)
    own_sum, far_sum, got = fence(own_sum, far_sum, got)
    far_sum = (far_sum + got[1].astype(FLOAT)).astype(BRAIN)
    far_got = other(far_sum, bits=2)
    early, late, come = tie((early, late, come), far_sum)
    tail_left.remove(1)
    tail = jnp.concatenate([added(early), added(late)])
    for axis in bits[::-1][1:-1]:
        pair = sent_half(tail, axis)
        tail_left.remove(axis)
        if axis != bits[1]:
            tail = added(pair)
    tail_keep, tail_come = sent_half(added(pair), rest[0])
    frames_grad = own_sum + got[0].astype(FLOAT) + far_got.astype(FLOAT)
    joined = (kept.astype(FLOAT) + come.astype(FLOAT))[0]

    arrays = [[], [], []]
    at = 0
    for portion in portions(width, hidden):
        for array, _, count in portion.spans:
            arrays[array].append(joined[:, at : at + count])
            at += count
    expand_grad, reduce_grad, output_grad = [jnp.concatenate(a, axis=1) for a in arrays]
    if riding:
        sums = jnp.swapaxes(output_grad[:, cols:].T.reshape(groups, 8, share), 0, 1)
        sums = sums.reshape(8, width)
        vector_grads, expand_bias_grad = sums[:6], sums[6, :hidden]
    else:
        everyone = lax.all_gather(small, ("dp", "tensor")).reshape(groups, 4, 16, width)
        vector_grads = jnp.sum(everyone[:, :, :6], axis=(0, 1))
        picked = [
            lax.dynamic_index_in_dim(everyone[:, s], 8 + (me ^ s), 1, False) for s in range(4)
        ]
        expand_bias_grad = sum(jnp.sum(p, axis=0) for p in picked)
    reduce_grad = reduce_grad.T
    output_grad = output_grad[:, :cols].T

    project_grad, tail = project_end(tail_keep[:, 0], tail_come[:, 0])
    spread = 3 * HEAD_DIM // share
    bias_sums = jnp.swapaxes(tail[:, :, :spread], 1, 2)
    bias_sums = bias_sums.reshape(heads, 3, HEAD_DIM)
    attend_bias_grad = jnp.stack([bias_sums[:, i].reshape(cols) for i in (2, 0)])
    return (
        layer_out,
        frames_grad,
        project_grad,
        attend_bias_grad,
        output_grad,
        expand_grad,
        expand_bias_grad,
        reduce_grad,
        vector_grads,
    )


def solution(mesh):
    placed = (
        P(("dp", "tensor"), None),
        P("dp", None),
        P(None, None, "tensor"),
        P(None, "tensor"),
        P("tensor", None),
        P(),
        P(),
        P(),
        P(None, "tensor"),
        P("tensor"),
        P("tensor", None),
        P(),
        P(),
        P(),
        P(("dp", "tensor"), None),
    )
    return jax.shard_map(
        functools.partial(body, groups=mesh.shape["dp"]),
        mesh=mesh,
        in_specs=placed,
        out_specs=(
            P(("dp", "tensor"), None),
            P(("dp", "tensor"), None),
            P(None, "dp", "tensor"),
            P(None, "tensor"),
            P("tensor", "dp"),
            P("dp", "tensor"),
            P("tensor"),
            P("tensor", "dp"),
            P(),
        ),
        check_vma=False,
    )
```

```python
import functools

import jax
import jax.numpy as jnp
import numpy as np
from jax import lax
from jax.experimental import pallas as pl
from jax.experimental.pallas import tpu as pltpu
from jax.sharding import PartitionSpec as P

HEAD_DIM = 64
ROW_LEN = 2048
EPS = 1e-05
FLOAT = jnp.float32
BRAIN = jnp.bfloat16
BIG = 1e30
SCALE = HEAD_DIM ** (-0.5)
VMEM_BYTES = 60 << 20
IDS = 8
LANES = 128
CHUNK = 1024
BACK_CHUNK = 512
SLOTS = 64

NN = (((1,), (0,)), ((), ()))
NT = (((1,), (1,)), ((), ()))


def dot(left, right, dims=NN):
    return lax.dot_general(left, right, dims, preferred_element_type=FLOAT)


def swap(value, axis, size, bits):
    return lax.ppermute(value, axis, [(i, i ^ bits) for i in range(size)])


def whole(shape):
    return pl.BlockSpec(shape, lambda *_: (0,) * len(shape), pipeline_mode=pl.Buffered(1))


def split_three(value):
    top = value.astype(BRAIN).astype(FLOAT)
    rest = value - top
    middle = rest.astype(BRAIN).astype(FLOAT)
    return top, middle, rest - middle


def project_kernel(heads, rows, first, *refs):
    x_refs = refs[:2]
    w_ref, bias_ref, segs_ref = refs[2:5]
    if first:
        held = refs[-1]
        spread = refs[-2]
        forms = refs[-9:-2]
    else:
        held = refs[-1]
        spread = w_ref
        forms = refs[-8:-1]
    qt_ref, ka_ref, vt_ref, qz_ref, kt_ref, va_ref, xt_ref = forms
    step = pl.program_id(0)
    for k in range(2):

        @pl.when(step == k)
        def _():
            held[...] = x_refs[k][...]

    if first:

        @pl.when(step == 0)
        def _():
            nothing = jnp.zeros((w_ref.shape[1], HEAD_DIM), BRAIN)
            for i in range(3):
                for h in range(heads):
                    own = w_ref[i, :, h * HEAD_DIM : (h + 1) * HEAD_DIM]
                    pair = [own, nothing] if i == 2 else [nothing, own]
                    spread[i, :, h * LANES : (h + 1) * LANES] = jnp.concatenate(pair, axis=1)

    x = held[...]
    xt_ref[...] = x.T
    segs = segs_ref[...].astype(FLOAT)
    number = lax.broadcasted_iota(jnp.int32, (HEAD_DIM, rows), 0).astype(FLOAT)
    qtail = jnp.where(jnp.broadcast_to(segs, (HEAD_DIM, rows)) == number, 1.0, 0.0).astype(BRAIN)
    lane = lax.broadcasted_iota(jnp.int32, (rows, LANES), 1)
    differ = jnp.broadcast_to(segs, (LANES, rows)).T != lane.astype(FLOAT)
    ktail = jnp.where(lane < IDS, jnp.where(differ, -BIG, 0.0), jnp.where(lane < IDS + 3, -1.0, 0.0))
    minus = jnp.where((lane >= HEAD_DIM) & (lane < HEAD_DIM + 3), -1.0, 0.0)
    query = (dot(x, spread[0]) + bias_ref[0:1]).astype(BRAIN).astype(FLOAT) * SCALE
    key = dot(x, spread[1])
    value = dot(x, spread[2]) + bias_ref[1:2]
    for h in range(heads):
        own = slice(h * LANES, (h + 1) * LANES)
        q, k_, v = query[:, own], key[:, own], value[:, own]
        qt_ref[h, :HEAD_DIM, :] = qtail
        qt_ref[h, HEAD_DIM:, :] = q.T[HEAD_DIM:].astype(BRAIN)
        kt_ref[h] = k_.T.astype(BRAIN)
        vt_ref[h] = v.T[:HEAD_DIM].astype(BRAIN)
        ka_ref[h] = (k_ + ktail).astype(BRAIN)
        va_ref[h] = (v + minus).astype(BRAIN)
        qz_ref[h, :HEAD_DIM, :] = jnp.zeros((HEAD_DIM, rows), BRAIN)
        qz_ref[h, HEAD_DIM:, :] = qt_ref[h, HEAD_DIM:, :]


def project(first, pieces, weight, bias, segs, before):
    rows, width = pieces[0].shape
    heads = bias.shape[1] // LANES
    length = 4 * rows
    by_lane = lambda i: (0, 0, first + i)
    by_row = lambda i: (0, first + i, 0)
    shapes = [
        ((heads, LANES, length), (heads, LANES, rows), by_lane),
        ((heads, length, LANES), (heads, rows, LANES), by_row),
        ((heads, HEAD_DIM, length), (heads, HEAD_DIM, rows), by_lane),
        ((heads, LANES, length), (heads, LANES, rows), by_lane),
        ((heads, LANES, length), (heads, LANES, rows), by_lane),
        ((heads, length, LANES), (heads, rows, LANES), by_row),
        ((width, length), (width, rows), lambda i: (0, first + i)),
    ]
    out_specs = [pl.BlockSpec(block, index) for _, block, index in shapes]
    if not before:
        shapes.append(((3, width, heads * LANES), None, None))
        out_specs.append(whole(shapes[-1][0]))
    return pl.pallas_call(
        functools.partial(project_kernel, heads, rows, not before),
        grid=(2,),
        in_specs=[
            whole((rows, width)),
            whole((rows, width)),
            whole(weight.shape),
            whole(bias.shape),
            pl.BlockSpec((1, rows), lambda i: (0, first + i)),
        ]
        + [pl.BlockSpec(memory_space=pl.ANY)] * len(before),
        out_specs=out_specs,
        out_shape=[jax.ShapeDtypeStruct(s[0], BRAIN) for s in shapes],
        scratch_shapes=[pltpu.VMEM((rows, width), BRAIN)],
        input_output_aliases={5 + n: n for n in range(len(before))},
        compiler_params=pltpu.CompilerParams(vmem_limit_bytes=VMEM_BYTES),
        cost_estimate=pl.CostEstimate(
            flops=12 * rows * width * heads * LANES, bytes_accessed=8 << 20, transcendentals=0
        ),
        name="project",
    )(*pieces, weight, bias, segs, *before)


def attend_kernel(rows, count, *refs):
    qt_ref, ka_ref, vt_ref = refs[:3]
    out_refs, exact_ref, log_ref, held = refs[3:-3], refs[-3], refs[-2], refs[-1]
    length = ka_ref.shape[1]
    part, chunk = held.shape[2], min(CHUNK, length)
    chunks = [slice(at, at + chunk) for at in range(0, length, chunk)]
    items = [(n, at) for n in range(count) for at in range(0, rows, part)]

    def score(item, keys):
        n, at = items[item]
        first = n * rows + at
        scores = dot(ka_ref[0, keys], qt_ref[0, :, first : first + part])
        held[item % 2, keys] = scores
        return jnp.max(scores, axis=0, keepdims=True)

    highest = functools.reduce(jnp.maximum, [score(0, keys) for keys in chunks])
    for item, (n, at) in enumerate(items):
        tops, total, mixed = [], 0.0, 0.0
        for keys in chunks:
            if item + 1 < len(items):
                tops.append(score(item + 1, keys))
            raised = jnp.exp(held[item % 2, keys] - highest)
            total = total + jnp.sum(raised, axis=0, keepdims=True)
            mixed = mixed + dot(vt_ref[0, :, keys], raised.astype(BRAIN))
        mixed = mixed / total
        lanes = slice(at, at + part)
        if len(out_refs) == 1:
            out_refs[0][n, :, lanes] = mixed.astype(BRAIN)
        else:
            out_refs[n][0, :, lanes] = mixed.astype(BRAIN)
        exact_ref[n, :, lanes] = mixed
        log_ref[0, n : n + 1, lanes] = highest + jnp.log(total)
        if tops:
            highest = functools.reduce(jnp.maximum, tops)


def attend(qt, ka, vt, rows, first, count, parted):
    heads, _, length = qt.shape
    cols = heads * HEAD_DIM
    by_head = lambda h: (0, h, 0)
    sizes = [1] * count if parted else [count]
    outs = pl.pallas_call(
        functools.partial(attend_kernel, rows, count),
        grid=(heads,),
        in_specs=[
            pl.BlockSpec((1, LANES, count * rows), lambda h: (h, 0, first // count)),
            pl.BlockSpec((1, length, LANES), lambda h: (h, 0, 0)),
            pl.BlockSpec((1, HEAD_DIM, length), lambda h: (h, 0, 0)),
        ],
        out_specs=[pl.BlockSpec((n, HEAD_DIM, rows), by_head) for n in sizes]
        + [
            pl.BlockSpec((count, HEAD_DIM, rows), by_head),
            pl.BlockSpec((1, count, rows), lambda h: (h, 0, 0)),
        ],
        out_shape=[jax.ShapeDtypeStruct((n, cols, rows), BRAIN) for n in sizes]
        + [
            jax.ShapeDtypeStruct((count, cols, rows), FLOAT),
            jax.ShapeDtypeStruct((heads, count, rows), FLOAT),
        ],
        scratch_shapes=[pltpu.VMEM((2, length, rows // 2), FLOAT)],
        compiler_params=pltpu.CompilerParams(vmem_limit_bytes=VMEM_BYTES),
        cost_estimate=pl.CostEstimate(
            flops=8 * heads * length * count * rows * LANES,
            bytes_accessed=8 << 20,
            transcendentals=heads * length * count * rows,
        ),
        name="attend",
    )(qt, ka, vt)
    return outs[:-2], outs[-2], outs[-1]


def fill(slot, queries, grads, plain, qt, grad, exact, log):
    rows = queries.shape[2]
    low = lax.broadcasted_iota(jnp.int32, (8, rows), 0)

    def stacked(value):
        top, middle, bottom = split_three(value)
        return jnp.where(
            low == 0, top, jnp.where(low == 1, middle, jnp.where(low == 2, bottom, 0.0))
        )

    nothing = jnp.zeros((LANES - HEAD_DIM - 16, rows), BRAIN)
    delta = jnp.sum(grad.astype(FLOAT) * exact, axis=0, keepdims=True)
    ids = qt[:16].astype(FLOAT)[:IDS]
    queries[slot, :16] = jnp.concatenate([ids, stacked(log)], axis=0).astype(BRAIN)
    queries[slot, 16:] = qt[16:]
    grads[slot, :HEAD_DIM] = grad
    grads[slot, HEAD_DIM : HEAD_DIM + 16] = jnp.concatenate(
        [stacked(delta), jnp.zeros((8, rows), FLOAT)], axis=0
    ).astype(BRAIN)
    grads[slot, HEAD_DIM + 16 :] = nothing
    plain[slot, :HEAD_DIM] = grad
    plain[slot, HEAD_DIM:] = jnp.zeros((LANES - HEAD_DIM, rows), BRAIN)


def back_block(slot, queries, grads, plain, qz, ka_ref, kt_ref, va_ref, add):
    length = ka_ref.shape[1]
    chunk = min(BACK_CHUNK, length)
    grad_query = 0.0
    for at in range(0, length, chunk):
        keys = slice(at, at + chunk)
        probs = jnp.exp(dot(ka_ref[0, keys], queries[slot]))
        grad_scores = (probs * dot(va_ref[0, keys], grads[slot])).astype(BRAIN)
        add(keys, dot(probs.astype(BRAIN), plain[slot], NT) + dot(grad_scores, qz, NT))
        grad_query = grad_query + dot(kt_ref[0, :, keys], grad_scores)
    return (grad_query * SCALE).T.astype(BRAIN)


def attend_back_own_kernel(*refs):
    qt_ref, ka_ref, qz_ref, kt_ref, va_ref = refs[:5]
    grad_ref, exact_ref, log_ref = refs[5:8]
    total_ref, query_ref = refs[8:10]
    scratch = refs[10:]
    fill(0, *scratch, qt_ref[0], grad_ref[0], exact_ref[0], log_ref[0, 0:1])

    def add(keys, value):
        total_ref[0, keys] = value

    query_ref[0] = back_block(0, *scratch, qz_ref[0], ka_ref, kt_ref, va_ref, add)


def attend_back_own(forms, grad, exact, log):
    qt, ka, qz, kt, va, _ = forms
    heads, length = ka.shape[:2]
    rows = length // 4
    by_head = lambda h: (h, 0, 0)
    return pl.pallas_call(
        attend_back_own_kernel,
        grid=(heads,),
        in_specs=[
            pl.BlockSpec((1, LANES, rows), by_head),
            pl.BlockSpec((1, length, LANES), by_head),
            pl.BlockSpec((1, LANES, rows), by_head),
            pl.BlockSpec((1, LANES, length), by_head),
            pl.BlockSpec((1, length, LANES), by_head),
            pl.BlockSpec((1, HEAD_DIM, rows), lambda h: (0, h, 0)),
            pl.BlockSpec((1, HEAD_DIM, rows), lambda h: (0, h, 0)),
            pl.BlockSpec((1, 2, rows), by_head),
        ],
        out_specs=[
            pl.BlockSpec((1, length, LANES), by_head),
            pl.BlockSpec((1, rows, LANES), by_head),
        ],
        out_shape=[
            jax.ShapeDtypeStruct((heads, length, LANES), FLOAT),
            jax.ShapeDtypeStruct((heads, rows, LANES), BRAIN),
        ],
        scratch_shapes=[pltpu.VMEM((1, LANES, rows), BRAIN)] * 3,
        compiler_params=pltpu.CompilerParams(vmem_limit_bytes=VMEM_BYTES),
        cost_estimate=pl.CostEstimate(
            flops=18 * length * length * LANES,
            bytes_accessed=8 << 20,
            transcendentals=length * length,
        ),
        name="attend_back_own",
    )(qt, ka, qz, kt, va, grad, exact, log)


def attend_back_kernel(rows, first, share, *refs):
    qt_ref, ka_ref, qz_ref, kt_ref, va_ref, xt_ref = refs[:6]
    grad_refs, exacts, logs = refs[6:9], refs[9:12], refs[12:14]
    begun_ref, query_ref = refs[14:16]
    out_ref, project_ref = refs[16:18]
    total, begun, xt = refs[18:21]
    scratch = refs[21:24]
    sem = refs[24]
    step = pl.program_id(0)
    begun_copy = pltpu.make_async_copy(begun_ref.at[first + step], begun, sem.at[0])
    xt_copy = pltpu.make_async_copy(xt_ref, xt, sem.at[1])
    begun_copy.start()
    pl.when(step == 0)(xt_copy.start)
    for k in range(3):
        at = pl.ds((k + 1) * rows, rows)
        log = logs[(k + 1) // 2][0, (k + 1) % 2 : (k + 1) % 2 + 1]
        fill(k, *scratch, qt_ref[0, :, at], grad_refs[k][0], exacts[k][0], log)
    out_ref[0, :rows, LANES:] = query_ref[0]
    for k in range(3):

        def add(keys, value):
            if k == 0:
                total[keys] = value
            else:
                total[keys] += value

        at = pl.ds((k + 1) * rows, rows)
        qz = qz_ref[0, :, at]
        out_ref[0, at, LANES:] = back_block(k, *scratch, qz, ka_ref, kt_ref, va_ref, add)
    begun_copy.wait()
    pl.when(step == 0)(xt_copy.wait)
    out_ref[0, :, :LANES] = (total[...] + begun[...]).astype(BRAIN)
    pieces = out_ref[0]
    project_ref[0] = dot(xt[...], pieces).astype(BRAIN)
    bias = jnp.sum(pieces.astype(FLOAT), axis=0, keepdims=True)
    if share % 16 == 0:
        bias = jnp.concatenate([bias[:, :LANES], bias[:, LANES + HEAD_DIM :]], axis=1)
        spread = 3 * HEAD_DIM // share
        line = jnp.concatenate(
            [bias[:, n * share : (n + 1) * share] for n in range(spread)]
            + [jnp.zeros((8 - spread, share), FLOAT)],
            axis=0,
        ).T.astype(BRAIN)
        for at in range(0, project_ref.shape[1], share):
            project_ref[0, at : at + share, LANES : LANES + 8] = line
    else:
        refs[25][0] = bias


def attend_back(first, count, share, forms, grads, exacts, logs, begun, query):
    qt, ka, qz, kt, va, xt = forms
    length, width = ka.shape[1], xt.shape[0]
    rows = length // 4
    cols = 2 * LANES
    own = lambda i: (first + i, 0, 0)
    by_block = lambda n: pl.BlockSpec((1, HEAD_DIM, rows), lambda i: (n, first + i, 0))
    each = lambda i: (i, 0, 0)
    out_specs = [pl.BlockSpec((1, length, cols), each), pl.BlockSpec((1, width, cols), each)]
    out_shape = [
        jax.ShapeDtypeStruct((count, length, cols), BRAIN),
        jax.ShapeDtypeStruct((count, width, cols), BRAIN),
    ]
    scratch = (
        [
            pltpu.VMEM((length, LANES), FLOAT),
            pltpu.VMEM((length, LANES), FLOAT),
            pltpu.VMEM((width, length), BRAIN),
        ]
        + [pltpu.VMEM((3, LANES, rows), BRAIN)] * 3
        + [pltpu.SemaphoreType.DMA((2,))]
    )
    kernel = functools.partial(attend_back_kernel, rows, first, share)
    if share % 16:
        out_specs.append(pl.BlockSpec((1, 1, cols), each))
        out_shape.append(jax.ShapeDtypeStruct((count, 1, cols), FLOAT))
        kernel = lambda *refs: attend_back_kernel(
            rows, first, share, *refs[:18], *refs[19:], refs[18]
        )
    res = pl.pallas_call(
        kernel,
        grid=(count,),
        in_specs=[
            pl.BlockSpec((1, LANES, length), own),
            pl.BlockSpec((1, length, LANES), own),
            pl.BlockSpec((1, LANES, length), own),
            pl.BlockSpec((1, LANES, length), own),
            pl.BlockSpec((1, length, LANES), own),
            pl.BlockSpec(memory_space=pl.ANY),
        ]
        + [by_block(0)] * 3
        + [by_block(1), by_block(0), by_block(1)]
        + [pl.BlockSpec((1, 2, rows), own)] * 2
        + [pl.BlockSpec(memory_space=pl.ANY), pl.BlockSpec((1, rows, LANES), own)],
        out_specs=out_specs,
        out_shape=out_shape,
        scratch_shapes=scratch,
        compiler_params=pltpu.CompilerParams(vmem_limit_bytes=VMEM_BYTES),
        cost_estimate=pl.CostEstimate(
            flops=20 * count * length * length * LANES,
            bytes_accessed=8 << 20,
            transcendentals=count * length * length,
        ),
        name="attend_back",
    )(qt, ka, qz, kt, va, xt, *grads, exacts[0], exacts[1], exacts[1], *logs, begun, query)
    project_grad = res[1].reshape(count, width // share, share, cols)
    if share % 16:
        spread = 3 * HEAD_DIM // share
        bias = jnp.concatenate([res[2][..., :LANES], res[2][..., LANES + HEAD_DIM :]], axis=2)
        bias = jnp.swapaxes(bias.reshape(count, 1, spread, share), 2, 3).astype(BRAIN)
        bias = jnp.broadcast_to(bias, (count, width // share, share, spread))
        project_grad = jnp.concatenate(
            [
                project_grad[..., :LANES],
                bias,
                project_grad[..., LANES + spread :],
            ],
            axis=3,
        )
    return res[0], project_grad


def gelu_parts(values):
    t = 1.0 / (1.0 + (0.3275911 * 0.7071067811865476) * jnp.abs(values))
    bell = jnp.exp(-0.5 * values * values)
    poly = 0.5 * 1.061405429
    for c in (-1.453152027, 1.421413741, -0.284496736, 0.254829592):
        poly = poly * t + 0.5 * c
    tail = poly * t * bell
    below = jnp.where(values >= 0, 1.0 - tail, tail)
    return values * below, below + values * bell * 0.3989422804014327


def mean_of(values):
    return jnp.mean(values, axis=-1, keepdims=True)


class Portion:
    def __init__(self, *spans):
        self.spans = spans
        self.columns = sum(span[2] for span in spans)


def portions(width, hidden):
    if hidden == 6 * LANES:
        return (
            Portion((0, 0, 4 * LANES)),
            Portion((0, 4 * LANES, 2 * LANES), (1, 0, 3 * LANES)),
            Portion((1, 3 * LANES, 3 * LANES), (2, 0, 2 * LANES)),
        )
    return (Portion((0, 0, hidden)), Portion((1, 0, hidden)), Portion((2, 0, 2 * LANES)))


def layer_kernel(parts, hidden, riding, *refs):
    t_ref = refs[0]
    mixed = refs[1:5]
    x_ref, cot_ref, vec_ref = refs[5:8]
    wide_refs, back_refs = refs[8:14], refs[14:20]
    out_ref, grad_first_ref = refs[20:22]
    d_refs = (refs[22].at[0], refs[23].at[0], refs[24].at[0], refs[24].at[1])
    small_ref = refs[25]
    keeps, sends = refs[26:29], refs[29:32]
    wet, wo, eb, back, orow, act, slope, dz, stage, tail_stage = refs[32:42]
    wide_sem, back_sem, out_sem = refs[42:]
    half, back_half = t_ref[0], t_ref[1]
    width = x_ref.shape[1]
    part = mixed[0].shape[1]
    bias_out, gain_one, shift_one, bias_red, gain_two, shift_two = (
        vec_ref[i : i + 1] for i in range(6)
    )

    split = hidden // 2 + part // 2 + 16

    def load_wide(k, n):
        if k < 2:
            source, first, which = wide_refs[k], n * split, n
        else:
            source, first, which = wide_refs[2 * k - 2 + n], 0, (half, 1 - half)[n]
        found = []
        for m, (at, count, target, to) in enumerate(
            [
                (0, hidden // 2, wet, k * hidden + which * (hidden // 2)),
                (hidden // 2, part // 2, wo, k * part + which * (part // 2)),
                (hidden // 2 + part // 2, 16, eb.at[k], which * 16),
            ]
        ):
            to = to if isinstance(to, int) else pl.multiple_of(to, 16)
            found.append(
                pltpu.make_async_copy(
                    source.at[pl.ds(first + at, count)],
                    target.at[pl.ds(to, count)],
                    wide_sem.at[k, n, m],
                )
            )
        return found

    loads = [[load_wide(k, n) for n in range(2)] for k in range(4)]
    def load_back(k, n):
        if k < 2:
            source, first, which = back_refs[k], n * (hidden // 2), n
        else:
            source, first, which = back_refs[2 * k - 2 + n], 0, (back_half, 1 - back_half)[n]
        to = k * hidden + which * (hidden // 2)
        to = to if isinstance(to, int) else pl.multiple_of(to, 16)
        return pltpu.make_async_copy(
            source.at[pl.ds(first, hidden // 2)],
            back.at[pl.ds(to, hidden // 2)],
            back_sem.at[k, n],
        )

    back_loads = [load_back(k, n) for k in range(4) for n in range(2)]

    def each(kind, k=None):
        return [c[kind] for pair in (loads if k is None else [loads[k]]) for c in pair]

    for copy in each(1):
        copy.start()
    for k in range(4):
        for copy in each(0, k) + each(2, k):
            copy.start()
    for k, ref in enumerate(mixed):
        orow[:, k * part : (k + 1) * part] = ref[0].astype(FLOAT).T.astype(BRAIN)
    for copy in each(1):
        copy.wait()
    for copy in back_loads:
        copy.start()
    total = x_ref[...].astype(FLOAT) + bias_out + dot(orow[...], wo[...])
    center = total - mean_of(total)
    inverse_one = lax.rsqrt(mean_of(center * center) + EPS)
    unit_one = center * inverse_one
    normed = unit_one * gain_one + shift_one
    hb = normed.astype(BRAIN)
    hbt = normed.T.astype(BRAIN)

    owns = [slice(j * hidden, (j + 1) * hidden) for j in range(4)]
    for copy in each(0) + each(2):
        copy.wait()
    inner = dot(hb, wet[owns[0]], NT)
    for j in range(4):
        now = inner + eb[j, :16].astype(FLOAT)[:1]
        if j < 3:
            inner = dot(hb, wet[owns[j + 1]], NT)
        active, derivative = gelu_parts(now)
        act[:, owns[j]] = active.astype(BRAIN)
        slope[:, owns[j]] = derivative
    for copy in back_loads:
        copy.wait()
    total = normed + dot(act[...], back[...]) + bias_red
    center = total - mean_of(total)
    inverse = lax.rsqrt(mean_of(center * center) + EPS)
    unit = center * inverse
    out_ref[...] = (unit * gain_two + shift_two).astype(BRAIN)
    cot = cot_ref[...].astype(FLOAT)
    scaled = cot * gain_two
    grad = inverse * (scaled - mean_of(scaled) - unit * mean_of(scaled * unit))
    small_ref[3:4] = jnp.sum(grad, axis=0, keepdims=True)
    small_ref[4:5] = jnp.sum(cot * unit, axis=0, keepdims=True)
    small_ref[5:6] = jnp.sum(cot, axis=0, keepdims=True)
    dfb = grad.astype(BRAIN)
    dfbt = grad.T.astype(BRAIN)

    def outgoing(block, array, first_sem):
        found = []
        for ref, portion in zip(keeps if block in (0, 2) else sends, parts):
            at = 0
            for held, first, count in portion.spans:
                if held == array:
                    source = tail_stage.at[block] if array == 2 else stage.at[block, array]
                    found.append(
                        pltpu.make_async_copy(
                            source.at[:, pl.ds(first, count)],
                            ref.at[block // 2, :, pl.ds(at, count)],
                            out_sem.at[block, first_sem + len(found)],
                        )
                    )
                at += count
        return found

    order = (1, 3, 0, 2)
    started = []
    for j in order:
        stage[j, 1] = dot(dfbt, act[:, owns[j]]).astype(BRAIN)
        copies = outgoing(j, 1, 2)
        for copy in copies:
            copy.start()
        started += copies
    grad_active = dot(dfb, back[owns[order[0]]], NT)
    for n, j in enumerate(order):
        now = grad_active
        if n < 3:
            grad_active = dot(dfb, back[owns[order[n + 1]]], NT)
        grad_inner = (now * slope[:, owns[j]]).astype(BRAIN)
        dz[:, owns[j]] = grad_inner
        small_ref[8 + j : 9 + j] = jnp.sum(grad_inner.astype(FLOAT), axis=0, keepdims=True)
        stage[j, 0] = dot(hbt, grad_inner).astype(BRAIN)
        copies = outgoing(j, 0, 0)
        for copy in copies:
            copy.start()
        started += copies
    grad = grad + dot(dz[...], wet[...])
    small_ref[1:2] = jnp.sum(grad * unit_one, axis=0, keepdims=True)
    small_ref[2:3] = jnp.sum(grad, axis=0, keepdims=True)
    scaled = grad * gain_one
    first = inverse_one * (scaled - mean_of(scaled) - unit_one * mean_of(scaled * unit_one))
    small_ref[0:1] = jnp.sum(first, axis=0, keepdims=True)
    small_ref[6:8] = jnp.zeros((2, width), FLOAT)
    small_ref[12:] = jnp.zeros((4, width), FLOAT)
    grad_first_ref[...] = first
    grad_mixed = dot(wo[...], first.astype(BRAIN), NT).astype(BRAIN)
    for k, ref in enumerate(d_refs):
        ref[...] = grad_mixed[k * part : (k + 1) * part]
    output_grad = dot(first.T.astype(BRAIN), orow[...]).astype(BRAIN)
    places = SLOTS // 8
    share = width // places
    sums = small_ref[...]
    for k in range(4):
        tail_stage[k, :, :part] = output_grad[:, k * part : (k + 1) * part]
        if riding:
            rows_k = jnp.concatenate([sums[:6], sums[8 + k : 9 + k], sums[6:7]], axis=0)
            lines = jnp.concatenate(
                [rows_k[:, c * share : (c + 1) * share] for c in range(places)], axis=0
            ).T.astype(BRAIN)
            tail_stage[k, :, part:] = jnp.concatenate([lines] * places, axis=0)
        else:
            tail_stage[k, :, part:] = jnp.zeros((width, 2 * LANES - part), BRAIN)
        copies = outgoing(k, 2, 4)
        for copy in copies:
            copy.start()
        started += copies
    for copy in started:
        copy.wait()


def layer(halves, mixed, frames, cotangent, vectors, wides, backs, riding):
    rows, width = frames.shape
    part = mixed[0].shape[1]
    hidden = backs[0].shape[0]
    parts = portions(width, hidden)
    grads = [jax.ShapeDtypeStruct((2, width, p.columns), BRAIN) for p in parts]
    grid_spec = pltpu.PrefetchScalarGridSpec(
        num_scalar_prefetch=1,
        grid=(1,),
        in_specs=[whole((1, part, rows))] * 4
        + [whole((rows, width)), whole((rows, width)), whole(vectors.shape)]
        + [pl.BlockSpec(memory_space=pl.ANY)] * 12,
        out_specs=[whole((rows, width)), whole((rows, width))]
        + [whole((n, part, rows)) for n in (1, 1, 2)]
        + [whole((16, width))]
        + [pl.BlockSpec(memory_space=pl.ANY)] * 6,
        scratch_shapes=[
            pltpu.VMEM((4 * hidden, width), BRAIN),
            pltpu.VMEM((4 * part, width), BRAIN),
            pltpu.VMEM((4, 32, width), BRAIN),
            pltpu.VMEM((4 * hidden, width), BRAIN),
            pltpu.VMEM((rows, width), BRAIN),
            pltpu.VMEM((rows, 4 * hidden), BRAIN),
            pltpu.VMEM((rows, 4 * hidden), FLOAT),
            pltpu.VMEM((rows, 4 * hidden), BRAIN),
            pltpu.VMEM((4, 2, width, hidden), BRAIN),
            pltpu.VMEM((4, width, 2 * LANES), BRAIN),
            pltpu.SemaphoreType.DMA((4, 2, 3)),
            pltpu.SemaphoreType.DMA((4, 2)),
            pltpu.SemaphoreType.DMA((4, 6)),
        ],
    )
    return pl.pallas_call(
        functools.partial(layer_kernel, parts, hidden, riding),
        grid_spec=grid_spec,
        out_shape=[
            jax.ShapeDtypeStruct((rows, width), BRAIN),
            jax.ShapeDtypeStruct((rows, width), FLOAT),
        ]
        + [jax.ShapeDtypeStruct((n, part, rows), BRAIN) for n in (1, 1, 2)]
        + [jax.ShapeDtypeStruct((16, width), FLOAT)]
        + grads
        + grads,
        compiler_params=pltpu.CompilerParams(vmem_limit_bytes=VMEM_BYTES),
        cost_estimate=pl.CostEstimate(
            flops=2 * rows * width * (24 * hidden + 3 * width),
            bytes_accessed=40 << 20,
            transcendentals=8 * rows * hidden,
        ),
        name="layer",
    )(halves, *mixed, frames, cotangent, vectors, *wides, *backs)


def frames_kernel(most_ref, last_ref, w_ref, base_ref, sent_ref, own_ref, far_ref, stack, weights):
    step = pl.program_id(0)
    heads = w_ref.shape[2] // LANES
    wide = 2 * LANES

    @pl.when(step == 0)
    def _():
        for h in range(heads):
            own = slice(h * LANES, (h + 1) * LANES)
            at = h * wide
            weights[:, at : at + LANES] = w_ref[1, :, own] + w_ref[2, :, own]
            weights[:, at + LANES : at + wide] = w_ref[0, :, own]

    for h in range(heads - 1):
        stack[:, h * wide : (h + 1) * wide] = most_ref[h]
    stack[:, (heads - 1) * wide :] = last_ref[0]
    value = dot(stack[...], weights[...], NT)

    @pl.when(step < 2)
    def _():
        sent_ref[0] = value.astype(BRAIN)

    @pl.when(step == 2)
    def _():
        own_ref[...] = base_ref[...] + value

    @pl.when(step == 3)
    def _():
        far_ref[...] = value


def frames_back(most, last, weight, base):
    heads = most.shape[0] + 1
    width = weight.shape[1]
    rows = most.shape[1] // 4
    cols = 2 * LANES
    block = lambda i: (0, jnp.where(i < 2, 2 * i + 1, 2 * i - 4), 0)
    return pl.pallas_call(
        frames_kernel,
        grid=(4,),
        in_specs=[
            pl.BlockSpec((heads - 1, rows, cols), block),
            pl.BlockSpec((1, rows, cols), block),
            whole(weight.shape),
            whole((rows, width)),
        ],
        out_specs=[
            pl.BlockSpec((1, rows, width), lambda i: (jnp.minimum(i, 1), 0, 0)),
            whole((rows, width)),
            whole((rows, width)),
        ],
        out_shape=[
            jax.ShapeDtypeStruct((2, rows, width), BRAIN),
            jax.ShapeDtypeStruct((rows, width), FLOAT),
            jax.ShapeDtypeStruct((rows, width), FLOAT),
        ],
        scratch_shapes=[
            pltpu.VMEM((rows, heads * cols), BRAIN),
            pltpu.VMEM((width, heads * cols), BRAIN),
        ],
        compiler_params=pltpu.CompilerParams(vmem_limit_bytes=VMEM_BYTES),
        cost_estimate=pl.CostEstimate(
            flops=8 * rows * heads * cols * width, bytes_accessed=16 << 20, transcendentals=0
        ),
        name="frames_back",
    )(most, last, weight, base)


def merge_kernel(count, joined, mine_ref, *refs):
    ins, outs = refs[: 4 * count], refs[4 * count :]
    at = 0
    for n in range(count):
        for which in range(2):
            value = ins[4 * n + which][...] + ins[4 * n + 2 + which][...]
            value = value.reshape(
                [d for i, d in enumerate(ins[4 * n].shape) if i != 1]
            )
            if joined:
                outs[which][:, :, :, at : at + value.shape[-1]] = value
            else:
                outs[2 * n + which][...] = value
        at += ins[4 * n].shape[-1]


def merge(mine, parts, places, steps, joined=False):
    ins, in_specs, outs, out_specs = [], [], [], []
    for (keep, come, outer, inner), place in zip(parts, places):
        rows, columns = keep.shape[-2:]
        size = outer * inner // steps
        if inner >= size:
            block, per = (1, size), inner // size
        else:
            block, per = (size // inner, inner), 1

        def index(which, g, m, place=place, per=per):
            return (g // per, m[place] if which == 0 else 1 - m[place], g % per, 0, 0)

        for array in (keep, come):
            for which in range(2):
                ins.append(array.reshape(outer, 2, inner, rows, columns))
                in_specs.append(
                    pl.BlockSpec(
                        (block[0], 1, block[1], rows, columns), functools.partial(index, which)
                    )
                )
        for which in range(2):
            outs.append(jax.ShapeDtypeStruct((outer, inner, rows, columns), BRAIN))
            out_specs.append(
                pl.BlockSpec(
                    block + (rows, columns), lambda g, m, per=per: (g // per, g % per, 0, 0)
                )
            )
    if joined:
        whole_columns = sum(o.shape[-1] for o in outs) // 2
        shape = outs[0].shape[:-1] + (whole_columns,)
        outs = [jax.ShapeDtypeStruct(shape, BRAIN)] * 2
        spec = pl.BlockSpec(
            out_specs[0].block_shape[:-1] + (whole_columns,), out_specs[0].index_map
        )
        out_specs = [spec] * 2
    res = pl.pallas_call(
        functools.partial(merge_kernel, len(parts), joined),
        grid_spec=pltpu.PrefetchScalarGridSpec(
            num_scalar_prefetch=1, grid=(steps,), in_specs=in_specs, out_specs=out_specs
        ),
        out_shape=outs,
        compiler_params=pltpu.CompilerParams(vmem_limit_bytes=VMEM_BYTES),
        cost_estimate=pl.CostEstimate(flops=1 << 22, bytes_accessed=8 << 20, transcendentals=0),
        name="merge",
    )(mine, *ins)
    flat = [r.reshape((-1,) + r.shape[2:]) for r in res]
    return [(flat[2 * n], flat[2 * n + 1]) for n in range(len(flat) // 2)]


def split_portions(parts, joined):
    arrays, at = [[], [], []], 0
    for portion in parts:
        for array, _, count in portion.spans:
            arrays[array].append(joined[:, at : at + count])
            at += count
    return [jnp.concatenate(a, axis=1) for a in arrays]


def weights_end_kernel(parts, cols, *refs):
    keep_ref, come_ref, expand_ref, reduce_ref, output_ref, vectors_ref, bias_ref = refs
    joined = keep_ref[0].astype(FLOAT) + come_ref[0].astype(FLOAT)
    expand, reduce, output = split_portions(parts, joined)
    expand_ref[...] = expand
    reduce_ref[...] = reduce
    output = output.T
    output_ref[...] = output[:cols]
    lines = output[cols:]
    share = joined.shape[0]
    for c in range(SLOTS // 8):
        at = slice(c * share, (c + 1) * share)
        vectors_ref[:, at] = lines[8 * c : 8 * c + 6]
        bias_ref[:, at] = lines[8 * c : 8 * c + 8]


def weights_end(parts, keep, come, hidden, cols, width):
    share = keep.shape[1]
    shapes = [(share, hidden), (share, hidden), (cols, share), (6, width), (8, width)]
    return pl.pallas_call(
        functools.partial(weights_end_kernel, parts, cols),
        out_shape=[jax.ShapeDtypeStruct(shape, FLOAT) for shape in shapes],
        cost_estimate=pl.CostEstimate(flops=1 << 18, bytes_accessed=1 << 20, transcendentals=0),
        name="weights_end",
    )(keep, come)


def project_end_kernel(riding, keep_ref, come_ref, out_ref, bias_ref):
    heads, share, _ = keep_ref.shape
    for h in range(heads):
        value = keep_ref[h].astype(FLOAT) + come_ref[h].astype(FLOAT)
        own = slice(h * HEAD_DIM, (h + 1) * HEAD_DIM)
        for i, at in enumerate((LANES + HEAD_DIM, HEAD_DIM, 0)):
            out_ref[i, :, own] = value[:, at : at + HEAD_DIM]
        free = value[:, LANES:]
        if riding:
            lines = free.T
            spread = 3 * HEAD_DIM // share
            line = jnp.concatenate([lines[n : n + 1] for n in range(spread)], axis=1)
            bias_ref[0:1, own] = line[:, 2 * HEAD_DIM :]
            bias_ref[1:2, own] = line[:, :HEAD_DIM]
        else:
            bias_ref[h] = free[:, :HEAD_DIM]


def project_end(keep, come, riding):
    heads, share, _ = keep.shape
    cols = heads * HEAD_DIM
    bias_shape = (2, cols) if riding else (heads, share, HEAD_DIM)
    return pl.pallas_call(
        functools.partial(project_end_kernel, riding),
        out_shape=[
            jax.ShapeDtypeStruct((3, share, cols), FLOAT),
            jax.ShapeDtypeStruct(bias_shape, FLOAT),
        ],
        cost_estimate=pl.CostEstimate(flops=1 << 18, bytes_accessed=1 << 20, transcendentals=0),
        name="project_end",
    )(keep, come)


def fence(*values):
    return lax.optimization_barrier(values)


def tie(first, second):
    return fence(first, second)[0]


def body(
    frames,
    segment_ids,
    project_weight,
    query_value_bias,
    output_weight,
    output_bias,
    first_gain,
    first_shift,
    expand_weight,
    expand_bias,
    reduce_weight,
    reduce_bias,
    second_gain,
    second_shift,
    cotangent,
    *,
    groups,
):
    rows, width = frames.shape
    cols = project_weight.shape[2]
    hidden = expand_weight.shape[1]
    heads = cols // HEAD_DIM
    length = 4 * rows
    me = lax.axis_index("tensor")
    half = lax.axis_index("dp") % 2
    half_two = (lax.axis_index("dp") // 2) % 2
    other = functools.partial(swap, axis="tensor", size=4)

    far = other(frames, bits=2)
    near = other(frames, bits=1)

    blocks = segment_ids.reshape(4, rows)
    segs = jnp.concatenate([lax.dynamic_index_in_dim(blocks, me ^ k, 0) for k in range(4)], axis=1)
    vectors = jnp.stack(
        [output_bias, first_gain, first_shift, reduce_bias, second_gain, second_shift]
    ).astype(FLOAT)
    vectors = jnp.pad(vectors, ((0, 2), (0, 0)))
    bias = query_value_bias.astype(FLOAT).reshape(2, heads, HEAD_DIM)
    bias = jnp.stack(
        [
            jnp.pad(bias[0], ((0, 0), (HEAD_DIM, 0))).reshape(-1),
            jnp.pad(bias[1], ((0, 0), (0, HEAD_DIM))).reshape(-1),
        ]
    )
    wide_halves = jnp.concatenate(
        [
            expand_weight.T.reshape(2, hidden // 2, width),
            output_weight.reshape(2, cols // 2, width),
            jnp.broadcast_to(
                jnp.pad(expand_bias[None], ((0, 15), (0, width - hidden))), (2, 16, width)
            ),
        ],
        axis=1,
    )
    wide = wide_halves.reshape(-1, width)
    wide_half = lax.dynamic_index_in_dim(wide_halves, half, 0, False)
    back_half = lax.dynamic_index_in_dim(
        reduce_weight.reshape(2, hidden // 2, width), half_two, 0, False
    )
    *started, spread_weight = project(0, (frames, near), project_weight, bias, segs, ())

    far, started, wide_half, back_half, wide_later, back_later = fence(
        far, started, wide_half, back_half, wide, reduce_weight
    )
    near_wide = other(wide_later, bits=1)
    near_back = other(back_later, bits=1)
    last = other(far, bits=1)

    got_wide = other(wide_half, bits=2)
    got_back = other(back_half, bits=2)
    qt, ka, vt, qz, kt, va, xt = project(
        2, (far, last), spread_weight, bias, segs, started
    )
    far_blocks = attend(qt, ka, vt, rows, 2, 2, False)
    far_blocks, got_wide, got_back, near_wide, near_back, qt_later = fence(
        far_blocks, got_wide, got_back, near_wide, near_back, qt
    )
    relayed = swap(got_wide, "dp", groups, 1)
    relayed_back = swap(got_back, "dp", groups, 2)
    far_mixed = other(far_blocks[0][0], bits=2)
    last_wide = other(got_wide, bits=1)
    last_back = other(got_back, bits=1)
    near_blocks = attend(qt_later, ka, vt, rows, 0, 2, True)
    near_blocks, relayed, relayed_back, far_mixed, last_wide, last_back = fence(
        near_blocks, relayed, relayed_back, far_mixed, last_wide, last_back
    )
    near_mixed = other(near_blocks[0][1], bits=1)
    last_mixed = other(far_mixed[1:], bits=1)
    mixed = [near_blocks[0][0], near_mixed, far_mixed, last_mixed]

    riding = groups * 8 == SLOTS and 2 * LANES - cols == SLOTS and (width // groups) % 16 == 0
    outs = layer(
        jnp.stack([half, half_two]).astype(jnp.int32),
        mixed,
        frames,
        cotangent,
        vectors,
        (wide, near_wide, got_wide, relayed, last_wide, other(relayed, bits=1)),
        (reduce_weight, near_back, got_back, relayed_back, last_back, other(relayed_back, bits=1)),
        riding,
    )
    layer_out, grad_first = outs[:2]
    own_grad, near_grad, far_grad, small = outs[2:6]
    keeps, sends = outs[6:9], outs[9:12]
    far_grad = other(far_grad, bits=2)
    near_grad = other(near_grad, bits=1)

    bits = [2**n for n in reversed(range(groups.bit_length() - 1))]
    share = width // groups
    steps = [0] + bits[::-1]
    orders = [steps[n:3] + steps[:n] for n in range(3)]
    arrived = [other(send, bits=1) for send in sends]
    forms = (qt, ka, qz, kt, va, xt)
    exacts = [near_blocks[1], far_blocks[1]]
    logs = [near_blocks[2], far_blocks[2]]
    begun, query = attend_back_own(forms, own_grad, exacts[0], logs[0])
    arrived, begun, far_grad, near_grad = fence(arrived, begun, far_grad, near_grad)
    grad_heads = [near_grad, far_grad, other(far_grad[1:], bits=1)]
    mine = jnp.stack([jnp.zeros_like(half)] + [(lax.axis_index("dp") // b) % 2 for b in bits])
    mine = mine.astype(jnp.int32)
    axes = [0] + bits
    left = [list(axes) for _ in orders]
    values = [
        (keep.reshape(2 * groups, share, -1), come.reshape(2 * groups, share, -1))
        for keep, come in zip(keeps, arrived)
    ]

    def divide(values, chosen, steps, joined=False):
        parts = []
        for n, ((keep, come), axis) in enumerate(zip(values, chosen)):
            at = left[n].index(axis)
            parts.append((keep, come, 2**at, 2 ** (len(left[n]) - at - 1)))
            left[n] = [b for b in left[n] if b != axis]
        return merge(mine, parts, [axes.index(axis) for axis in chosen], steps, joined)

    def go(value, axis):
        return other(value, bits=2) if axis == 0 else swap(value, "dp", groups, axis)

    def sent_half(value, axis):
        count, lead = value.shape[:2]
        at = tail_left.index(axis)
        view = value.reshape((count, 2**at, 2, lead // 2 ** (at + 1)) + value.shape[2:])
        bit = (lax.axis_index("dp") // axis) % 2
        shape = (count, lead // 2) + value.shape[2:]
        keep_ = lax.dynamic_index_in_dim(view, bit, 2, keepdims=False).reshape(shape)
        send = lax.dynamic_index_in_dim(view, 1 - bit, 2, keepdims=False).reshape(shape)
        return keep_, swap(send, "dp", groups, axis)

    def added(pair):
        return (pair[0].astype(FLOAT) + pair[1].astype(FLOAT)).astype(BRAIN)

    def phase(values, number, steps):
        order = [o[number] for o in orders]
        halves = divide(values, order, steps)
        return [(half_[0], go(half_[1], axis)) for half_, axis in zip(halves, order)]

    def keeps_of(values):
        return [value[0] for value in values]

    tail_left = list(bits)
    values = phase(values, 0, 4)
    begun = tie(begun, keeps_of(values))
    head_args = (share, forms, grad_heads, exacts, logs)
    most = attend_back(0, heads - 1, *head_args, begun, query)
    most, values = fence(most, values)

    values = phase(values, 1, 2)
    begun = tie(begun, keeps_of(values))
    final = attend_back(heads - 1, 1, *head_args, begun, query)
    final, values = fence(final, values)

    pair = sent_half(jnp.concatenate([most[1], final[1]]), 1)
    tail_left.remove(1)
    values = tie(values, pair[0])
    values = phase(values, 2, 1)
    most_rows, final_rows, grad_first = tie(
        (most[0], final[0], grad_first), keeps_of(values)
    )
    sums = frames_back(most_rows, final_rows, spread_weight, grad_first)
    (sent, own_sum, far_sum), values, pair = fence(sums, values, pair)
    got = other(sent, bits=1)
    tail = added(pair)
    for axis in bits[::-1][1:-1]:
        pair = sent_half(tail, axis)
        tail_left.remove(axis)
        if axis != bits[1]:
            tail = added(pair)
    far_sum, got = tie((far_sum, got), pair[0])
    far_sum = (far_sum + got[1].astype(FLOAT)).astype(BRAIN)
    far_got = other(far_sum, bits=2)
    values = tie(values, far_sum)
    rest = steps[3:]
    while len(rest) > 1:
        values = [
            (half_[0], go(half_[1], rest[0])) for half_ in divide(values, [rest[0]] * 3, 1)
        ]
        rest = rest[1:]
    ((kept, going),) = divide(values, [rest[0]] * 3, 1, True)
    kept, going, pair = fence(kept, going, pair)
    come = go(going, rest[0])
    tail_keep, tail_come = sent_half(added(pair), rest[0])
    frames_grad = own_sum + got[0].astype(FLOAT) + far_got.astype(FLOAT)
    kept, come, frames_grad = fence(kept, come, frames_grad)

    parts = portions(width, hidden)
    if riding:
        expand_grad, reduce_grad, output_grad, vector_grads, expand_bias_grad = weights_end(
            parts, kept, come, hidden, cols, width
        )
        expand_bias_grad = expand_bias_grad[6, :hidden]
    else:
        joined = (kept.astype(FLOAT) + come.astype(FLOAT))[0]
        expand_grad, reduce_grad, output_grad = split_portions(parts, joined)
        output_grad = output_grad[:, :cols].T
        everyone = lax.all_gather(small, ("dp", "tensor")).reshape(groups, 4, 16, width)
        vector_grads = jnp.sum(everyone[:, :, :6], axis=(0, 1))
        picked = [
            lax.dynamic_index_in_dim(everyone[:, s], 8 + (me ^ s), 1, False) for s in range(4)
        ]
        expand_bias_grad = sum(jnp.sum(p, axis=0) for p in picked)

    reduce_grad = reduce_grad.T
    project_grad, attend_bias_grad = project_end(tail_keep[:, 0], tail_come[:, 0], riding)
    if not riding:
        spread = 3 * HEAD_DIM // share
        bias_sums = jnp.swapaxes(attend_bias_grad[:, :, :spread], 1, 2)
        bias_sums = bias_sums.reshape(heads, 3, HEAD_DIM)
        attend_bias_grad = jnp.stack([bias_sums[:, i].reshape(cols) for i in (2, 0)])
    return (
        layer_out,
        frames_grad,
        project_grad,
        attend_bias_grad,
        output_grad,
        expand_grad,
        expand_bias_grad,
        reduce_grad,
        vector_grads,
    )


def solution(mesh):
    placed = (
        P(("dp", "tensor"), None),
        P("dp", None),
        P(None, None, "tensor"),
        P(None, "tensor"),
        P("tensor", None),
        P(),
        P(),
        P(),
        P(None, "tensor"),
        P("tensor"),
        P("tensor", None),
        P(),
        P(),
        P(),
        P(("dp", "tensor"), None),
    )
    return jax.shard_map(
        functools.partial(body, groups=mesh.shape["dp"]),
        mesh=mesh,
        in_specs=placed,
        out_specs=(
            P(("dp", "tensor"), None),
            P(("dp", "tensor"), None),
            P(None, "dp", "tensor"),
            P(None, "tensor"),
            P("tensor", "dp"),
            P("dp", "tensor"),
            P("tensor"),
            P("tensor", "dp"),
            P(),
        ),
        check_vma=False,
    )
```

```python
import functools

import jax
import jax.numpy as jnp
import numpy as np
from jax import lax
from jax.experimental import pallas as pl
from jax.experimental.pallas import tpu as pltpu
from jax.sharding import PartitionSpec as P

HEAD_DIM = 64
ROW_LEN = 2048
EPS = 1e-05
FLOAT = jnp.float32
BRAIN = jnp.bfloat16
BIG = 1e30
SCALE = HEAD_DIM ** (-0.5)
VMEM_BYTES = 60 << 20
IDS = 8
LANES = 128
CHUNK = 1024
BACK_CHUNK = 512
SLOTS = 64

NN = (((1,), (0,)), ((), ()))
NT = (((1,), (1,)), ((), ()))


def dot(left, right, dims=NN):
    return lax.dot_general(left, right, dims, preferred_element_type=FLOAT)


def swap(value, axis, size, bits):
    return lax.ppermute(value, axis, [(i, i ^ bits) for i in range(size)])


def whole(shape):
    return pl.BlockSpec(shape, lambda *_: (0,) * len(shape), pipeline_mode=pl.Buffered(1))


def split_three(value):
    top = value.astype(BRAIN).astype(FLOAT)
    rest = value - top
    middle = rest.astype(BRAIN).astype(FLOAT)
    return top, middle, rest - middle


def project_kernel(heads, rows, first, where_ref, *refs):
    x_refs = refs[:2]
    w_ref, bias_ref, segs_ref = refs[2:5]
    if first:
        held = refs[-1]
        spread = refs[-2]
        forms = refs[-9:-2]
    else:
        held = refs[-1]
        spread = w_ref
        forms = refs[-8:-1]
    qt_ref, ka_ref, vt_ref, qz_ref, kt_ref, va_ref, xt_ref = forms
    step = pl.program_id(0)
    for k in range(2):

        @pl.when(step == k)
        def _():
            held[...] = x_refs[k][...]

    if first:

        @pl.when(step == 0)
        def _():
            nothing = jnp.zeros((w_ref.shape[1], HEAD_DIM), BRAIN)
            for i in range(3):
                for h in range(heads):
                    own = w_ref[i, :, h * HEAD_DIM : (h + 1) * HEAD_DIM]
                    pair = [own, nothing] if i == 2 else [nothing, own]
                    spread[i, :, h * LANES : (h + 1) * LANES] = jnp.concatenate(pair, axis=1)

    x = held[...]
    xt_ref[...] = x.T
    segs = segs_ref[...].astype(FLOAT)
    number = lax.broadcasted_iota(jnp.int32, (HEAD_DIM, rows), 0).astype(FLOAT)
    qtail = jnp.where(jnp.broadcast_to(segs, (HEAD_DIM, rows)) == number, 1.0, 0.0).astype(BRAIN)
    lane = lax.broadcasted_iota(jnp.int32, (rows, LANES), 1)
    differ = jnp.broadcast_to(segs, (LANES, rows)).T != lane.astype(FLOAT)
    ktail = jnp.where(lane < IDS, jnp.where(differ, -BIG, 0.0), jnp.where(lane < IDS + 3, -1.0, 0.0))
    minus = jnp.where((lane >= HEAD_DIM) & (lane < HEAD_DIM + 3), -1.0, 0.0)
    query = (dot(x, spread[0]) + bias_ref[0:1]).astype(BRAIN).astype(FLOAT) * SCALE
    key = dot(x, spread[1])
    value = dot(x, spread[2]) + bias_ref[1:2]
    for h in range(heads):
        own = slice(h * LANES, (h + 1) * LANES)
        q, k_, v = query[:, own], key[:, own], value[:, own]
        qt_ref[h, :HEAD_DIM, :] = qtail
        qt_ref[h, HEAD_DIM:, :] = q.T[HEAD_DIM:].astype(BRAIN)
        kt_ref[h] = k_.T.astype(BRAIN)
        vt_ref[h] = v.T[:HEAD_DIM].astype(BRAIN)
        ka_ref[h] = (k_ + ktail).astype(BRAIN)
        va_ref[h] = (v + minus).astype(BRAIN)
        qz_ref[h, :HEAD_DIM, :] = jnp.zeros((HEAD_DIM, rows), BRAIN)
        qz_ref[h, HEAD_DIM:, :] = qt_ref[h, HEAD_DIM:, :]


def project(where, first, pieces, weight, bias, segs, before):
    rows, width = pieces[0].shape
    heads = bias.shape[1] // LANES
    length = 4 * rows
    by_lane = lambda i, m: (0, 0, first + i)
    by_row = lambda i, m: (0, first + i, 0)
    shapes = [
        ((heads, LANES, length), (heads, LANES, rows), by_lane),
        ((heads, length, LANES), (heads, rows, LANES), by_row),
        ((heads, HEAD_DIM, length), (heads, HEAD_DIM, rows), by_lane),
        ((heads, LANES, length), (heads, LANES, rows), by_lane),
        ((heads, LANES, length), (heads, LANES, rows), by_lane),
        ((heads, length, LANES), (heads, rows, LANES), by_row),
        ((width, length), (width, rows), lambda i, m: (0, first + i)),
    ]
    out_specs = [pl.BlockSpec(block, index) for _, block, index in shapes]
    if not before:
        shapes.append(((3, width, heads * LANES), None, None))
        out_specs.append(whole(shapes[-1][0]))
    return pl.pallas_call(
        functools.partial(project_kernel, heads, rows, not before),
        grid_spec=pltpu.PrefetchScalarGridSpec(
            num_scalar_prefetch=1,
            grid=(2,),
            in_specs=[
                whole((rows, width)),
                whole((rows, width)),
                whole(weight.shape),
                whole(bias.shape),
                pl.BlockSpec((1, rows), lambda i, m: (0, m[0] ^ (first + i))),
            ]
            + [pl.BlockSpec(memory_space=pl.ANY)] * len(before),
            out_specs=out_specs,
            scratch_shapes=[pltpu.VMEM((rows, width), BRAIN)],
        ),
        out_shape=[jax.ShapeDtypeStruct(s[0], BRAIN) for s in shapes],
        input_output_aliases={6 + n: n for n in range(len(before))},
        compiler_params=pltpu.CompilerParams(vmem_limit_bytes=VMEM_BYTES),
        cost_estimate=pl.CostEstimate(
            flops=12 * rows * width * heads * LANES, bytes_accessed=8 << 20, transcendentals=0
        ),
        name="project",
    )(where, *pieces, weight, bias, segs, *before)


def attend_kernel(rows, count, *refs):
    qt_ref, ka_ref, vt_ref = refs[:3]
    out_refs, exact_ref, log_ref, held = refs[3:-3], refs[-3], refs[-2], refs[-1]
    length = ka_ref.shape[1]
    part, chunk = held.shape[2], min(CHUNK, length)
    chunks = [slice(at, at + chunk) for at in range(0, length, chunk)]
    items = [(n, at) for n in range(count) for at in range(0, rows, part)]

    def score(item, keys):
        n, at = items[item]
        first = n * rows + at
        scores = dot(ka_ref[0, keys], qt_ref[0, :, first : first + part])
        held[item % 2, keys] = scores
        return jnp.max(scores, axis=0, keepdims=True)

    highest = functools.reduce(jnp.maximum, [score(0, keys) for keys in chunks])
    for item, (n, at) in enumerate(items):
        tops, total, mixed = [], 0.0, 0.0
        for keys in chunks:
            if item + 1 < len(items):
                tops.append(score(item + 1, keys))
            raised = jnp.exp(held[item % 2, keys] - highest)
            total = total + jnp.sum(raised, axis=0, keepdims=True)
            mixed = mixed + dot(vt_ref[0, :, keys], raised.astype(BRAIN))
        mixed = mixed / total
        lanes = slice(at, at + part)
        if len(out_refs) == 1:
            out_refs[0][n, :, lanes] = mixed.astype(BRAIN)
        else:
            out_refs[n][0, :, lanes] = mixed.astype(BRAIN)
        exact_ref[n, :, lanes] = mixed
        log_ref[0, n : n + 1, lanes] = highest + jnp.log(total)
        if tops:
            highest = functools.reduce(jnp.maximum, tops)


def attend(qt, ka, vt, rows, first, count, parted):
    heads, _, length = qt.shape
    cols = heads * HEAD_DIM
    by_head = lambda h: (0, h, 0)
    sizes = [1] * count if parted else [count]
    outs = pl.pallas_call(
        functools.partial(attend_kernel, rows, count),
        grid=(heads,),
        in_specs=[
            pl.BlockSpec((1, LANES, count * rows), lambda h: (h, 0, first // count)),
            pl.BlockSpec((1, length, LANES), lambda h: (h, 0, 0)),
            pl.BlockSpec((1, HEAD_DIM, length), lambda h: (h, 0, 0)),
        ],
        out_specs=[pl.BlockSpec((n, HEAD_DIM, rows), by_head) for n in sizes]
        + [
            pl.BlockSpec((count, HEAD_DIM, rows), by_head),
            pl.BlockSpec((1, count, rows), lambda h: (h, 0, 0)),
        ],
        out_shape=[jax.ShapeDtypeStruct((n, cols, rows), BRAIN) for n in sizes]
        + [
            jax.ShapeDtypeStruct((count, cols, rows), FLOAT),
            jax.ShapeDtypeStruct((heads, count, rows), FLOAT),
        ],
        scratch_shapes=[pltpu.VMEM((2, length, rows // 2), FLOAT)],
        compiler_params=pltpu.CompilerParams(vmem_limit_bytes=VMEM_BYTES),
        cost_estimate=pl.CostEstimate(
            flops=8 * heads * length * count * rows * LANES,
            bytes_accessed=8 << 20,
            transcendentals=heads * length * count * rows,
        ),
        name="attend",
    )(qt, ka, vt)
    return outs[:-2], outs[-2], outs[-1]


def fill(slot, queries, grads, plain, qt, grad, exact, log):
    rows = queries.shape[2]
    low = lax.broadcasted_iota(jnp.int32, (8, rows), 0)

    def stacked(value):
        top, middle, bottom = split_three(value)
        return jnp.where(
            low == 0, top, jnp.where(low == 1, middle, jnp.where(low == 2, bottom, 0.0))
        )

    nothing = jnp.zeros((LANES - HEAD_DIM - 16, rows), BRAIN)
    delta = jnp.sum(grad.astype(FLOAT) * exact, axis=0, keepdims=True)
    ids = qt[:16].astype(FLOAT)[:IDS]
    queries[slot, :16] = jnp.concatenate([ids, stacked(log)], axis=0).astype(BRAIN)
    queries[slot, 16:] = qt[16:]
    grads[slot, :HEAD_DIM] = grad
    grads[slot, HEAD_DIM : HEAD_DIM + 16] = jnp.concatenate(
        [stacked(delta), jnp.zeros((8, rows), FLOAT)], axis=0
    ).astype(BRAIN)
    grads[slot, HEAD_DIM + 16 :] = nothing
    plain[slot, :HEAD_DIM] = grad
    plain[slot, HEAD_DIM:] = jnp.zeros((LANES - HEAD_DIM, rows), BRAIN)


def back_block(slot, queries, grads, plain, qz, ka_ref, kt_ref, va_ref, add):
    length = ka_ref.shape[1]
    chunk = min(BACK_CHUNK, length)
    grad_query = 0.0
    for at in range(0, length, chunk):
        keys = slice(at, at + chunk)
        probs = jnp.exp(dot(ka_ref[0, keys], queries[slot]))
        grad_scores = (probs * dot(va_ref[0, keys], grads[slot])).astype(BRAIN)
        add(keys, dot(probs.astype(BRAIN), plain[slot], NT) + dot(grad_scores, qz, NT))
        grad_query = grad_query + dot(kt_ref[0, :, keys], grad_scores)
    return (grad_query * SCALE).T.astype(BRAIN)


def attend_back_own_kernel(*refs):
    qt_ref, ka_ref, qz_ref, kt_ref, va_ref = refs[:5]
    grad_ref, exact_ref, log_ref = refs[5:8]
    total_ref, query_ref = refs[8:10]
    scratch = refs[10:]
    fill(0, *scratch, qt_ref[0], grad_ref[0], exact_ref[0], log_ref[0, 0:1])

    def add(keys, value):
        total_ref[0, keys] = value

    query_ref[0] = back_block(0, *scratch, qz_ref[0], ka_ref, kt_ref, va_ref, add)


def attend_back_own(forms, grad, exact, log):
    qt, ka, qz, kt, va, _ = forms
    heads, length = ka.shape[:2]
    rows = length // 4
    by_head = lambda h: (h, 0, 0)
    return pl.pallas_call(
        attend_back_own_kernel,
        grid=(heads,),
        in_specs=[
            pl.BlockSpec((1, LANES, rows), by_head),
            pl.BlockSpec((1, length, LANES), by_head),
            pl.BlockSpec((1, LANES, rows), by_head),
            pl.BlockSpec((1, LANES, length), by_head),
            pl.BlockSpec((1, length, LANES), by_head),
            pl.BlockSpec((1, HEAD_DIM, rows), lambda h: (0, h, 0)),
            pl.BlockSpec((1, HEAD_DIM, rows), lambda h: (0, h, 0)),
            pl.BlockSpec((1, 2, rows), by_head),
        ],
        out_specs=[
            pl.BlockSpec((1, length, LANES), by_head),
            pl.BlockSpec((1, rows, LANES), by_head),
        ],
        out_shape=[
            jax.ShapeDtypeStruct((heads, length, LANES), FLOAT),
            jax.ShapeDtypeStruct((heads, rows, LANES), BRAIN),
        ],
        scratch_shapes=[pltpu.VMEM((1, LANES, rows), BRAIN)] * 3,
        compiler_params=pltpu.CompilerParams(vmem_limit_bytes=VMEM_BYTES),
        cost_estimate=pl.CostEstimate(
            flops=18 * length * length * LANES,
            bytes_accessed=8 << 20,
            transcendentals=length * length,
        ),
        name="attend_back_own",
    )(qt, ka, qz, kt, va, grad, exact, log)


def attend_back_kernel(rows, first, share, *refs):
    qt_ref, ka_ref, qz_ref, kt_ref, va_ref, xt_ref = refs[:6]
    grad_refs, exacts, logs = refs[6:9], refs[9:12], refs[12:14]
    begun_ref, query_ref = refs[14:16]
    out_ref, project_ref = refs[16:18]
    total, begun, xt = refs[18:21]
    scratch = refs[21:24]
    sem = refs[24]
    step = pl.program_id(0)
    begun_copy = pltpu.make_async_copy(begun_ref.at[first + step], begun, sem.at[0])
    xt_copy = pltpu.make_async_copy(xt_ref, xt, sem.at[1])
    begun_copy.start()
    pl.when(step == 0)(xt_copy.start)
    for k in range(3):
        at = pl.ds((k + 1) * rows, rows)
        log = logs[(k + 1) // 2][0, (k + 1) % 2 : (k + 1) % 2 + 1]
        fill(k, *scratch, qt_ref[0, :, at], grad_refs[k][0], exacts[k][0], log)
    out_ref[0, :rows, LANES:] = query_ref[0]
    for k in range(3):

        def add(keys, value):
            if k == 0:
                total[keys] = value
            else:
                total[keys] += value

        at = pl.ds((k + 1) * rows, rows)
        qz = qz_ref[0, :, at]
        out_ref[0, at, LANES:] = back_block(k, *scratch, qz, ka_ref, kt_ref, va_ref, add)
    begun_copy.wait()
    pl.when(step == 0)(xt_copy.wait)
    out_ref[0, :, :LANES] = (total[...] + begun[...]).astype(BRAIN)
    pieces = out_ref[0]
    project_ref[0] = dot(xt[...], pieces).astype(BRAIN)
    bias = jnp.sum(pieces.astype(FLOAT), axis=0, keepdims=True)
    if share % 16 == 0:
        bias = jnp.concatenate([bias[:, :LANES], bias[:, LANES + HEAD_DIM :]], axis=1)
        spread = 3 * HEAD_DIM // share
        line = jnp.concatenate(
            [bias[:, n * share : (n + 1) * share] for n in range(spread)]
            + [jnp.zeros((8 - spread, share), FLOAT)],
            axis=0,
        ).T.astype(BRAIN)
        for at in range(0, project_ref.shape[1], share):
            project_ref[0, at : at + share, LANES : LANES + 8] = line
    else:
        refs[25][0] = bias


def attend_back(first, count, share, forms, grads, exacts, logs, begun, query):
    qt, ka, qz, kt, va, xt = forms
    length, width = ka.shape[1], xt.shape[0]
    rows = length // 4
    cols = 2 * LANES
    own = lambda i: (first + i, 0, 0)
    by_block = lambda n: pl.BlockSpec((1, HEAD_DIM, rows), lambda i: (n, first + i, 0))
    each = lambda i: (i, 0, 0)
    out_specs = [pl.BlockSpec((1, length, cols), each), pl.BlockSpec((1, width, cols), each)]
    out_shape = [
        jax.ShapeDtypeStruct((count, length, cols), BRAIN),
        jax.ShapeDtypeStruct((count, width, cols), BRAIN),
    ]
    scratch = (
        [
            pltpu.VMEM((length, LANES), FLOAT),
            pltpu.VMEM((length, LANES), FLOAT),
            pltpu.VMEM((width, length), BRAIN),
        ]
        + [pltpu.VMEM((3, LANES, rows), BRAIN)] * 3
        + [pltpu.SemaphoreType.DMA((2,))]
    )
    kernel = functools.partial(attend_back_kernel, rows, first, share)
    if share % 16:
        out_specs.append(pl.BlockSpec((1, 1, cols), each))
        out_shape.append(jax.ShapeDtypeStruct((count, 1, cols), FLOAT))
        kernel = lambda *refs: attend_back_kernel(
            rows, first, share, *refs[:18], *refs[19:], refs[18]
        )
    res = pl.pallas_call(
        kernel,
        grid=(count,),
        in_specs=[
            pl.BlockSpec((1, LANES, length), own),
            pl.BlockSpec((1, length, LANES), own),
            pl.BlockSpec((1, LANES, length), own),
            pl.BlockSpec((1, LANES, length), own),
            pl.BlockSpec((1, length, LANES), own),
            pl.BlockSpec(memory_space=pl.ANY),
        ]
        + [by_block(0)] * 3
        + [by_block(1), by_block(0), by_block(1)]
        + [pl.BlockSpec((1, 2, rows), own)] * 2
        + [pl.BlockSpec(memory_space=pl.ANY), pl.BlockSpec((1, rows, LANES), own)],
        out_specs=out_specs,
        out_shape=out_shape,
        scratch_shapes=scratch,
        compiler_params=pltpu.CompilerParams(vmem_limit_bytes=VMEM_BYTES),
        cost_estimate=pl.CostEstimate(
            flops=20 * count * length * length * LANES,
            bytes_accessed=8 << 20,
            transcendentals=count * length * length,
        ),
        name="attend_back",
    )(qt, ka, qz, kt, va, xt, *grads, exacts[0], exacts[1], exacts[1], *logs, begun, query)
    project_grad = res[1].reshape(count, width // share, share, cols)
    if share % 16:
        spread = 3 * HEAD_DIM // share
        bias = jnp.concatenate([res[2][..., :LANES], res[2][..., LANES + HEAD_DIM :]], axis=2)
        bias = jnp.swapaxes(bias.reshape(count, 1, spread, share), 2, 3).astype(BRAIN)
        bias = jnp.broadcast_to(bias, (count, width // share, share, spread))
        project_grad = jnp.concatenate(
            [
                project_grad[..., :LANES],
                bias,
                project_grad[..., LANES + spread :],
            ],
            axis=3,
        )
    return res[0], project_grad


def gelu_parts(values):
    t = 1.0 / (1.0 + (0.3275911 * 0.7071067811865476) * jnp.abs(values))
    bell = jnp.exp(-0.5 * values * values)
    poly = 0.5 * 1.061405429
    for c in (-1.453152027, 1.421413741, -0.284496736, 0.254829592):
        poly = poly * t + 0.5 * c
    tail = poly * t * bell
    below = jnp.where(values >= 0, 1.0 - tail, tail)
    return values * below, below + values * bell * 0.3989422804014327


def mean_of(values):
    return jnp.mean(values, axis=-1, keepdims=True)


class Portion:
    def __init__(self, *spans):
        self.spans = spans
        self.columns = sum(span[2] for span in spans)


def portions(width, hidden):
    if hidden == 6 * LANES:
        return (
            Portion((0, 0, 4 * LANES)),
            Portion((0, 4 * LANES, 2 * LANES), (1, 0, 3 * LANES)),
            Portion((1, 3 * LANES, 3 * LANES), (2, 0, 2 * LANES)),
        )
    return (Portion((0, 0, hidden)), Portion((1, 0, hidden)), Portion((2, 0, 2 * LANES)))


def layer_kernel(parts, hidden, riding, *refs):
    t_ref = refs[0]
    mixed = refs[1:5]
    x_ref, cot_ref, vec_ref = refs[5:8]
    wide_refs, back_refs = refs[8:14], refs[14:20]
    out_ref, grad_first_ref = refs[20:22]
    d_refs = (refs[22].at[0], refs[23].at[0], refs[24].at[0], refs[24].at[1])
    small_ref = refs[25]
    keeps, sends = refs[26:29], refs[29:32]
    wet, wo, eb, back, orow, act, slope, dz, stage, tail_stage = refs[32:42]
    wide_sem, back_sem, out_sem = refs[42:]
    half, back_half = t_ref[1], t_ref[2]
    width = x_ref.shape[1]
    part = mixed[0].shape[1]
    bias_out, gain_one, shift_one, bias_red, gain_two, shift_two = (
        vec_ref[i : i + 1] for i in range(6)
    )

    split = hidden // 2 + part // 2 + 16

    def load_wide(k, n):
        if k < 2:
            source, first, which = wide_refs[k], n * split, n
        else:
            source, first, which = wide_refs[2 * k - 2 + n], 0, (half, 1 - half)[n]
        found = []
        for m, (at, count, target, to) in enumerate(
            [
                (0, hidden // 2, wet, k * hidden + which * (hidden // 2)),
                (hidden // 2, part // 2, wo, k * part + which * (part // 2)),
                (hidden // 2 + part // 2, 16, eb.at[k], which * 16),
            ]
        ):
            to = to if isinstance(to, int) else pl.multiple_of(to, 16)
            found.append(
                pltpu.make_async_copy(
                    source.at[pl.ds(first + at, count)],
                    target.at[pl.ds(to, count)],
                    wide_sem.at[k, n, m],
                )
            )
        return found

    loads = [[load_wide(k, n) for n in range(2)] for k in range(4)]
    def load_back(k, n):
        if k < 2:
            source, first, which = back_refs[k], n * (hidden // 2), n
        else:
            source, first, which = back_refs[2 * k - 2 + n], 0, (back_half, 1 - back_half)[n]
        to = k * hidden + which * (hidden // 2)
        to = to if isinstance(to, int) else pl.multiple_of(to, 16)
        return pltpu.make_async_copy(
            source.at[pl.ds(first, hidden // 2)],
            back.at[pl.ds(to, hidden // 2)],
            back_sem.at[k, n],
        )

    back_loads = [load_back(k, n) for k in range(4) for n in range(2)]

    def each(kind, k=None):
        return [c[kind] for pair in (loads if k is None else [loads[k]]) for c in pair]

    for copy in each(1):
        copy.start()
    for k in range(4):
        for copy in each(0, k) + each(2, k):
            copy.start()
    for k, ref in enumerate(mixed):
        orow[:, k * part : (k + 1) * part] = ref[0].astype(FLOAT).T.astype(BRAIN)
    for copy in each(1):
        copy.wait()
    for copy in back_loads:
        copy.start()
    total = x_ref[...].astype(FLOAT) + bias_out + dot(orow[...], wo[...])
    center = total - mean_of(total)
    inverse_one = lax.rsqrt(mean_of(center * center) + EPS)
    unit_one = center * inverse_one
    normed = unit_one * gain_one + shift_one
    hb = normed.astype(BRAIN)
    hbt = normed.T.astype(BRAIN)

    owns = [slice(j * hidden, (j + 1) * hidden) for j in range(4)]
    for copy in each(0) + each(2):
        copy.wait()
    inner = dot(hb, wet[owns[0]], NT)
    for j in range(4):
        now = inner + eb[j, :16].astype(FLOAT)[:1]
        if j < 3:
            inner = dot(hb, wet[owns[j + 1]], NT)
        active, derivative = gelu_parts(now)
        act[:, owns[j]] = active.astype(BRAIN)
        slope[:, owns[j]] = derivative
    for copy in back_loads:
        copy.wait()
    total = normed + dot(act[...], back[...]) + bias_red
    center = total - mean_of(total)
    inverse = lax.rsqrt(mean_of(center * center) + EPS)
    unit = center * inverse
    out_ref[...] = (unit * gain_two + shift_two).astype(BRAIN)
    cot = cot_ref[...].astype(FLOAT)
    scaled = cot * gain_two
    grad = inverse * (scaled - mean_of(scaled) - unit * mean_of(scaled * unit))
    small_ref[3:4] = jnp.sum(grad, axis=0, keepdims=True)
    small_ref[4:5] = jnp.sum(cot * unit, axis=0, keepdims=True)
    small_ref[5:6] = jnp.sum(cot, axis=0, keepdims=True)
    dfb = grad.astype(BRAIN)
    dfbt = grad.T.astype(BRAIN)

    def outgoing(block, array, first_sem):
        found = []
        for ref, portion in zip(keeps if block in (0, 2) else sends, parts):
            at = 0
            for held, first, count in portion.spans:
                if held == array:
                    source = tail_stage.at[block] if array == 2 else stage.at[block, array]
                    found.append(
                        pltpu.make_async_copy(
                            source.at[:, pl.ds(first, count)],
                            ref.at[block // 2, :, pl.ds(at, count)],
                            out_sem.at[block, first_sem + len(found)],
                        )
                    )
                at += count
        return found

    order = (1, 3, 0, 2)
    started = []
    for j in order:
        stage[j, 1] = dot(dfbt, act[:, owns[j]]).astype(BRAIN)
        copies = outgoing(j, 1, 2)
        for copy in copies:
            copy.start()
        started += copies
    grad_active = dot(dfb, back[owns[order[0]]], NT)
    for n, j in enumerate(order):
        now = grad_active
        if n < 3:
            grad_active = dot(dfb, back[owns[order[n + 1]]], NT)
        grad_inner = (now * slope[:, owns[j]]).astype(BRAIN)
        dz[:, owns[j]] = grad_inner
        small_ref[8 + j : 9 + j] = jnp.sum(grad_inner.astype(FLOAT), axis=0, keepdims=True)
        stage[j, 0] = dot(hbt, grad_inner).astype(BRAIN)
        copies = outgoing(j, 0, 0)
        for copy in copies:
            copy.start()
        started += copies
    grad = grad + dot(dz[...], wet[...])
    small_ref[1:2] = jnp.sum(grad * unit_one, axis=0, keepdims=True)
    small_ref[2:3] = jnp.sum(grad, axis=0, keepdims=True)
    scaled = grad * gain_one
    first = inverse_one * (scaled - mean_of(scaled) - unit_one * mean_of(scaled * unit_one))
    small_ref[0:1] = jnp.sum(first, axis=0, keepdims=True)
    small_ref[6:8] = jnp.zeros((2, width), FLOAT)
    small_ref[12:] = jnp.zeros((4, width), FLOAT)
    grad_first_ref[...] = first
    grad_mixed = dot(wo[...], first.astype(BRAIN), NT).astype(BRAIN)
    for k, ref in enumerate(d_refs):
        ref[...] = grad_mixed[k * part : (k + 1) * part]
    output_grad = dot(first.T.astype(BRAIN), orow[...]).astype(BRAIN)
    places = SLOTS // 8
    share = width // places
    sums = small_ref[...]
    for k in range(4):
        tail_stage[k, :, :part] = output_grad[:, k * part : (k + 1) * part]
        if riding:
            rows_k = jnp.concatenate([sums[:6], sums[8 + k : 9 + k], sums[6:7]], axis=0)
            lines = jnp.concatenate(
                [rows_k[:, c * share : (c + 1) * share] for c in range(places)], axis=0
            ).T.astype(BRAIN)
            tail_stage[k, :, part:] = jnp.concatenate([lines] * places, axis=0)
        else:
            tail_stage[k, :, part:] = jnp.zeros((width, 2 * LANES - part), BRAIN)
        copies = outgoing(k, 2, 4)
        for copy in copies:
            copy.start()
        started += copies
    for copy in started:
        copy.wait()


def layer(halves, mixed, frames, cotangent, vectors, wides, backs, riding):
    rows, width = frames.shape
    part = mixed[0].shape[1]
    hidden = backs[0].shape[0]
    parts = portions(width, hidden)
    grads = [jax.ShapeDtypeStruct((2, width, p.columns), BRAIN) for p in parts]
    grid_spec = pltpu.PrefetchScalarGridSpec(
        num_scalar_prefetch=1,
        grid=(1,),
        in_specs=[whole((1, part, rows))] * 4
        + [whole((rows, width)), whole((rows, width)), whole(vectors.shape)]
        + [pl.BlockSpec(memory_space=pl.ANY)] * 12,
        out_specs=[whole((rows, width)), whole((rows, width))]
        + [whole((n, part, rows)) for n in (1, 1, 2)]
        + [whole((16, width))]
        + [pl.BlockSpec(memory_space=pl.ANY)] * 6,
        scratch_shapes=[
            pltpu.VMEM((4 * hidden, width), BRAIN),
            pltpu.VMEM((4 * part, width), BRAIN),
            pltpu.VMEM((4, 32, width), BRAIN),
            pltpu.VMEM((4 * hidden, width), BRAIN),
            pltpu.VMEM((rows, width), BRAIN),
            pltpu.VMEM((rows, 4 * hidden), BRAIN),
            pltpu.VMEM((rows, 4 * hidden), FLOAT),
            pltpu.VMEM((rows, 4 * hidden), BRAIN),
            pltpu.VMEM((4, 2, width, hidden), BRAIN),
            pltpu.VMEM((4, width, 2 * LANES), BRAIN),
            pltpu.SemaphoreType.DMA((4, 2, 3)),
            pltpu.SemaphoreType.DMA((4, 2)),
            pltpu.SemaphoreType.DMA((4, 6)),
        ],
    )
    return pl.pallas_call(
        functools.partial(layer_kernel, parts, hidden, riding),
        grid_spec=grid_spec,
        out_shape=[
            jax.ShapeDtypeStruct((rows, width), BRAIN),
            jax.ShapeDtypeStruct((rows, width), FLOAT),
        ]
        + [jax.ShapeDtypeStruct((n, part, rows), BRAIN) for n in (1, 1, 2)]
        + [jax.ShapeDtypeStruct((16, width), FLOAT)]
        + grads
        + grads,
        compiler_params=pltpu.CompilerParams(vmem_limit_bytes=VMEM_BYTES),
        cost_estimate=pl.CostEstimate(
            flops=2 * rows * width * (24 * hidden + 3 * width),
            bytes_accessed=40 << 20,
            transcendentals=8 * rows * hidden,
        ),
        name="layer",
    )(halves, *mixed, frames, cotangent, vectors, *wides, *backs)


def frames_kernel(most_ref, last_ref, w_ref, base_ref, sent_ref, own_ref, far_ref, stack, weights):
    step = pl.program_id(0)
    heads = w_ref.shape[2] // LANES
    wide = 2 * LANES

    @pl.when(step == 0)
    def _():
        for h in range(heads):
            own = slice(h * LANES, (h + 1) * LANES)
            at = h * wide
            weights[:, at : at + LANES] = w_ref[1, :, own] + w_ref[2, :, own]
            weights[:, at + LANES : at + wide] = w_ref[0, :, own]

    for h in range(heads - 1):
        stack[:, h * wide : (h + 1) * wide] = most_ref[h]
    stack[:, (heads - 1) * wide :] = last_ref[0]
    value = dot(stack[...], weights[...], NT)

    @pl.when(step < 2)
    def _():
        sent_ref[0] = value.astype(BRAIN)

    @pl.when(step == 2)
    def _():
        own_ref[...] = base_ref[...] + value

    @pl.when(step == 3)
    def _():
        far_ref[...] = value


def frames_back(most, last, weight, base):
    heads = most.shape[0] + 1
    width = weight.shape[1]
    rows = most.shape[1] // 4
    cols = 2 * LANES
    block = lambda i: (0, jnp.where(i < 2, 2 * i + 1, 2 * i - 4), 0)
    return pl.pallas_call(
        frames_kernel,
        grid=(4,),
        in_specs=[
            pl.BlockSpec((heads - 1, rows, cols), block),
            pl.BlockSpec((1, rows, cols), block),
            whole(weight.shape),
            whole((rows, width)),
        ],
        out_specs=[
            pl.BlockSpec((1, rows, width), lambda i: (jnp.minimum(i, 1), 0, 0)),
            whole((rows, width)),
            whole((rows, width)),
        ],
        out_shape=[
            jax.ShapeDtypeStruct((2, rows, width), BRAIN),
            jax.ShapeDtypeStruct((rows, width), FLOAT),
            jax.ShapeDtypeStruct((rows, width), FLOAT),
        ],
        scratch_shapes=[
            pltpu.VMEM((rows, heads * cols), BRAIN),
            pltpu.VMEM((width, heads * cols), BRAIN),
        ],
        compiler_params=pltpu.CompilerParams(vmem_limit_bytes=VMEM_BYTES),
        cost_estimate=pl.CostEstimate(
            flops=8 * rows * heads * cols * width, bytes_accessed=16 << 20, transcendentals=0
        ),
        name="frames_back",
    )(most, last, weight, base)


def merge_kernel(count, joined, where_ref, *refs):
    ins, outs = refs[: 4 * count], refs[4 * count :]
    at = 0
    for n in range(count):
        for which in range(2):
            value = ins[4 * n + which][...] + ins[4 * n + 2 + which][...]
            value = value.reshape(
                [d for i, d in enumerate(ins[4 * n].shape) if i != 1]
            )
            if joined:
                outs[which][:, :, :, at : at + value.shape[-1]] = value
            else:
                outs[2 * n + which][...] = value
        at += ins[4 * n].shape[-1]


def merge(where, parts, places, steps, joined=False):
    ins, in_specs, outs, out_specs = [], [], [], []
    for (keep, come, outer, inner), place in zip(parts, places):
        rows, columns = keep.shape[-2:]
        size = outer * inner // steps
        if inner >= size:
            block, per = (1, size), inner // size
        else:
            block, per = (size // inner, inner), 1

        def index(which, g, m, place=place, per=per):
            half = m[3 + place]
            return (g // per, half if which == 0 else 1 - half, g % per, 0, 0)

        for array in (keep, come):
            for which in range(2):
                ins.append(array.reshape(outer, 2, inner, rows, columns))
                in_specs.append(
                    pl.BlockSpec(
                        (block[0], 1, block[1], rows, columns), functools.partial(index, which)
                    )
                )
        for which in range(2):
            outs.append(jax.ShapeDtypeStruct((outer, inner, rows, columns), BRAIN))
            out_specs.append(
                pl.BlockSpec(
                    block + (rows, columns), lambda g, m, per=per: (g // per, g % per, 0, 0)
                )
            )
    if joined:
        whole_columns = sum(o.shape[-1] for o in outs) // 2
        shape = outs[0].shape[:-1] + (whole_columns,)
        outs = [jax.ShapeDtypeStruct(shape, BRAIN)] * 2
        spec = pl.BlockSpec(
            out_specs[0].block_shape[:-1] + (whole_columns,), out_specs[0].index_map
        )
        out_specs = [spec] * 2
    res = pl.pallas_call(
        functools.partial(merge_kernel, len(parts), joined),
        grid_spec=pltpu.PrefetchScalarGridSpec(
            num_scalar_prefetch=1, grid=(steps,), in_specs=in_specs, out_specs=out_specs
        ),
        out_shape=outs,
        compiler_params=pltpu.CompilerParams(vmem_limit_bytes=VMEM_BYTES),
        cost_estimate=pl.CostEstimate(flops=1 << 22, bytes_accessed=8 << 20, transcendentals=0),
        name="merge",
    )(where, *ins)
    flat = [r.reshape((-1,) + r.shape[2:]) for r in res]
    return [(flat[2 * n], flat[2 * n + 1]) for n in range(len(flat) // 2)]


def split_portions(parts, joined):
    arrays, at = [[], [], []], 0
    for portion in parts:
        for array, _, count in portion.spans:
            arrays[array].append(joined[:, at : at + count])
            at += count
    return [jnp.concatenate(a, axis=1) for a in arrays]


def weights_end_kernel(parts, cols, *refs):
    keep_ref, come_ref, expand_ref, reduce_ref, output_ref, vectors_ref, bias_ref, held = refs
    joined = keep_ref[0].astype(FLOAT) + come_ref[0].astype(FLOAT)
    expand, reduce, output = split_portions(parts, joined)
    expand_ref[...] = expand
    reduce_ref[...] = reduce
    output = output.T
    output_ref[...] = output[:cols]
    lines = output[cols:]
    share = joined.shape[0]
    for c in range(SLOTS // 8):
        at = slice(c * share, (c + 1) * share)
        held[:, at] = lines[8 * c : 8 * c + 8]
    vectors_ref[...] = held[:6]
    for n in range(bias_ref.shape[0]):
        bias_ref[n : n + 1] = held[6:7, n * LANES : (n + 1) * LANES]


def weights_end(parts, keep, come, hidden, cols, width):
    share = keep.shape[1]
    shapes = [(share, hidden), (share, hidden), (cols, share), (6, width)]
    shapes.append((hidden // LANES, LANES))
    return pl.pallas_call(
        functools.partial(weights_end_kernel, parts, cols),
        out_shape=[jax.ShapeDtypeStruct(shape, FLOAT) for shape in shapes],
        scratch_shapes=[pltpu.VMEM((8, width), FLOAT)],
        cost_estimate=pl.CostEstimate(flops=1 << 18, bytes_accessed=1 << 20, transcendentals=0),
        name="weights_end",
    )(keep, come)


def project_end_kernel(riding, keep_ref, come_ref, out_ref, bias_ref):
    heads, share, _ = keep_ref.shape
    for h in range(heads):
        value = keep_ref[h].astype(FLOAT) + come_ref[h].astype(FLOAT)
        own = slice(h * HEAD_DIM, (h + 1) * HEAD_DIM)
        for i, at in enumerate((LANES + HEAD_DIM, HEAD_DIM, 0)):
            out_ref[i, :, own] = value[:, at : at + HEAD_DIM]
        free = value[:, LANES:]
        if riding:
            lines = free.T
            spread = 3 * HEAD_DIM // share
            line = jnp.concatenate([lines[n : n + 1] for n in range(spread)], axis=1)
            bias_ref[0:1, own] = line[:, 2 * HEAD_DIM :]
            bias_ref[1:2, own] = line[:, :HEAD_DIM]
        else:
            bias_ref[h] = free[:, :HEAD_DIM]


def project_end(keep, come, riding):
    heads, share, _ = keep.shape
    cols = heads * HEAD_DIM
    bias_shape = (2, cols) if riding else (heads, share, HEAD_DIM)
    return pl.pallas_call(
        functools.partial(project_end_kernel, riding),
        out_shape=[
            jax.ShapeDtypeStruct((3, share, cols), FLOAT),
            jax.ShapeDtypeStruct(bias_shape, FLOAT),
        ],
        cost_estimate=pl.CostEstimate(flops=1 << 18, bytes_accessed=1 << 20, transcendentals=0),
        name="project_end",
    )(keep, come)


def fence(*values):
    return lax.optimization_barrier(values)


def tie(first, second):
    return fence(first, second)[0]


def body(
    frames,
    segment_ids,
    project_weight,
    query_value_bias,
    output_weight,
    output_bias,
    first_gain,
    first_shift,
    expand_weight,
    expand_bias,
    reduce_weight,
    reduce_bias,
    second_gain,
    second_shift,
    cotangent,
    *,
    groups,
):
    rows, width = frames.shape
    cols = project_weight.shape[2]
    hidden = expand_weight.shape[1]
    heads = cols // HEAD_DIM
    length = 4 * rows
    me = lax.axis_index("tensor")
    half = lax.axis_index("dp") % 2
    half_two = (lax.axis_index("dp") // 2) % 2
    other = functools.partial(swap, axis="tensor", size=4)

    far = other(frames, bits=2)
    near = other(frames, bits=1)

    bits = [2**n for n in reversed(range(groups.bit_length() - 1))]
    where = [me, half, half_two, jnp.zeros_like(me)]
    where = jnp.stack(where + [(lax.axis_index("dp") // b) % 2 for b in bits]).astype(jnp.int32)
    vectors = jnp.stack(
        [output_bias, first_gain, first_shift, reduce_bias, second_gain, second_shift]
    ).astype(FLOAT)
    vectors = jnp.pad(vectors, ((0, 2), (0, 0)))
    bias = query_value_bias.astype(FLOAT).reshape(2, heads, HEAD_DIM)
    bias = jnp.stack(
        [
            jnp.pad(bias[0], ((0, 0), (HEAD_DIM, 0))).reshape(-1),
            jnp.pad(bias[1], ((0, 0), (0, HEAD_DIM))).reshape(-1),
        ]
    )
    wide_halves = jnp.concatenate(
        [
            expand_weight.T.reshape(2, hidden // 2, width),
            output_weight.reshape(2, cols // 2, width),
            jnp.broadcast_to(
                jnp.pad(expand_bias[None], ((0, 15), (0, width - hidden))), (2, 16, width)
            ),
        ],
        axis=1,
    )
    wide = wide_halves.reshape(-1, width)
    wide_half = lax.dynamic_index_in_dim(wide_halves, half, 0, False)
    back_half = lax.dynamic_index_in_dim(
        reduce_weight.reshape(2, hidden // 2, width), half_two, 0, False
    )
    *started, spread_weight = project(
        where, 0, (frames, near), project_weight, bias, segment_ids, ()
    )

    far, started, wide_half, back_half, wide_later, back_later, where = fence(
        far, started, wide_half, back_half, wide, reduce_weight, where
    )
    near_wide = other(wide_later, bits=1)
    near_back = other(back_later, bits=1)
    last = other(far, bits=1)

    got_wide = other(wide_half, bits=2)
    got_back = other(back_half, bits=2)
    qt, ka, vt, qz, kt, va, xt = project(
        where, 2, (far, last), spread_weight, bias, segment_ids, started
    )
    far_blocks = attend(qt, ka, vt, rows, 2, 2, False)
    far_blocks, got_wide, got_back, near_wide, near_back, qt_later = fence(
        far_blocks, got_wide, got_back, near_wide, near_back, qt
    )
    relayed = swap(got_wide, "dp", groups, 1)
    relayed_back = swap(got_back, "dp", groups, 2)
    far_mixed = other(far_blocks[0][0], bits=2)
    last_wide = other(got_wide, bits=1)
    last_back = other(got_back, bits=1)
    near_blocks = attend(qt_later, ka, vt, rows, 0, 2, True)
    near_blocks, relayed, relayed_back, far_mixed, last_wide, last_back = fence(
        near_blocks, relayed, relayed_back, far_mixed, last_wide, last_back
    )
    near_mixed = other(near_blocks[0][1], bits=1)
    last_mixed = other(far_mixed[1:], bits=1)
    mixed = [near_blocks[0][0], near_mixed, far_mixed, last_mixed]

    riding = groups * 8 == SLOTS and 2 * LANES - cols == SLOTS and (width // groups) % 16 == 0
    outs = layer(
        where,
        mixed,
        frames,
        cotangent,
        vectors,
        (wide, near_wide, got_wide, relayed, last_wide, other(relayed, bits=1)),
        (reduce_weight, near_back, got_back, relayed_back, last_back, other(relayed_back, bits=1)),
        riding,
    )
    layer_out, grad_first = outs[:2]
    own_grad, near_grad, far_grad, small = outs[2:6]
    keeps, sends = outs[6:9], outs[9:12]
    far_grad = other(far_grad, bits=2)
    near_grad = other(near_grad, bits=1)

    share = width // groups
    steps = [0] + bits[::-1]
    orders = [steps[n:3] + steps[:n] for n in range(3)]
    arrived = [other(send, bits=1) for send in sends]
    forms = (qt, ka, qz, kt, va, xt)
    exacts = [near_blocks[1], far_blocks[1]]
    logs = [near_blocks[2], far_blocks[2]]
    begun, query = attend_back_own(forms, own_grad, exacts[0], logs[0])
    arrived, begun, far_grad, near_grad = fence(arrived, begun, far_grad, near_grad)
    grad_heads = [near_grad, far_grad, other(far_grad[1:], bits=1)]
    axes = [0] + bits
    left = [list(axes) for _ in orders]
    values = [
        (keep.reshape(2 * groups, share, -1), come.reshape(2 * groups, share, -1))
        for keep, come in zip(keeps, arrived)
    ]

    def divide(values, chosen, steps, joined=False):
        parts = []
        for n, ((keep, come), axis) in enumerate(zip(values, chosen)):
            at = left[n].index(axis)
            parts.append((keep, come, 2**at, 2 ** (len(left[n]) - at - 1)))
            left[n] = [b for b in left[n] if b != axis]
        return merge(where, parts, [axes.index(axis) for axis in chosen], steps, joined)

    def go(value, axis):
        return other(value, bits=2) if axis == 0 else swap(value, "dp", groups, axis)

    def sent_half(value, axis):
        count, lead = value.shape[:2]
        at = tail_left.index(axis)
        view = value.reshape((count, 2**at, 2, lead // 2 ** (at + 1)) + value.shape[2:])
        bit = (lax.axis_index("dp") // axis) % 2
        shape = (count, lead // 2) + value.shape[2:]
        keep_ = lax.dynamic_index_in_dim(view, bit, 2, keepdims=False).reshape(shape)
        send = lax.dynamic_index_in_dim(view, 1 - bit, 2, keepdims=False).reshape(shape)
        return keep_, swap(send, "dp", groups, axis)

    def added(pair):
        return (pair[0].astype(FLOAT) + pair[1].astype(FLOAT)).astype(BRAIN)

    def phase(values, number, steps):
        order = [o[number] for o in orders]
        halves = divide(values, order, steps)
        return [(half_[0], go(half_[1], axis)) for half_, axis in zip(halves, order)]

    def keeps_of(values):
        return [value[0] for value in values]

    tail_left = list(bits)
    values = phase(values, 0, 4)
    begun = tie(begun, keeps_of(values))
    head_args = (share, forms, grad_heads, exacts, logs)
    most = attend_back(0, heads - 1, *head_args, begun, query)
    most, values = fence(most, values)

    values = phase(values, 1, 2)
    begun = tie(begun, keeps_of(values))
    final = attend_back(heads - 1, 1, *head_args, begun, query)
    final, values = fence(final, values)

    pair = sent_half(jnp.concatenate([most[1], final[1]]), 1)
    tail_left.remove(1)
    values = tie(values, pair[0])
    values = phase(values, 2, 1)
    most_rows, final_rows, grad_first = tie(
        (most[0], final[0], grad_first), keeps_of(values)
    )
    sums = frames_back(most_rows, final_rows, spread_weight, grad_first)
    (sent, own_sum, far_sum), values, pair = fence(sums, values, pair)
    got = other(sent, bits=1)
    tail = added(pair)
    for axis in bits[::-1][1:-1]:
        pair = sent_half(tail, axis)
        tail_left.remove(axis)
        if axis != bits[1]:
            tail = added(pair)
    far_sum, got = tie((far_sum, got), pair[0])
    far_sum = (far_sum + got[1].astype(FLOAT)).astype(BRAIN)
    far_got = other(far_sum, bits=2)
    values = tie(values, far_sum)
    rest = steps[3:]
    while len(rest) > 1:
        values = [
            (half_[0], go(half_[1], rest[0])) for half_ in divide(values, [rest[0]] * 3, 1)
        ]
        rest = rest[1:]
    ((kept, going),) = divide(values, [rest[0]] * 3, 1, True)
    kept, going, pair = fence(kept, going, pair)
    come = go(going, rest[0])
    tail_keep, tail_come = sent_half(added(pair), rest[0])
    frames_grad = own_sum + got[0].astype(FLOAT) + far_got.astype(FLOAT)
    kept, come, frames_grad = fence(kept, come, frames_grad)

    parts = portions(width, hidden)
    if riding:
        expand_grad, reduce_grad, output_grad, vector_grads, expand_bias_grad = weights_end(
            parts, kept, come, hidden, cols, width
        )
        expand_bias_grad = expand_bias_grad.reshape(hidden)
    else:
        joined = (kept.astype(FLOAT) + come.astype(FLOAT))[0]
        expand_grad, reduce_grad, output_grad = split_portions(parts, joined)
        output_grad = output_grad[:, :cols].T
        everyone = lax.all_gather(small, ("dp", "tensor")).reshape(groups, 4, 16, width)
        vector_grads = jnp.sum(everyone[:, :, :6], axis=(0, 1))
        picked = [
            lax.dynamic_index_in_dim(everyone[:, s], 8 + (me ^ s), 1, False) for s in range(4)
        ]
        expand_bias_grad = sum(jnp.sum(p, axis=0) for p in picked)

    reduce_grad = reduce_grad.T
    project_grad, attend_bias_grad = project_end(tail_keep[:, 0], tail_come[:, 0], riding)
    if not riding:
        spread = 3 * HEAD_DIM // share
        bias_sums = jnp.swapaxes(attend_bias_grad[:, :, :spread], 1, 2)
        bias_sums = bias_sums.reshape(heads, 3, HEAD_DIM)
        attend_bias_grad = jnp.stack([bias_sums[:, i].reshape(cols) for i in (2, 0)])
    return (
        layer_out,
        frames_grad,
        project_grad,
        attend_bias_grad,
        output_grad,
        expand_grad,
        expand_bias_grad,
        reduce_grad,
        vector_grads,
    )


def solution(mesh):
    placed = (
        P(("dp", "tensor"), None),
        P("dp", None),
        P(None, None, "tensor"),
        P(None, "tensor"),
        P("tensor", None),
        P(),
        P(),
        P(),
        P(None, "tensor"),
        P("tensor"),
        P("tensor", None),
        P(),
        P(),
        P(),
        P(("dp", "tensor"), None),
    )
    return jax.shard_map(
        functools.partial(body, groups=mesh.shape["dp"]),
        mesh=mesh,
        in_specs=placed,
        out_specs=(
            P(("dp", "tensor"), None),
            P(("dp", "tensor"), None),
            P(None, "dp", "tensor"),
            P(None, "tensor"),
            P("tensor", "dp"),
            P("dp", "tensor"),
            P("tensor"),
            P("tensor", "dp"),
            P(),
        ),
        check_vma=False,
    )
```

```python
import functools

import jax
import jax.numpy as jnp
import numpy as np
from jax import lax
from jax.experimental import pallas as pl
from jax.experimental.pallas import tpu as pltpu
from jax.sharding import PartitionSpec as P

HEAD_DIM = 64
ROW_LEN = 2048
EPS = 1e-05
FLOAT = jnp.float32
BRAIN = jnp.bfloat16
BIG = 1e30
SCALE = HEAD_DIM ** (-0.5)
VMEM_BYTES = 63 << 20
IDS = 8
LANES = 128
CHUNK = 1024
BACK_CHUNK = 512
SLOTS = 64

NN = (((1,), (0,)), ((), ()))
NT = (((1,), (1,)), ((), ()))


def dot(left, right, dims=NN):
    return lax.dot_general(left, right, dims, preferred_element_type=FLOAT)


def swap(value, axis, size, bits):
    return lax.ppermute(value, axis, [(i, i ^ bits) for i in range(size)])


def whole(shape):
    return pl.BlockSpec(shape, lambda *_: (0,) * len(shape), pipeline_mode=pl.Buffered(1))


def split_three(value):
    top = value.astype(BRAIN).astype(FLOAT)
    rest = value - top
    middle = rest.astype(BRAIN).astype(FLOAT)
    return top, middle, rest - middle


def project_kernel(heads, rows, first, where_ref, *refs):
    x_refs = refs[:2]
    w_ref, bias_ref, segs_ref = refs[2:5]
    if first:
        held = refs[-1]
        spread = refs[-2]
        forms = refs[-9:-2]
    else:
        held = refs[-1]
        spread = w_ref
        forms = refs[-8:-1]
    qt_ref, ka_ref, vt_ref, qz_ref, kt_ref, va_ref, xt_ref = forms
    step = pl.program_id(0)
    for k in range(2):

        @pl.when(step == k)
        def _():
            held[...] = x_refs[k][...]

    if first:

        @pl.when(step == 0)
        def _():
            nothing = jnp.zeros((w_ref.shape[1], HEAD_DIM), BRAIN)
            for i in range(3):
                for h in range(heads):
                    own = w_ref[i, :, h * HEAD_DIM : (h + 1) * HEAD_DIM]
                    pair = [own, nothing] if i == 2 else [nothing, own]
                    spread[i, :, h * LANES : (h + 1) * LANES] = jnp.concatenate(pair, axis=1)

    x = held[...]
    xt_ref[...] = x.T
    segs = segs_ref[...].astype(FLOAT)
    number = lax.broadcasted_iota(jnp.int32, (HEAD_DIM, rows), 0).astype(FLOAT)
    qtail = jnp.where(jnp.broadcast_to(segs, (HEAD_DIM, rows)) == number, 1.0, 0.0).astype(BRAIN)
    lane = lax.broadcasted_iota(jnp.int32, (rows, LANES), 1)
    differ = jnp.broadcast_to(segs, (LANES, rows)).T != lane.astype(FLOAT)
    ktail = jnp.where(lane < IDS, jnp.where(differ, -BIG, 0.0), jnp.where(lane < IDS + 3, -1.0, 0.0))
    minus = jnp.where((lane >= HEAD_DIM) & (lane < HEAD_DIM + 3), -1.0, 0.0)
    query = (dot(x, spread[0]) + bias_ref[0:1]).astype(BRAIN).astype(FLOAT) * SCALE
    key = dot(x, spread[1])
    value = dot(x, spread[2]) + bias_ref[1:2]
    for h in range(heads):
        own = slice(h * LANES, (h + 1) * LANES)
        q, k_, v = query[:, own], key[:, own], value[:, own]
        qt_ref[h, :HEAD_DIM, :] = qtail
        qt_ref[h, HEAD_DIM:, :] = q.T[HEAD_DIM:].astype(BRAIN)
        kt_ref[h] = k_.T.astype(BRAIN)
        vt_ref[h] = v.T[:HEAD_DIM].astype(BRAIN)
        ka_ref[h] = (k_ + ktail).astype(BRAIN)
        va_ref[h] = (v + minus).astype(BRAIN)
        qz_ref[h, :HEAD_DIM, :] = jnp.zeros((HEAD_DIM, rows), BRAIN)
        qz_ref[h, HEAD_DIM:, :] = qt_ref[h, HEAD_DIM:, :]


def project(where, first, pieces, weight, bias, segs, before):
    rows, width = pieces[0].shape
    heads = bias.shape[1] // LANES
    length = 4 * rows
    by_lane = lambda i, m: (0, 0, first + i)
    by_row = lambda i, m: (0, first + i, 0)
    shapes = [
        ((heads, LANES, length), (heads, LANES, rows), by_lane),
        ((heads, length, LANES), (heads, rows, LANES), by_row),
        ((heads, HEAD_DIM, length), (heads, HEAD_DIM, rows), by_lane),
        ((heads, LANES, length), (heads, LANES, rows), by_lane),
        ((heads, LANES, length), (heads, LANES, rows), by_lane),
        ((heads, length, LANES), (heads, rows, LANES), by_row),
        ((width, length), (width, rows), lambda i, m: (0, first + i)),
    ]
    out_specs = [pl.BlockSpec(block, index) for _, block, index in shapes]
    if not before:
        shapes.append(((3, width, heads * LANES), None, None))
        out_specs.append(whole(shapes[-1][0]))
    return pl.pallas_call(
        functools.partial(project_kernel, heads, rows, not before),
        grid_spec=pltpu.PrefetchScalarGridSpec(
            num_scalar_prefetch=1,
            grid=(2,),
            in_specs=[
                whole((rows, width)),
                whole((rows, width)),
                whole(weight.shape),
                whole(bias.shape),
                pl.BlockSpec((1, rows), lambda i, m: (0, m[0] ^ (first + i))),
            ]
            + [pl.BlockSpec(memory_space=pl.ANY)] * len(before),
            out_specs=out_specs,
            scratch_shapes=[pltpu.VMEM((rows, width), BRAIN)],
        ),
        out_shape=[jax.ShapeDtypeStruct(s[0], BRAIN) for s in shapes],
        input_output_aliases={6 + n: n for n in range(len(before))},
        compiler_params=pltpu.CompilerParams(vmem_limit_bytes=VMEM_BYTES),
        cost_estimate=pl.CostEstimate(
            flops=12 * rows * width * heads * LANES, bytes_accessed=8 << 20, transcendentals=0
        ),
        name="project",
    )(where, *pieces, weight, bias, segs, *before)


def attend_kernel(rows, count, *refs):
    qt_ref, ka_ref, vt_ref = refs[:3]
    out_refs, exact_ref, log_ref, held = refs[3:-3], refs[-3], refs[-2], refs[-1]
    length = ka_ref.shape[1]
    part, chunk = held.shape[2], min(CHUNK, length)
    chunks = [slice(at, at + chunk) for at in range(0, length, chunk)]
    items = [(n, at) for n in range(count) for at in range(0, rows, part)]

    def score(item, keys):
        n, at = items[item]
        first = n * rows + at
        scores = dot(ka_ref[0, keys], qt_ref[0, :, first : first + part])
        held[item % 2, keys] = scores
        return jnp.max(scores, axis=0, keepdims=True)

    highest = functools.reduce(jnp.maximum, [score(0, keys) for keys in chunks])
    for item, (n, at) in enumerate(items):
        tops, total, mixed = [], 0.0, 0.0
        for keys in chunks:
            if item + 1 < len(items):
                tops.append(score(item + 1, keys))
            raised = jnp.exp(held[item % 2, keys] - highest)
            total = total + jnp.sum(raised, axis=0, keepdims=True)
            mixed = mixed + dot(vt_ref[0, :, keys], raised.astype(BRAIN))
        mixed = mixed / total
        lanes = slice(at, at + part)
        if len(out_refs) == 1:
            out_refs[0][n, :, lanes] = mixed.astype(BRAIN)
        else:
            out_refs[n][0, :, lanes] = mixed.astype(BRAIN)
        exact_ref[n, :, lanes] = mixed
        log_ref[0, n : n + 1, lanes] = highest + jnp.log(total)
        if tops:
            highest = functools.reduce(jnp.maximum, tops)


def attend(qt, ka, vt, rows, first, count, parted):
    heads, _, length = qt.shape
    cols = heads * HEAD_DIM
    by_head = lambda h: (0, h, 0)
    sizes = [1] * count if parted else [count]
    outs = pl.pallas_call(
        functools.partial(attend_kernel, rows, count),
        grid=(heads,),
        in_specs=[
            pl.BlockSpec((1, LANES, count * rows), lambda h: (h, 0, first // count)),
            pl.BlockSpec((1, length, LANES), lambda h: (h, 0, 0)),
            pl.BlockSpec((1, HEAD_DIM, length), lambda h: (h, 0, 0)),
        ],
        out_specs=[pl.BlockSpec((n, HEAD_DIM, rows), by_head) for n in sizes]
        + [
            pl.BlockSpec((count, HEAD_DIM, rows), by_head),
            pl.BlockSpec((1, count, rows), lambda h: (h, 0, 0)),
        ],
        out_shape=[jax.ShapeDtypeStruct((n, cols, rows), BRAIN) for n in sizes]
        + [
            jax.ShapeDtypeStruct((count, cols, rows), FLOAT),
            jax.ShapeDtypeStruct((heads, count, rows), FLOAT),
        ],
        scratch_shapes=[pltpu.VMEM((2, length, rows // 2), FLOAT)],
        compiler_params=pltpu.CompilerParams(vmem_limit_bytes=VMEM_BYTES),
        cost_estimate=pl.CostEstimate(
            flops=8 * heads * length * count * rows * LANES,
            bytes_accessed=8 << 20,
            transcendentals=heads * length * count * rows,
        ),
        name="attend",
    )(qt, ka, vt)
    return outs[:-2], outs[-2], outs[-1]


def fill(slot, queries, grads, plain, qt, grad, exact, log):
    rows = queries.shape[2]
    low = lax.broadcasted_iota(jnp.int32, (8, rows), 0)

    def stacked(value):
        top, middle, bottom = split_three(value)
        return jnp.where(
            low == 0, top, jnp.where(low == 1, middle, jnp.where(low == 2, bottom, 0.0))
        )

    nothing = jnp.zeros((LANES - HEAD_DIM - 16, rows), BRAIN)
    delta = jnp.sum(grad.astype(FLOAT) * exact, axis=0, keepdims=True)
    ids = qt[:16].astype(FLOAT)[:IDS]
    queries[slot, :16] = jnp.concatenate([ids, stacked(log)], axis=0).astype(BRAIN)
    queries[slot, 16:] = qt[16:]
    grads[slot, :HEAD_DIM] = grad
    grads[slot, HEAD_DIM : HEAD_DIM + 16] = jnp.concatenate(
        [stacked(delta), jnp.zeros((8, rows), FLOAT)], axis=0
    ).astype(BRAIN)
    grads[slot, HEAD_DIM + 16 :] = nothing
    plain[slot, :HEAD_DIM] = grad
    plain[slot, HEAD_DIM:] = jnp.zeros((LANES - HEAD_DIM, rows), BRAIN)


def back_block(slot, queries, grads, plain, qz, ka_ref, kt_ref, va_ref, add):
    length = ka_ref.shape[1]
    chunk = min(BACK_CHUNK, length)
    grad_query = 0.0
    for at in range(0, length, chunk):
        keys = slice(at, at + chunk)
        probs = jnp.exp(dot(ka_ref[0, keys], queries[slot]))
        grad_scores = (probs * dot(va_ref[0, keys], grads[slot])).astype(BRAIN)
        add(keys, dot(probs.astype(BRAIN), plain[slot], NT) + dot(grad_scores, qz, NT))
        grad_query = grad_query + dot(kt_ref[0, :, keys], grad_scores)
    return (grad_query * SCALE).T.astype(BRAIN)


def attend_back_own_kernel(*refs):
    qt_ref, ka_ref, qz_ref, kt_ref, va_ref = refs[:5]
    grad_ref, exact_ref, log_ref = refs[5:8]
    total_ref, query_ref = refs[8:10]
    scratch = refs[10:]
    fill(0, *scratch, qt_ref[0], grad_ref[0], exact_ref[0], log_ref[0, 0:1])

    def add(keys, value):
        total_ref[0, keys] = value

    query_ref[0] = back_block(0, *scratch, qz_ref[0], ka_ref, kt_ref, va_ref, add)


def attend_back_own(forms, grad, exact, log):
    qt, ka, qz, kt, va, _ = forms
    heads, length = ka.shape[:2]
    rows = length // 4
    by_head = lambda h: (h, 0, 0)
    return pl.pallas_call(
        attend_back_own_kernel,
        grid=(heads,),
        in_specs=[
            pl.BlockSpec((1, LANES, rows), by_head),
            pl.BlockSpec((1, length, LANES), by_head),
            pl.BlockSpec((1, LANES, rows), by_head),
            pl.BlockSpec((1, LANES, length), by_head),
            pl.BlockSpec((1, length, LANES), by_head),
            pl.BlockSpec((1, HEAD_DIM, rows), lambda h: (0, h, 0)),
            pl.BlockSpec((1, HEAD_DIM, rows), lambda h: (0, h, 0)),
            pl.BlockSpec((1, 2, rows), by_head),
        ],
        out_specs=[
            pl.BlockSpec((1, length, LANES), by_head),
            pl.BlockSpec((1, rows, LANES), by_head),
        ],
        out_shape=[
            jax.ShapeDtypeStruct((heads, length, LANES), FLOAT),
            jax.ShapeDtypeStruct((heads, rows, LANES), BRAIN),
        ],
        scratch_shapes=[pltpu.VMEM((1, LANES, rows), BRAIN)] * 3,
        compiler_params=pltpu.CompilerParams(vmem_limit_bytes=VMEM_BYTES),
        cost_estimate=pl.CostEstimate(
            flops=18 * length * length * LANES,
            bytes_accessed=8 << 20,
            transcendentals=length * length,
        ),
        name="attend_back_own",
    )(qt, ka, qz, kt, va, grad, exact, log)


def attend_back_kernel(rows, first, share, *refs):
    qt_ref, ka_ref, qz_ref, kt_ref, va_ref, xt_ref = refs[:6]
    grad_refs, exacts, logs = refs[6:9], refs[9:12], refs[12:14]
    begun_ref, query_ref = refs[14:16]
    out_ref, project_ref = refs[16:18]
    total, begun, xt = refs[18:21]
    scratch = refs[21:24]
    sem = refs[24]
    step = pl.program_id(0)
    begun_copy = pltpu.make_async_copy(begun_ref.at[first + step], begun, sem.at[0])
    xt_copy = pltpu.make_async_copy(xt_ref, xt, sem.at[1])
    begun_copy.start()
    pl.when(step == 0)(xt_copy.start)
    for k in range(3):
        at = pl.ds((k + 1) * rows, rows)
        log = logs[(k + 1) // 2][0, (k + 1) % 2 : (k + 1) % 2 + 1]
        fill(k, *scratch, qt_ref[0, :, at], grad_refs[k][0], exacts[k][0], log)
    out_ref[0, :rows, LANES:] = query_ref[0]
    for k in range(3):

        def add(keys, value):
            if k == 0:
                total[keys] = value
            else:
                total[keys] += value

        at = pl.ds((k + 1) * rows, rows)
        qz = qz_ref[0, :, at]
        out_ref[0, at, LANES:] = back_block(k, *scratch, qz, ka_ref, kt_ref, va_ref, add)
    begun_copy.wait()
    pl.when(step == 0)(xt_copy.wait)
    out_ref[0, :, :LANES] = (total[...] + begun[...]).astype(BRAIN)
    pieces = out_ref[0]
    project_ref[0] = dot(xt[...], pieces).astype(BRAIN)
    bias = jnp.sum(pieces.astype(FLOAT), axis=0, keepdims=True)
    if share % 16 == 0:
        bias = jnp.concatenate([bias[:, :LANES], bias[:, LANES + HEAD_DIM :]], axis=1)
        spread = 3 * HEAD_DIM // share
        line = jnp.concatenate(
            [bias[:, n * share : (n + 1) * share] for n in range(spread)]
            + [jnp.zeros((8 - spread, share), FLOAT)],
            axis=0,
        ).T.astype(BRAIN)
        for at in range(0, project_ref.shape[1], share):
            project_ref[0, at : at + share, LANES : LANES + 8] = line
    else:
        refs[25][0] = bias


def attend_back(first, count, share, forms, grads, exacts, logs, begun, query):
    qt, ka, qz, kt, va, xt = forms
    length, width = ka.shape[1], xt.shape[0]
    rows = length // 4
    cols = 2 * LANES
    own = lambda i: (first + i, 0, 0)
    by_block = lambda n: pl.BlockSpec((1, HEAD_DIM, rows), lambda i: (n, first + i, 0))
    each = lambda i: (i, 0, 0)
    out_specs = [pl.BlockSpec((1, length, cols), each), pl.BlockSpec((1, width, cols), each)]
    out_shape = [
        jax.ShapeDtypeStruct((count, length, cols), BRAIN),
        jax.ShapeDtypeStruct((count, width, cols), BRAIN),
    ]
    scratch = (
        [
            pltpu.VMEM((length, LANES), FLOAT),
            pltpu.VMEM((length, LANES), FLOAT),
            pltpu.VMEM((width, length), BRAIN),
        ]
        + [pltpu.VMEM((3, LANES, rows), BRAIN)] * 3
        + [pltpu.SemaphoreType.DMA((2,))]
    )
    kernel = functools.partial(attend_back_kernel, rows, first, share)
    if share % 16:
        out_specs.append(pl.BlockSpec((1, 1, cols), each))
        out_shape.append(jax.ShapeDtypeStruct((count, 1, cols), FLOAT))
        kernel = lambda *refs: attend_back_kernel(
            rows, first, share, *refs[:18], *refs[19:], refs[18]
        )
    res = pl.pallas_call(
        kernel,
        grid=(count,),
        in_specs=[
            pl.BlockSpec((1, LANES, length), own),
            pl.BlockSpec((1, length, LANES), own),
            pl.BlockSpec((1, LANES, length), own),
            pl.BlockSpec((1, LANES, length), own),
            pl.BlockSpec((1, length, LANES), own),
            pl.BlockSpec(memory_space=pl.ANY),
        ]
        + [by_block(0)] * 3
        + [by_block(1), by_block(0), by_block(1)]
        + [pl.BlockSpec((1, 2, rows), own)] * 2
        + [pl.BlockSpec(memory_space=pl.ANY), pl.BlockSpec((1, rows, LANES), own)],
        out_specs=out_specs,
        out_shape=out_shape,
        scratch_shapes=scratch,
        compiler_params=pltpu.CompilerParams(vmem_limit_bytes=VMEM_BYTES),
        cost_estimate=pl.CostEstimate(
            flops=20 * count * length * length * LANES,
            bytes_accessed=8 << 20,
            transcendentals=count * length * length,
        ),
        name="attend_back",
    )(qt, ka, qz, kt, va, xt, *grads, exacts[0], exacts[1], exacts[1], *logs, begun, query)
    project_grad = res[1].reshape(count, width // share, share, cols)
    if share % 16:
        spread = 3 * HEAD_DIM // share
        bias = jnp.concatenate([res[2][..., :LANES], res[2][..., LANES + HEAD_DIM :]], axis=2)
        bias = jnp.swapaxes(bias.reshape(count, 1, spread, share), 2, 3).astype(BRAIN)
        bias = jnp.broadcast_to(bias, (count, width // share, share, spread))
        project_grad = jnp.concatenate(
            [
                project_grad[..., :LANES],
                bias,
                project_grad[..., LANES + spread :],
            ],
            axis=3,
        )
    return res[0], project_grad


def gelu_parts(values):
    t = 1.0 / (1.0 + (0.3275911 * 0.7071067811865476) * jnp.abs(values))
    bell = jnp.exp(-0.5 * values * values)
    poly = 0.5 * 1.061405429
    for c in (-1.453152027, 1.421413741, -0.284496736, 0.254829592):
        poly = poly * t + 0.5 * c
    tail = poly * t * bell
    below = jnp.where(values >= 0, 1.0 - tail, tail)
    return values * below, below + values * bell * 0.3989422804014327


def mean_of(values):
    return jnp.mean(values, axis=-1, keepdims=True)


class Portion:
    def __init__(self, *spans):
        self.spans = spans
        self.columns = sum(span[2] for span in spans)


def portions(width, hidden):
    if hidden == 6 * LANES:
        return (
            Portion((0, 0, 4 * LANES)),
            Portion((0, 4 * LANES, 2 * LANES), (1, 0, 3 * LANES)),
            Portion((1, 3 * LANES, 3 * LANES), (2, 0, 2 * LANES)),
        )
    return (Portion((0, 0, hidden)), Portion((1, 0, hidden)), Portion((2, 0, 2 * LANES)))


def layer_kernel(parts, hidden, riding, *refs):
    t_ref = refs[0]
    mixed = refs[1:5]
    x_ref, cot_ref, vec_ref = refs[5:8]
    wide_refs, back_refs = refs[8:14], refs[14:20]
    out_ref, grad_first_ref = refs[20:22]
    d_refs = (refs[22].at[0], refs[23].at[0], refs[24].at[0], refs[24].at[1])
    small_ref = refs[25]
    keeps, sends = refs[26:29], refs[29:32]
    wet, wo, eb, back, orow, act, slope, dz, stage, tail_stage = refs[32:42]
    wide_sem, back_sem, out_sem = refs[42:]
    half, back_half = t_ref[1], t_ref[2]
    width = x_ref.shape[1]
    part = mixed[0].shape[1]
    bias_out, gain_one, shift_one, bias_red, gain_two, shift_two = (
        vec_ref[i : i + 1] for i in range(6)
    )

    split = hidden // 2 + part // 2 + 16

    def load_wide(k, n):
        if k < 2:
            source, first, which = wide_refs[k], n * split, n
        else:
            source, first, which = wide_refs[2 * k - 2 + n], 0, (half, 1 - half)[n]
        found = []
        for m, (at, count, target, to) in enumerate(
            [
                (0, hidden // 2, wet, k * hidden + which * (hidden // 2)),
                (hidden // 2, part // 2, wo, k * part + which * (part // 2)),
                (hidden // 2 + part // 2, 16, eb.at[k], which * 16),
            ]
        ):
            to = to if isinstance(to, int) else pl.multiple_of(to, 16)
            found.append(
                pltpu.make_async_copy(
                    source.at[pl.ds(first + at, count)],
                    target.at[pl.ds(to, count)],
                    wide_sem.at[k, n, m],
                )
            )
        return found

    loads = [[load_wide(k, n) for n in range(2)] for k in range(4)]
    def load_back(k, n):
        if k < 2:
            source, first, which = back_refs[k], n * (hidden // 2), n
        else:
            source, first, which = back_refs[2 * k - 2 + n], 0, (back_half, 1 - back_half)[n]
        to = k * hidden + which * (hidden // 2)
        to = to if isinstance(to, int) else pl.multiple_of(to, 16)
        return pltpu.make_async_copy(
            source.at[pl.ds(first, hidden // 2)],
            back.at[pl.ds(to, hidden // 2)],
            back_sem.at[k, n],
        )

    back_loads = [load_back(k, n) for k in range(4) for n in range(2)]

    def each(kind, k=None):
        return [c[kind] for pair in (loads if k is None else [loads[k]]) for c in pair]

    for copy in each(1):
        copy.start()
    for k in range(4):
        for copy in each(0, k) + each(2, k):
            copy.start()
    for k, ref in enumerate(mixed):
        orow[:, k * part : (k + 1) * part] = ref[0].astype(FLOAT).T.astype(BRAIN)
    for copy in each(1):
        copy.wait()
    for copy in back_loads:
        copy.start()
    total = x_ref[...].astype(FLOAT) + bias_out + dot(orow[...], wo[...])
    center = total - mean_of(total)
    inverse_one = lax.rsqrt(mean_of(center * center) + EPS)
    unit_one = center * inverse_one
    normed = unit_one * gain_one + shift_one
    hb = normed.astype(BRAIN)
    hbt = normed.T.astype(BRAIN)

    owns = [slice(j * hidden, (j + 1) * hidden) for j in range(4)]
    for copy in each(0) + each(2):
        copy.wait()
    inner = dot(hb, wet[owns[0]], NT)
    for j in range(4):
        now = inner + eb[j, :16].astype(FLOAT)[:1]
        if j < 3:
            inner = dot(hb, wet[owns[j + 1]], NT)
        active, derivative = gelu_parts(now)
        act[:, owns[j]] = active.astype(BRAIN)
        slope[:, owns[j]] = derivative
    for copy in back_loads:
        copy.wait()
    total = normed + dot(act[...], back[...]) + bias_red
    center = total - mean_of(total)
    inverse = lax.rsqrt(mean_of(center * center) + EPS)
    unit = center * inverse
    out_ref[...] = (unit * gain_two + shift_two).astype(BRAIN)
    cot = cot_ref[...].astype(FLOAT)
    scaled = cot * gain_two
    grad = inverse * (scaled - mean_of(scaled) - unit * mean_of(scaled * unit))
    small_ref[3:4] = jnp.sum(grad, axis=0, keepdims=True)
    small_ref[4:5] = jnp.sum(cot * unit, axis=0, keepdims=True)
    small_ref[5:6] = jnp.sum(cot, axis=0, keepdims=True)
    dfb = grad.astype(BRAIN)
    dfbt = grad.T.astype(BRAIN)

    def outgoing(block, array, first_sem):
        found = []
        for ref, portion in zip(keeps if block in (0, 2) else sends, parts):
            at = 0
            for held, first, count in portion.spans:
                if held == array:
                    source = tail_stage.at[block] if array == 2 else stage.at[block, array]
                    found.append(
                        pltpu.make_async_copy(
                            source.at[:, pl.ds(first, count)],
                            ref.at[block // 2, :, pl.ds(at, count)],
                            out_sem.at[block, first_sem + len(found)],
                        )
                    )
                at += count
        return found

    order = (1, 3, 0, 2)
    started = []
    for j in order:
        stage[j, 1] = dot(dfbt, act[:, owns[j]]).astype(BRAIN)
        copies = outgoing(j, 1, 2)
        for copy in copies:
            copy.start()
        started += copies
    grad_active = dot(dfb, back[owns[order[0]]], NT)
    for n, j in enumerate(order):
        now = grad_active
        if n < 3:
            grad_active = dot(dfb, back[owns[order[n + 1]]], NT)
        grad_inner = (now * slope[:, owns[j]]).astype(BRAIN)
        dz[:, owns[j]] = grad_inner
        small_ref[8 + j : 9 + j] = jnp.sum(grad_inner.astype(FLOAT), axis=0, keepdims=True)
        stage[j, 0] = dot(hbt, grad_inner).astype(BRAIN)
        copies = outgoing(j, 0, 0)
        for copy in copies:
            copy.start()
        started += copies
    grad = grad + dot(dz[...], wet[...])
    small_ref[1:2] = jnp.sum(grad * unit_one, axis=0, keepdims=True)
    small_ref[2:3] = jnp.sum(grad, axis=0, keepdims=True)
    scaled = grad * gain_one
    first = inverse_one * (scaled - mean_of(scaled) - unit_one * mean_of(scaled * unit_one))
    small_ref[0:1] = jnp.sum(first, axis=0, keepdims=True)
    small_ref[6:8] = jnp.zeros((2, width), FLOAT)
    small_ref[12:] = jnp.zeros((4, width), FLOAT)
    grad_first_ref[...] = first
    grad_mixed = dot(wo[...], first.astype(BRAIN), NT).astype(BRAIN)
    for k, ref in enumerate(d_refs):
        ref[...] = grad_mixed[k * part : (k + 1) * part]
    output_grad = dot(first.T.astype(BRAIN), orow[...]).astype(BRAIN)
    places = SLOTS // 8
    share = width // places
    sums = small_ref[...]
    for k in range(4):
        tail_stage[k, :, :part] = output_grad[:, k * part : (k + 1) * part]
        if riding:
            rows_k = jnp.concatenate([sums[:6], sums[8 + k : 9 + k], sums[6:7]], axis=0)
            lines = jnp.concatenate(
                [rows_k[:, c * share : (c + 1) * share] for c in range(places)], axis=0
            ).T.astype(BRAIN)
            tail_stage[k, :, part:] = jnp.concatenate([lines] * places, axis=0)
        else:
            tail_stage[k, :, part:] = jnp.zeros((width, 2 * LANES - part), BRAIN)
        copies = outgoing(k, 2, 4)
        for copy in copies:
            copy.start()
        started += copies
    for copy in started:
        copy.wait()


def layer(halves, mixed, frames, cotangent, vectors, wides, backs, riding):
    rows, width = frames.shape
    part = mixed[0].shape[1]
    hidden = backs[0].shape[0]
    parts = portions(width, hidden)
    grads = [jax.ShapeDtypeStruct((2, width, p.columns), BRAIN) for p in parts]
    grid_spec = pltpu.PrefetchScalarGridSpec(
        num_scalar_prefetch=1,
        grid=(1,),
        in_specs=[whole((1, part, rows))] * 4
        + [whole((rows, width)), whole((rows, width)), whole(vectors.shape)]
        + [pl.BlockSpec(memory_space=pl.ANY)] * 12,
        out_specs=[whole((rows, width)), whole((rows, width))]
        + [whole((n, part, rows)) for n in (1, 1, 2)]
        + [whole((16, width))]
        + [pl.BlockSpec(memory_space=pl.ANY)] * 6,
        scratch_shapes=[
            pltpu.VMEM((4 * hidden, width), BRAIN),
            pltpu.VMEM((4 * part, width), BRAIN),
            pltpu.VMEM((4, 32, width), BRAIN),
            pltpu.VMEM((4 * hidden, width), BRAIN),
            pltpu.VMEM((rows, width), BRAIN),
            pltpu.VMEM((rows, 4 * hidden), BRAIN),
            pltpu.VMEM((rows, 4 * hidden), FLOAT),
            pltpu.VMEM((rows, 4 * hidden), BRAIN),
            pltpu.VMEM((4, 2, width, hidden), BRAIN),
            pltpu.VMEM((4, width, 2 * LANES), BRAIN),
            pltpu.SemaphoreType.DMA((4, 2, 3)),
            pltpu.SemaphoreType.DMA((4, 2)),
            pltpu.SemaphoreType.DMA((4, 6)),
        ],
    )
    return pl.pallas_call(
        functools.partial(layer_kernel, parts, hidden, riding),
        grid_spec=grid_spec,
        out_shape=[
            jax.ShapeDtypeStruct((rows, width), BRAIN),
            jax.ShapeDtypeStruct((rows, width), FLOAT),
        ]
        + [jax.ShapeDtypeStruct((n, part, rows), BRAIN) for n in (1, 1, 2)]
        + [jax.ShapeDtypeStruct((16, width), FLOAT)]
        + grads
        + grads,
        compiler_params=pltpu.CompilerParams(vmem_limit_bytes=VMEM_BYTES),
        cost_estimate=pl.CostEstimate(
            flops=2 * rows * width * (24 * hidden + 3 * width),
            bytes_accessed=40 << 20,
            transcendentals=8 * rows * hidden,
        ),
        name="layer",
    )(halves, *mixed, frames, cotangent, vectors, *wides, *backs)


def frames_kernel(most_ref, last_ref, w_ref, base_ref, sent_ref, own_ref, far_ref, stack, weights):
    step = pl.program_id(0)
    heads = w_ref.shape[2] // LANES
    wide = 2 * LANES

    @pl.when(step == 0)
    def _():
        for h in range(heads):
            own = slice(h * LANES, (h + 1) * LANES)
            at = h * wide
            weights[:, at : at + LANES] = w_ref[1, :, own] + w_ref[2, :, own]
            weights[:, at + LANES : at + wide] = w_ref[0, :, own]

    for h in range(heads - 1):
        stack[:, h * wide : (h + 1) * wide] = most_ref[h]
    stack[:, (heads - 1) * wide :] = last_ref[0]
    value = dot(stack[...], weights[...], NT)

    @pl.when(step < 2)
    def _():
        sent_ref[0] = value.astype(BRAIN)

    @pl.when(step == 2)
    def _():
        own_ref[...] = base_ref[...] + value

    @pl.when(step == 3)
    def _():
        far_ref[...] = value


def frames_back(most, last, weight, base):
    heads = most.shape[0] + 1
    width = weight.shape[1]
    rows = most.shape[1] // 4
    cols = 2 * LANES
    block = lambda i: (0, jnp.where(i < 2, 2 * i + 1, 2 * i - 4), 0)
    return pl.pallas_call(
        frames_kernel,
        grid=(4,),
        in_specs=[
            pl.BlockSpec((heads - 1, rows, cols), block),
            pl.BlockSpec((1, rows, cols), block),
            whole(weight.shape),
            whole((rows, width)),
        ],
        out_specs=[
            pl.BlockSpec((1, rows, width), lambda i: (jnp.minimum(i, 1), 0, 0)),
            whole((rows, width)),
            whole((rows, width)),
        ],
        out_shape=[
            jax.ShapeDtypeStruct((2, rows, width), BRAIN),
            jax.ShapeDtypeStruct((rows, width), FLOAT),
            jax.ShapeDtypeStruct((rows, width), FLOAT),
        ],
        scratch_shapes=[
            pltpu.VMEM((rows, heads * cols), BRAIN),
            pltpu.VMEM((width, heads * cols), BRAIN),
        ],
        compiler_params=pltpu.CompilerParams(vmem_limit_bytes=VMEM_BYTES),
        cost_estimate=pl.CostEstimate(
            flops=8 * rows * heads * cols * width, bytes_accessed=16 << 20, transcendentals=0
        ),
        name="frames_back",
    )(most, last, weight, base)


def merge_kernel(count, joined, where_ref, *refs):
    ins, outs = refs[: 4 * count], refs[4 * count :]
    at = 0
    for n in range(count):
        for which in range(2):
            value = ins[4 * n + which][...] + ins[4 * n + 2 + which][...]
            value = value.reshape(
                [d for i, d in enumerate(ins[4 * n].shape) if i != 1]
            )
            if joined:
                outs[which][:, :, :, at : at + value.shape[-1]] = value
            else:
                outs[2 * n + which][...] = value
        at += ins[4 * n].shape[-1]


def merge(where, parts, places, steps, joined=False):
    ins, in_specs, outs, out_specs = [], [], [], []
    for (keep, come, outer, inner), place in zip(parts, places):
        rows, columns = keep.shape[-2:]
        size = outer * inner // steps
        if inner >= size:
            block, per = (1, size), inner // size
        else:
            block, per = (size // inner, inner), 1

        def index(which, g, m, place=place, per=per):
            half = m[3 + place]
            return (g // per, half if which == 0 else 1 - half, g % per, 0, 0)

        for array in (keep, come):
            for which in range(2):
                ins.append(array.reshape(outer, 2, inner, rows, columns))
                in_specs.append(
                    pl.BlockSpec(
                        (block[0], 1, block[1], rows, columns), functools.partial(index, which)
                    )
                )
        for which in range(2):
            outs.append(jax.ShapeDtypeStruct((outer, inner, rows, columns), BRAIN))
            out_specs.append(
                pl.BlockSpec(
                    block + (rows, columns), lambda g, m, per=per: (g // per, g % per, 0, 0)
                )
            )
    if joined:
        whole_columns = sum(o.shape[-1] for o in outs) // 2
        shape = outs[0].shape[:-1] + (whole_columns,)
        outs = [jax.ShapeDtypeStruct(shape, BRAIN)] * 2
        spec = pl.BlockSpec(
            out_specs[0].block_shape[:-1] + (whole_columns,), out_specs[0].index_map
        )
        out_specs = [spec] * 2
    res = pl.pallas_call(
        functools.partial(merge_kernel, len(parts), joined),
        grid_spec=pltpu.PrefetchScalarGridSpec(
            num_scalar_prefetch=1, grid=(steps,), in_specs=in_specs, out_specs=out_specs
        ),
        out_shape=outs,
        compiler_params=pltpu.CompilerParams(vmem_limit_bytes=VMEM_BYTES),
        cost_estimate=pl.CostEstimate(flops=1 << 22, bytes_accessed=8 << 20, transcendentals=0),
        name="merge",
    )(where, *ins)
    flat = [r.reshape((-1,) + r.shape[2:]) for r in res]
    return [(flat[2 * n], flat[2 * n + 1]) for n in range(len(flat) // 2)]


def split_portions(parts, joined):
    arrays, at = [[], [], []], 0
    for portion in parts:
        for array, _, count in portion.spans:
            arrays[array].append(joined[:, at : at + count])
            at += count
    return [jnp.concatenate(a, axis=1) for a in arrays]


def weights_end_kernel(parts, cols, *refs):
    keep_ref, come_ref, expand_ref, reduce_ref, output_ref, vectors_ref, bias_ref, held = refs
    joined = keep_ref[0].astype(FLOAT) + come_ref[0].astype(FLOAT)
    expand, reduce, output = split_portions(parts, joined)
    expand_ref[...] = expand
    reduce_ref[...] = reduce
    output = output.T
    output_ref[...] = output[:cols]
    lines = output[cols:]
    share = joined.shape[0]
    for c in range(SLOTS // 8):
        at = slice(c * share, (c + 1) * share)
        held[:, at] = lines[8 * c : 8 * c + 8]
    vectors_ref[...] = held[:6]
    for n in range(bias_ref.shape[0]):
        bias_ref[n : n + 1] = held[6:7, n * LANES : (n + 1) * LANES]


def weights_end(parts, keep, come, hidden, cols, width):
    share = keep.shape[1]
    shapes = [(share, hidden), (share, hidden), (cols, share), (6, width)]
    shapes.append((hidden // LANES, LANES))
    return pl.pallas_call(
        functools.partial(weights_end_kernel, parts, cols),
        out_shape=[jax.ShapeDtypeStruct(shape, FLOAT) for shape in shapes],
        scratch_shapes=[pltpu.VMEM((8, width), FLOAT)],
        cost_estimate=pl.CostEstimate(flops=1 << 18, bytes_accessed=1 << 20, transcendentals=0),
        name="weights_end",
    )(keep, come)


def project_end_kernel(riding, keep_ref, come_ref, out_ref, bias_ref):
    heads, share, _ = keep_ref.shape
    for h in range(heads):
        value = keep_ref[h].astype(FLOAT) + come_ref[h].astype(FLOAT)
        own = slice(h * HEAD_DIM, (h + 1) * HEAD_DIM)
        for i, at in enumerate((LANES + HEAD_DIM, HEAD_DIM, 0)):
            out_ref[i, :, own] = value[:, at : at + HEAD_DIM]
        free = value[:, LANES:]
        if riding:
            lines = free.T
            spread = 3 * HEAD_DIM // share
            line = jnp.concatenate([lines[n : n + 1] for n in range(spread)], axis=1)
            bias_ref[0:1, own] = line[:, 2 * HEAD_DIM :]
            bias_ref[1:2, own] = line[:, :HEAD_DIM]
        else:
            bias_ref[h] = free[:, :HEAD_DIM]


def project_end(keep, come, riding):
    heads, share, _ = keep.shape
    cols = heads * HEAD_DIM
    bias_shape = (2, cols) if riding else (heads, share, HEAD_DIM)
    return pl.pallas_call(
        functools.partial(project_end_kernel, riding),
        out_shape=[
            jax.ShapeDtypeStruct((3, share, cols), FLOAT),
            jax.ShapeDtypeStruct(bias_shape, FLOAT),
        ],
        cost_estimate=pl.CostEstimate(flops=1 << 18, bytes_accessed=1 << 20, transcendentals=0),
        name="project_end",
    )(keep, come)


def fence(*values):
    return lax.optimization_barrier(values)


def tie(first, second):
    return fence(first, second)[0]


def body(
    frames,
    segment_ids,
    project_weight,
    query_value_bias,
    output_weight,
    output_bias,
    first_gain,
    first_shift,
    expand_weight,
    expand_bias,
    reduce_weight,
    reduce_bias,
    second_gain,
    second_shift,
    cotangent,
    *,
    groups,
):
    rows, width = frames.shape
    cols = project_weight.shape[2]
    hidden = expand_weight.shape[1]
    heads = cols // HEAD_DIM
    length = 4 * rows
    me = lax.axis_index("tensor")
    half = lax.axis_index("dp") % 2
    half_two = (lax.axis_index("dp") // 2) % 2
    other = functools.partial(swap, axis="tensor", size=4)

    far = other(frames, bits=2)
    near = other(frames, bits=1)

    bits = [2**n for n in reversed(range(groups.bit_length() - 1))]
    where = [me, half, half_two, jnp.zeros_like(me)]
    where = jnp.stack(where + [(lax.axis_index("dp") // b) % 2 for b in bits]).astype(jnp.int32)
    vectors = jnp.stack(
        [output_bias, first_gain, first_shift, reduce_bias, second_gain, second_shift]
    ).astype(FLOAT)
    vectors = jnp.pad(vectors, ((0, 2), (0, 0)))
    bias = query_value_bias.astype(FLOAT).reshape(2, heads, HEAD_DIM)
    bias = jnp.stack(
        [
            jnp.pad(bias[0], ((0, 0), (HEAD_DIM, 0))).reshape(-1),
            jnp.pad(bias[1], ((0, 0), (0, HEAD_DIM))).reshape(-1),
        ]
    )
    wide_halves = jnp.concatenate(
        [
            expand_weight.T.reshape(2, hidden // 2, width),
            output_weight.reshape(2, cols // 2, width),
            jnp.broadcast_to(
                jnp.pad(expand_bias[None], ((0, 15), (0, width - hidden))), (2, 16, width)
            ),
        ],
        axis=1,
    )
    wide = wide_halves.reshape(-1, width)
    wide_half = lax.dynamic_index_in_dim(wide_halves, half, 0, False)
    back_half = lax.dynamic_index_in_dim(
        reduce_weight.reshape(2, hidden // 2, width), half_two, 0, False
    )
    *started, spread_weight = project(
        where, 0, (frames, near), project_weight, bias, segment_ids, ()
    )

    far, started, wide_half, back_half, wide_later, back_later, where = fence(
        far, started, wide_half, back_half, wide, reduce_weight, where
    )
    near_wide = other(wide_later, bits=1)
    near_back = other(back_later, bits=1)
    last = other(far, bits=1)

    got_wide = other(wide_half, bits=2)
    got_back = other(back_half, bits=2)
    qt, ka, vt, qz, kt, va, xt = project(
        where, 2, (far, last), spread_weight, bias, segment_ids, started
    )
    far_blocks = attend(qt, ka, vt, rows, 2, 2, False)
    far_blocks, got_wide, got_back, near_wide, near_back, qt_later = fence(
        far_blocks, got_wide, got_back, near_wide, near_back, qt
    )
    relayed = swap(got_wide, "dp", groups, 1)
    relayed_back = swap(got_back, "dp", groups, 2)
    far_mixed = other(far_blocks[0][0], bits=2)
    last_wide = other(got_wide, bits=1)
    last_back = other(got_back, bits=1)
    near_blocks = attend(qt_later, ka, vt, rows, 0, 2, True)
    near_blocks, relayed, relayed_back, far_mixed, last_wide, last_back = fence(
        near_blocks, relayed, relayed_back, far_mixed, last_wide, last_back
    )
    near_mixed = other(near_blocks[0][1], bits=1)
    last_mixed = other(far_mixed[1:], bits=1)
    mixed = [near_blocks[0][0], near_mixed, far_mixed, last_mixed]

    riding = groups * 8 == SLOTS and 2 * LANES - cols == SLOTS and (width // groups) % 16 == 0
    outs = layer(
        where,
        mixed,
        frames,
        cotangent,
        vectors,
        (wide, near_wide, got_wide, relayed, last_wide, other(relayed, bits=1)),
        (reduce_weight, near_back, got_back, relayed_back, last_back, other(relayed_back, bits=1)),
        riding,
    )
    layer_out, grad_first = outs[:2]
    own_grad, near_grad, far_grad, small = outs[2:6]
    keeps, sends = outs[6:9], outs[9:12]
    far_grad = other(far_grad, bits=2)
    near_grad = other(near_grad, bits=1)

    share = width // groups
    steps = [0] + bits[::-1]
    orders = [steps[n:3] + steps[:n] for n in range(3)]
    arrived = [other(send, bits=1) for send in sends]
    forms = (qt, ka, qz, kt, va, xt)
    exacts = [near_blocks[1], far_blocks[1]]
    logs = [near_blocks[2], far_blocks[2]]
    begun, query = attend_back_own(forms, own_grad, exacts[0], logs[0])
    arrived, begun, far_grad, near_grad = fence(arrived, begun, far_grad, near_grad)
    grad_heads = [near_grad, far_grad, other(far_grad[1:], bits=1)]
    axes = [0] + bits
    left = [list(axes) for _ in orders]
    values = [
        (keep.reshape(2 * groups, share, -1), come.reshape(2 * groups, share, -1))
        for keep, come in zip(keeps, arrived)
    ]

    def divide(values, chosen, steps, joined=False):
        parts = []
        for n, ((keep, come), axis) in enumerate(zip(values, chosen)):
            at = left[n].index(axis)
            parts.append((keep, come, 2**at, 2 ** (len(left[n]) - at - 1)))
            left[n] = [b for b in left[n] if b != axis]
        return merge(where, parts, [axes.index(axis) for axis in chosen], steps, joined)

    def go(value, axis):
        return other(value, bits=2) if axis == 0 else swap(value, "dp", groups, axis)

    def sent_half(value, axis):
        count, lead = value.shape[:2]
        at = tail_left.index(axis)
        view = value.reshape((count, 2**at, 2, lead // 2 ** (at + 1)) + value.shape[2:])
        bit = (lax.axis_index("dp") // axis) % 2
        shape = (count, lead // 2) + value.shape[2:]
        keep_ = lax.dynamic_index_in_dim(view, bit, 2, keepdims=False).reshape(shape)
        send = lax.dynamic_index_in_dim(view, 1 - bit, 2, keepdims=False).reshape(shape)
        return keep_, swap(send, "dp", groups, axis)

    def added(pair):
        return (pair[0].astype(FLOAT) + pair[1].astype(FLOAT)).astype(BRAIN)

    def phase(values, number, steps):
        order = [o[number] for o in orders]
        halves = divide(values, order, steps)
        return [(half_[0], go(half_[1], axis)) for half_, axis in zip(halves, order)]

    def keeps_of(values):
        return [value[0] for value in values]

    tail_left = list(bits)
    values = phase(values, 0, 4)
    begun = tie(begun, keeps_of(values))
    head_args = (share, forms, grad_heads, exacts, logs)
    most = attend_back(0, heads - 1, *head_args, begun, query)
    most, values = fence(most, values)

    values = phase(values, 1, 2)
    begun = tie(begun, keeps_of(values))
    final = attend_back(heads - 1, 1, *head_args, begun, query)
    final, values = fence(final, values)

    pair = sent_half(jnp.concatenate([most[1], final[1]]), 1)
    tail_left.remove(1)
    values = tie(values, pair[0])
    values = phase(values, 2, 1)
    most_rows, final_rows, grad_first = tie(
        (most[0], final[0], grad_first), keeps_of(values)
    )
    sums = frames_back(most_rows, final_rows, spread_weight, grad_first)
    (sent, own_sum, far_sum), values, pair = fence(sums, values, pair)
    got = other(sent, bits=1)
    tail = added(pair)
    for axis in bits[::-1][1:-1]:
        pair = sent_half(tail, axis)
        tail_left.remove(axis)
        if axis != bits[1]:
            tail = added(pair)
    far_sum, got = tie((far_sum, got), pair[0])
    far_sum = (far_sum + got[1].astype(FLOAT)).astype(BRAIN)
    far_got = other(far_sum, bits=2)
    values = tie(values, far_sum)
    rest = steps[3:]
    while len(rest) > 1:
        values = [
            (half_[0], go(half_[1], rest[0])) for half_ in divide(values, [rest[0]] * 3, 1)
        ]
        rest = rest[1:]
    ((kept, going),) = divide(values, [rest[0]] * 3, 1, True)
    kept, going, pair = fence(kept, going, pair)
    come = go(going, rest[0])
    tail_keep, tail_come = sent_half(added(pair), rest[0])
    frames_grad = own_sum + got[0].astype(FLOAT) + far_got.astype(FLOAT)
    kept, come, frames_grad = fence(kept, come, frames_grad)

    parts = portions(width, hidden)
    if riding:
        expand_grad, reduce_grad, output_grad, vector_grads, expand_bias_grad = weights_end(
            parts, kept, come, hidden, cols, width
        )
        expand_bias_grad = expand_bias_grad.reshape(hidden)
    else:
        joined = (kept.astype(FLOAT) + come.astype(FLOAT))[0]
        expand_grad, reduce_grad, output_grad = split_portions(parts, joined)
        output_grad = output_grad[:, :cols].T
        everyone = lax.all_gather(small, ("dp", "tensor")).reshape(groups, 4, 16, width)
        vector_grads = jnp.sum(everyone[:, :, :6], axis=(0, 1))
        picked = [
            lax.dynamic_index_in_dim(everyone[:, s], 8 + (me ^ s), 1, False) for s in range(4)
        ]
        expand_bias_grad = sum(jnp.sum(p, axis=0) for p in picked)

    reduce_grad = reduce_grad.T
    project_grad, attend_bias_grad = project_end(tail_keep[:, 0], tail_come[:, 0], riding)
    if not riding:
        spread = 3 * HEAD_DIM // share
        bias_sums = jnp.swapaxes(attend_bias_grad[:, :, :spread], 1, 2)
        bias_sums = bias_sums.reshape(heads, 3, HEAD_DIM)
        attend_bias_grad = jnp.stack([bias_sums[:, i].reshape(cols) for i in (2, 0)])
    return (
        layer_out,
        frames_grad,
        project_grad,
        attend_bias_grad,
        output_grad,
        expand_grad,
        expand_bias_grad,
        reduce_grad,
        vector_grads,
    )


def solution(mesh):
    placed = (
        P(("dp", "tensor"), None),
        P("dp", None),
        P(None, None, "tensor"),
        P(None, "tensor"),
        P("tensor", None),
        P(),
        P(),
        P(),
        P(None, "tensor"),
        P("tensor"),
        P("tensor", None),
        P(),
        P(),
        P(),
        P(("dp", "tensor"), None),
    )
    return jax.shard_map(
        functools.partial(body, groups=mesh.shape["dp"]),
        mesh=mesh,
        in_specs=placed,
        out_specs=(
            P(("dp", "tensor"), None),
            P(("dp", "tensor"), None),
            P(None, "dp", "tensor"),
            P(None, "tensor"),
            P("tensor", "dp"),
            P("dp", "tensor"),
            P("tensor"),
            P("tensor", "dp"),
            P(),
        ),
        check_vma=False,
    )
```
